32 devices in a mesh: blk: 4 (over z), wa: 8 (over y, x, core).
Axes of the slice: x: 2, y: 2, z: 4, core: 2. Of those that a mesh axis runs over, the one named last changes fastest.
Arguments:
- tokens: bfloat16 [8, 16, 64, 256], P('wa', 'blk'), may hold values from -6 to 6
- placement: int32 [8, 16], P('wa'), may hold values from 0 to 15, as said below
- block_mask: int32 [4, 8, 8], replicated, may hold values from 0 to 1, as said below
- w_qkv: bfloat16 [2, 256, 768], P(None, ('blk', 'wa')), may hold values from -0.375 to 0.375
- w_out: bfloat16 [2, 256, 256], P(None, ('blk', 'wa')), may hold values from -1.5 to 1.5
- w_in: bfloat16 [2, 256, 1024], P(None, ('blk', 'wa')), may hold values from -0.375 to 0.375
- w_down: bfloat16 [2, 1024, 256], P(None, ('blk', 'wa')), may hold values from -0.1875 to 0.1875
- biases: bfloat16 [2, 2560], P(None, ('blk', 'wa')), may hold values from -1.796875 to 1.796875
- gains: bfloat16 [2, 512], P(None, ('blk', 'wa')), may hold values from 0.5 to 1.5
- mask_logits: bfloat16 [2, 256], P(None, ('blk', 'wa')), may hold values from -3 to 1
- masked_pos: int32 [8, 4, 64], P('wa', 'blk'), may hold values from 0 to 255, as said below
- masked_count: int32 [8, 4], P('wa', 'blk'), may hold values from 17 to 64, as said below
- masked_grad: float32 [8, 4, 64, 256], P('wa', 'blk'), may hold values from -6 to 6
Outputs:
- out: float32 [8, 16, 64, 256], P('wa', 'blk')
- grad_tokens: float32 [8, 16, 64, 256], P('wa', 'blk')
- grad_w_qkv: float32 [2, 256, 768], P(None, ('blk', 'wa'))
- grad_w_out: float32 [2, 256, 256], P(None, ('blk', 'wa'))
- grad_w_in: float32 [2, 256, 1024], P(None, ('blk', 'wa'))
- grad_w_down: float32 [2, 1024, 256], P(None, ('blk', 'wa'))
- grad_biases: float32 [2, 2560], P(None, ('blk', 'wa'))
- grad_gains: float32 [2, 512], P(None, ('blk', 'wa'))
- grad_mask_logits: float32 [2, 256], P(None, ('blk', 'wa'))
The draws below stay inside these ranges and needn't reach their ends.
Inputs may be any that keep to these rules, and one draw needn't show every extreme that they name: Each row of placement is a permutation of the 16 blocks of the group's 16 // 8 sequences. block_mask[h, i, i] = 1 for every head h and block i. `masked_pos`: the 64 entries of one device's list are distinct local rows. The first masked_count[g, b] entries of device (g, b)'s list are its masked rows; the other entries carry no gradient.
All inputs are finite; a program needn't handle non-finite values.
Results may differ from the reference program's by a relative error of at most 0.017.
Values may be sent and summed in bfloat16 or wider, within the bound.
A program may use at most 128 MiB of HBM per device.

```python
import jax
import jax.numpy as jnp
from jax import lax

D = 256
H = 4
HD = 64
FF = 1024
LAYERS = 2
NB = 8
BS = 64
BLK_DEV = 4
SEQ = 512
TOK_DEV = 256
GBLK = 16
MCAP = 64
N_BLK = 4
N_WA = 8


def draw_placement(key, part):
    key = jax.random.fold_in(key, 7)
    device_count = GBLK // BLK_DEV
    block_ids = jnp.arange(NB, dtype=jnp.int32)
    fixed_slots = block_ids % device_count * BLK_DEV + block_ids // device_count
    is_fixed = jnp.zeros((GBLK,), jnp.int32).at[fixed_slots].set(1)
    rest_count = max(GBLK - NB, 1)
    free_rank = jnp.clip(jnp.cumsum(1 - is_fixed) - 1, 0, rest_count - 1)

    def one_group(group_index):
        group_key = jax.random.fold_in(key, group_index)
        pick_key, order_key, spread_key = jax.random.split(group_key, 3)
        chosen = jax.random.randint(pick_key, (), 0, GBLK // NB)
        others = jnp.arange(rest_count, dtype=jnp.int32)
        others = jnp.where(others < chosen * NB, others, others + NB)
        others = jax.random.permutation(order_key, others)
        chosen_blocks = jax.random.permutation(spread_key, block_ids)
        filled = jnp.where(is_fixed == 1, 0, others[free_rank])
        return filled.at[fixed_slots].set(chosen * NB + chosen_blocks).astype(jnp.int32)
    return jax.vmap(one_group)(jnp.arange(N_WA, dtype=jnp.int32))


def draw_block_mask(key, part):
    key = jax.random.fold_in(key, 11)
    level_key, entry_key = jax.random.split(key)
    density = jax.random.randint(level_key, (H, 1, 1), 25, 76)
    entries = jax.random.randint(entry_key, (H, NB, NB), 0, 100)
    diagonal = jnp.arange(NB)[:, None] == jnp.arange(NB)[None, :]
    return jnp.where(diagonal[None, :, :] | (entries < density), 1, 0).astype(jnp.int32)


def draw_masked_pos(key, part):
    key = jax.random.fold_in(key, 13)
    device_keys = jax.random.split(key, N_WA * N_BLK)
    listed = jax.vmap(lambda sub_key: jax.random.permutation(sub_key, TOK_DEV)[:MCAP])(device_keys)
    return listed.reshape(N_WA, N_BLK, MCAP).astype(jnp.int32)


def draw_masked_count(key, part):
    key = jax.random.fold_in(key, 17)
    first_key, second_key, third_key = jax.random.split(key, 3)
    shape = (N_WA * N_BLK,)
    first_draw = jax.random.randint(first_key, shape, 0, MCAP + 1)
    second_draw = jax.random.randint(second_key, shape, 0, MCAP + 1)
    counts = jnp.minimum(MCAP, 1 + MCAP // 4 + first_draw * second_draw // MCAP)
    busiest = jax.random.randint(third_key, (), 0, N_WA * N_BLK)
    counts = counts.at[busiest].set(MCAP)
    return counts.reshape(N_WA, N_BLK).astype(jnp.int32)


def block_scale(own_key, shape, shards, smallest, high):
    loudness = 1.0
    for axis_at, parts in shards:
        steps = jax.random.uniform(jax.random.fold_in(jax.random.fold_in(own_key, 6), axis_at), (parts,), jnp.float32, smallest / len(shards), high / len(shards))
        loudness = loudness * jnp.repeat(jnp.exp(steps), shape[axis_at] // parts).reshape((-1,) + (1,) * (len(shape) - 1 - axis_at))
    return loudness


def normal_values(key, shape, width, reach, pieces=(), held_as=jnp.bfloat16):
    loudness = block_scale(key, shape, pieces, -0.22, 0.18) if pieces else 1.0
    values = jax.random.normal(key, shape, jnp.float32) * width * loudness
    return jnp.minimum(jnp.maximum(values, -reach), reach).astype(held_as)


def setup_inputs(seed: int = 0) -> dict:
    arg_keys = jax.random.split(jax.random.key(seed), 14)
    tokens = normal_values(arg_keys[0], (N_WA, GBLK, BS, D), 1.0, 6.0, ((0, 8), (1, 4)))
    placement = draw_placement(jax.random.fold_in(arg_keys[13], 71), 0)
    block_mask = draw_block_mask(jax.random.fold_in(arg_keys[13], 71), 0)
    w_qkv = normal_values(arg_keys[3], (LAYERS, D, 3 * D), D ** -0.5, 0.375, ((1, 32),))
    w_out = normal_values(arg_keys[4], (LAYERS, D, D), (D // 16) ** -0.5, 1.5, ((1, 32),))
    w_in = normal_values(arg_keys[5], (LAYERS, D, FF), D ** -0.5, 0.375, ((1, 32),))
    w_down = normal_values(arg_keys[6], (LAYERS, FF, D), FF ** -0.5, 0.1875, ((1, 32),))
    biases = normal_values(arg_keys[7], (LAYERS, 6 * D + FF), 0.3, 1.796875, ((1, 32),))
    gains = jnp.clip(1.0 + 0.1 * jax.random.normal(arg_keys[8], (LAYERS, 2 * D), jnp.float32), 0.5, 1.5).astype(jnp.bfloat16)
    mask_logits = jnp.clip(-3.0 + 4.0 * jax.random.uniform(arg_keys[9], (LAYERS, H * NB * NB), jnp.float32) ** block_scale(arg_keys[9], (LAYERS, H * NB * NB), ((1, 32),), -0.2, 0.2), -3.0, 1.0).astype(jnp.bfloat16)
    masked_pos = draw_masked_pos(jax.random.fold_in(arg_keys[13], 71), 0)
    masked_count = draw_masked_count(jax.random.fold_in(arg_keys[13], 71), 0)
    masked_grad = normal_values(arg_keys[12], (N_WA, N_BLK, MCAP, D), 1.0, 6.0, ((0, 8), (1, 4)), jnp.float32)
    return dict(tokens=tokens, placement=placement, block_mask=block_mask, w_qkv=w_qkv, w_out=w_out, w_in=w_in, w_down=w_down, biases=biases, gains=gains, mask_logits=mask_logits, masked_pos=masked_pos, masked_count=masked_count, masked_grad=masked_grad)


@jax.custom_vjp
def low(v):
    return lax.optimization_barrier(v.astype(jnp.bfloat16)).astype(jnp.float32)

@jax.custom_vjp
def low_back(v):
    return v

def low_keep(v):
    return (low(v), None)

def low_pass(kept, grad):
    return (grad,)

def back_keep(v):
    return (v, None)

def back_low(kept, grad):
    return (low(grad),)
low.defvjp(low_keep, low_pass)
low_back.defvjp(back_keep, back_low)
HIGHEST = lax.Precision.HIGHEST

def matmul(left, right):
    return jnp.dot(left, right, precision=HIGHEST)

def normalize(hidden, norm_gain, norm_shift):
    row_mean = lax.optimization_barrier(jnp.mean(hidden, axis=-1, keepdims=True))
    centred = hidden - row_mean
    row_var = lax.optimization_barrier(jnp.mean(centred * centred, axis=-1, keepdims=True))
    return centred * lax.rsqrt(row_var + 1e-05) * norm_gain + norm_shift

def expand(table):
    return jnp.repeat(jnp.repeat(table, BS, axis=1), BS, axis=2)

def block_layer(row_data, weights, allowed):
    w_qkv, w_out, w_in, w_down, biases, gains, logits = weights
    b_query = biases[0:D]
    b_value = biases[D:2 * D]
    b_output = biases[2 * D:3 * D]
    shift_one = biases[3 * D:4 * D]
    b_inner = biases[4 * D:4 * D + FF]
    b_down = biases[4 * D + FF:5 * D + FF]
    shift_two = biases[5 * D + FF:6 * D + FF]
    bias_qkv = jnp.concatenate([b_query, jnp.zeros((D,), jnp.float32), b_value])
    qkv = low(low_back(matmul(low(row_data), w_qkv) + bias_qkv))
    seq_count = row_data.shape[0] // SEQ
    qkv = qkv.reshape(seq_count, SEQ, 3, H, HD)
    score_bias = expand(jax.nn.log_sigmoid(logits.reshape(H, NB, NB)))

    def attend(seq_item):
        queries, key_rows, values = seq_item
        scores = jnp.einsum('qhd,khd->hqk', queries, key_rows, precision=HIGHEST) * 0.125 + score_bias
        scores = jnp.where(allowed, low_back(scores), -1e+30)
        row_max = lax.optimization_barrier(jnp.max(scores, axis=-1, keepdims=True))
        exp_scores = jnp.exp(scores - row_max)
        attn_probs = exp_scores / lax.optimization_barrier(jnp.sum(exp_scores, axis=-1, keepdims=True))
        return jnp.einsum('hqk,khd->qhd', low(attn_probs), values, precision=HIGHEST)
    attended = lax.map(jax.checkpoint(attend), (qkv[:, :, 0], qkv[:, :, 1], qkv[:, :, 2]))
    attended = low(low_back(attended.reshape(-1, D)))
    branch = low_back(matmul(attended, w_out) + b_output)
    first_sum = row_data + branch
    normed = normalize(first_sum, gains[:D], shift_one)
    feed_inner = low_back(matmul(low(normed), w_in) + b_inner)
    feed_act = low(jax.nn.gelu(feed_inner, approximate=False))
    feed_out = low_back(matmul(feed_act, w_down) + b_down)
    return normalize(normed + feed_out, gains[D:], shift_two)

def reference(tokens, placement, block_mask, w_qkv, w_out, w_in, w_down, biases, gains, mask_logits, masked_pos, masked_count, masked_grad):
    params = tuple((arr.astype(jnp.float32) for arr in (w_qkv, w_out, w_in, w_down, biases, gains, mask_logits)))
    allowed = expand(block_mask) == 1
    slot_ids = jnp.arange(GBLK, dtype=jnp.int32)
    lane_ids = jnp.arange(MCAP, dtype=jnp.int32)

    def forward(row_data, weights):
        for layer_index in range(LAYERS):
            row_data = block_layer(row_data, tuple((arr[layer_index] for arr in weights)), allowed)
        return row_data

    def place_rows(row_list, row_grad):
        return jnp.zeros((TOK_DEV, D), jnp.float32).at[row_list].add(row_grad)

    def group(totals, seq_item):
        block_x, slot_order, row_lists, counts, grads_in = seq_item
        inverse = jnp.zeros((GBLK,), jnp.int32).at[slot_order].set(slot_ids)
        live_rows = (lane_ids[None, :] < counts[:, None]).astype(jnp.float32)
        cotangent = jax.vmap(place_rows)(row_lists, grads_in.astype(jnp.float32) * live_rows[:, :, None])
        cotangent = cotangent.reshape(GBLK, BS, D)[inverse].reshape(GBLK * BS, D)
        row_data = block_x.astype(jnp.float32)[inverse].reshape(GBLK * BS, D)
        result, pull_back = jax.vjp(forward, row_data, params)
        d_rows, d_params = pull_back(cotangent)
        totals = jax.tree.map(jnp.add, totals, d_params)
        out_block = result.reshape(GBLK, BS, D)[slot_order]
        grad_block = d_rows.reshape(GBLK, BS, D)[slot_order]
        return (totals, (out_block, grad_block))
    zero_grads = tuple((jnp.zeros(arr.shape, jnp.float32) for arr in params))
    totals, outputs = lax.scan(group, zero_grads, (tokens, placement, masked_pos, masked_count, masked_grad))
    return (outputs[0], outputs[1], totals[0], totals[1], totals[2], totals[3], totals[4], totals[5], totals[6])
```

```python
import functools

import jax
import jax.numpy as jnp
from jax import lax
from jax.experimental import pallas as pl
from jax.experimental.pallas import tpu as pltpu
from jax.sharding import PartitionSpec as P

D = 256
H = 4
HD = 64
FF = 1024
NB = 8
BS = 64
SEQ = 512
LAYERS = 2
BLK_DEV = 4
HALF = 256
MY_FF = FF // 2
NEG = -1e30
EPS = 1e-05
MESH = pl.DeviceIdType.MESH
F32 = jnp.float32
BF16 = jnp.bfloat16
HIGHEST = lax.Precision.HIGHEST

ROW_BQ, ROW_BV, ROW_BO, ROW_S1, ROW_BI, ROW_BD, ROW_S2, ROW_G1, ROW_G2 = 0, 2, 4, 6, 8, 16, 18, 20, 22
PV_ROWS = 24
SG_BQ, SG_BV, SG_BI, SG_BO, SG_S1, SG_BD, SG_S2, SG_G1, SG_G2, SG_LG = 0, 1, 2, 6, 8, 10, 12, 14, 16, 24
SG_ROWS = 40


def nn(left, right):
    return jnp.dot(left, right, preferred_element_type=F32)


def nt(left, right):
    return lax.dot_general(left, right, (((1,), (1,)), ((), ())), preferred_element_type=F32)


def tn(left, right):
    return lax.dot_general(left, right, (((0,), (0,)), ((), ())), preferred_element_type=F32)


def lanes(shape):
    return lax.broadcasted_iota(jnp.int32, shape, len(shape) - 1)


def turn(value, shift):
    return pltpu.roll(value, shift % 128, 1)


def pick_groups(first, second, core):
    if isinstance(core, int):
        if core == 1:
            first, second = turn(first, -32), turn(second, -32)
    else:
        first = jnp.where(core == 1, turn(first, -32), first)
        second = jnp.where(core == 1, turn(second, -32), second)
    group = lanes(first.shape) // 32
    return jnp.where(
        group == 0,
        first,
        jnp.where(group == 1, turn(first, -32), jnp.where(group == 2, turn(second, 64), turn(second, 32))),
    )


def weave_groups(zero, one):
    group = lanes(zero.shape) // 32
    first = jnp.where(
        group == 0, zero, jnp.where(group == 1, turn(one, 32), jnp.where(group == 2, turn(zero, 32), turn(one, 64)))
    )
    second = jnp.where(
        group == 0,
        turn(zero, -64),
        jnp.where(group == 1, turn(one, -32), jnp.where(group == 2, turn(zero, -32), one)),
    )
    return first, second


class Links:
    def __init__(self, send, recv, anyone):
        self.send, self.recv, self.anyone = send, recv, anyone
        self.send_used = self.recv_used = 0
        self.pending = {}

    def recv_sem(self):
        self.recv_used += 1
        return self.recv_used - 1

    def send_sem(self, bytes_like):
        self.send_used += 1
        self.pending[self.send_used - 1] = bytes_like
        return self.send_used - 1

    def push(self, source, target, send_sem, recv_sem, device):
        remote(source, target, self.send.at[send_sem], self.recv.at[recv_sem], device).start()

    def arrived(self, bytes_like, recv_sem):
        remote(bytes_like, bytes_like, self.send.at[0], self.recv.at[recv_sem], self.anyone).wait_recv()

    def drain(self):
        for send_sem, bytes_like in self.pending.items():
            remote(bytes_like, bytes_like, self.send.at[send_sem], self.recv.at[0], self.anyone).wait_send()


def remote(source, target, send_sem, recv_sem, device):
    return pltpu.make_async_remote_copy(
        src_ref=source,
        dst_ref=target,
        send_sem=send_sem,
        recv_sem=recv_sem,
        device_id=device,
        device_id_type=MESH,
    )


def layer_norm(hidden, gain, shift):
    mean = jnp.sum(hidden, axis=1, keepdims=True) * (1.0 / D)
    centred = hidden - mean
    var = jnp.sum(centred * centred, axis=1, keepdims=True) * (1.0 / D)
    rstd = lax.rsqrt(var + EPS)
    unit = centred * rstd
    return unit * gain + shift, unit, rstd


def layer_norm_back(grad, unit, rstd, gain):
    scaled = grad * gain
    mean_one = jnp.sum(scaled, axis=1, keepdims=True) * (1.0 / D)
    mean_two = jnp.sum(scaled * unit, axis=1, keepdims=True) * (1.0 / D)
    return rstd * (scaled - mean_one - unit * mean_two)


def fold(value):
    rows, cols = value.shape
    return jnp.sum(value.reshape(rows // 8, 8, cols), axis=0)


def column_sum(value):
    return jnp.sum(value, axis=0, keepdims=True)


SEND_SEMS, RECV_SEMS = 34, 70


def scratch_shapes(n_blk, n_wa, gather):
    n_plane, n_seq = n_wa // 2, n_blk // 2
    vmem = pltpu.VMEM
    shapes = dict(
        TOK=vmem((n_blk, 2, 2, BS, D), BF16),
        MGS=vmem((2, 32, D), BF16),
        MRS=vmem((8, 128), jnp.int32),
        MG=vmem((n_blk, 2, 32, D), BF16),
        MR=vmem((n_blk, 8, 128), jnp.int32),
        PGV=vmem((2, 8, 128), jnp.int32),
        PGS=pltpu.SMEM((2, 8, 128), jnp.int32),
        YB0=vmem((NB, BS, D), BF16),
        YB1=vmem((NB, BS, D), BF16),
        SND0=vmem((n_blk, 2, BS, D), BF16),
        SND1=vmem((n_blk, 2, BS, D), BF16),
        RET0=vmem((n_seq, 2, 2, BS, D), BF16),
        RET1=vmem((n_seq, 2, 2, BS, D), BF16),
        PSEND=vmem((4 * LAYERS, 2, HALF, D), BF16),
        PRECV=vmem((4 * LAYERS, 2, HALF, D), BF16),
        X=vmem((SEQ, D), F32),
        XL=vmem((LAYERS, SEQ, D), BF16),
        QKV=vmem((LAYERS, SEQ, 384), BF16),
        KT=vmem((LAYERS, 128, SEQ), BF16),
        VT=vmem((128, SEQ), BF16),
        PR=vmem((LAYERS, 2, SEQ, SEQ), BF16),
        AT=vmem((LAYERS, 128, SEQ), F32),
        AN=vmem((LAYERS, SEQ, 128), BF16),
        AX=vmem((LAYERS, SEQ, 128), BF16),
        ST=vmem((SEQ, HALF), F32),
        DS=vmem((2, SEQ, SEQ), BF16),
        PO=vmem((SEQ, D), F32),
        U1=vmem((LAYERS, SEQ, D), F32),
        R1=vmem((LAYERS, SEQ, 1), F32),
        U2=vmem((LAYERS, SEQ, D), F32),
        R2=vmem((LAYERS, SEQ, 1), F32),
        Y1B=vmem((LAYERS, SEQ, D), BF16),
        FS=vmem((HALF, MY_FF), F32),
        G=vmem((LAYERS, SEQ, MY_FF), BF16),
        GP=vmem((LAYERS, SEQ, MY_FF), BF16),
        DY=vmem((SEQ, D), F32),
        DD=vmem((SEQ, D), BF16),
        DF=vmem((SEQ, MY_FF), BF16),
        DH=vmem((SEQ, D), F32),
        DO=vmem((SEQ, D), BF16),
        DA=vmem((SEQ, 128), BF16),
        DAT=vmem((128, SEQ), F32),
        DQKV=vmem((SEQ, 384), BF16),
        BIAS=vmem((LAYERS, 2, NB, SEQ), F32),
        LR=vmem((2, NB, SEQ), F32),
        SGL=vmem((LAYERS, SG_ROWS, 128), F32),
        SGF=vmem((2, LAYERS, SG_ROWS, 128), F32),
        link_send=pltpu.SemaphoreType.DMA((SEND_SEMS if gather else 8,)),
        link_recv=pltpu.SemaphoreType.DMA((RECV_SEMS if gather else 12,)),
        tok_send=pltpu.SemaphoreType.DMA((3,)),
        tok_recv=pltpu.SemaphoreType.DMA((3,)),
        ret_send=pltpu.SemaphoreType.DMA((2,)),
        ret_recv=pltpu.SemaphoreType.DMA((2,)),
        local_sems=pltpu.SemaphoreType.DMA((6,)),
    )
    if gather:
        shapes.update(
            WA=vmem((LAYERS, n_blk, n_plane, 16, 512), BF16),
            WI=vmem((LAYERS, n_blk, n_plane, 16, MY_FF), BF16),
            WD=vmem((LAYERS, n_blk, n_plane, 32, D), BF16),
            WO=vmem((LAYERS, 128, D), BF16),
            WOX=vmem((LAYERS, n_blk // 2, n_plane, 16, 128), BF16),
            PV=vmem((LAYERS, PV_ROWS, 128), F32),
            LG=vmem((LAYERS, H, NB, 128), F32),
            S0=vmem((2, 16, 512), BF16),
            R0=vmem((2, 16, 512), BF16),
            SP=vmem((n_blk, n_plane, 2, 8, 128), F32),
            FX=vmem((LAYERS, 8, 1024), F32),
            RX=vmem((LAYERS, 8, 1024), F32),
            SGP=vmem((LAYERS, n_plane - 1, SG_ROWS, 128), F32),
            SGS=vmem((LAYERS, SG_ROWS, 128), F32),
            SGZ=vmem((LAYERS, n_blk - 1, SG_ROWS, 128), F32),
            BT=vmem((LAYERS, PV_ROWS, 128), F32),
        )
        for kind, (rows, cols) in RS_KINDS.items():
            shapes["G_" + kind] = vmem((LAYERS, n_blk, n_plane, rows, cols), BF16)
            shapes["RP_" + kind] = vmem((LAYERS, 2, 3, n_blk // 2, rows, cols), BF16)
            shapes["SZ_" + kind] = vmem((LAYERS, n_blk, rows, cols), BF16)
            shapes["RZ_" + kind] = vmem((LAYERS, n_blk - 1, rows, cols), BF16)
    return shapes


RS_KINDS = {"d": (32, D), "i": (16, MY_FF), "o": (16, 128), "q": (16, 384)}


def make_kernel(n_blk, n_wa, gather, in_names, out_names, scratch_names):
    n_plane = n_wa // 2
    n_seq = n_blk // 2
    n_slots = n_blk * BLK_DEV

    def kernel(*refs):
        r = dict(zip(in_names + out_names + scratch_names, refs))
        place_smem = r["place_smem"]
        z = lax.axis_index("blk")
        w = lax.axis_index("wa")
        c = lax.rem(w, 2)
        p = lax.div(w, 2)
        group = lax.div(z, n_seq)
        seq = lax.rem(z, n_seq)
        partner = (z, p * 2 + (1 - c))
        links = Links(r["link_send"], r["link_recv"], partner)
        x_peer, y_peer = (z, w ^ 2), (z, w ^ 4)
        local_sems = r["local_sems"]
        my_cols = pl.ds(pl.multiple_of(c * 128, 128), 128)
        other_cols = pl.ds(pl.multiple_of((1 - c) * 128, 128), 128)

        TOK, MGS, MRS, MG, MR = (r[name] for name in ("TOK", "MGS", "MRS", "MG", "MR"))
        PGV, PGS = r["PGV"], r["PGS"]
        PGV[c, 0:1, 0:n_slots] = r["place_vmem"][...]
        MGS[...] = r["masked_grad"][...].astype(BF16).reshape(2, 32, D)
        chosen = r["masked_pos"][...]
        slot_of = lax.shift_right_logical(chosen, 6)
        block_of = jnp.zeros_like(chosen)
        for j in range(BLK_DEV):
            block_of = jnp.where(slot_of == j, place_smem[0, z * BLK_DEV + j], block_of)
        target_row = block_of * BS + (chosen & (BS - 1))
        target_row = jnp.where(lanes(chosen.shape) < r["masked_count"][0, 0], target_row, -1)
        MRS[0:1, 0:64] = target_row
        MRS[0:1, 64:128] = target_row
        if gather:
            WA, WI, WD, SP = r["WA"], r["WI"], r["WD"], r["SP"]
            own_rows = ([], [])
            give_rows = ([], [])
            for l in range(LAYERS):
                qkv = r["w_qkv"][l].astype(F32)
                out_part = r["w_out"][l].astype(F32)
                inner = r["w_in"][l].astype(F32)
                sides = []
                for side in (0, 1):
                    at = 128 * side
                    attn = [qkv[:, 256 * j + at : 256 * j + at + 128] for j in range(3)]
                    attn = jnp.concatenate(attn + [out_part[:, at : at + 128]], axis=1)
                    feed = []
                    for t in range(4):
                        first = inner[:, 256 * t : 256 * t + 128]
                        second = inner[:, 256 * t + 128 : 256 * t + 256]
                        feed.append(pick_groups(first, second, side))
                    sides.append((attn, jnp.concatenate(feed, axis=1)))
                for kind in (0, 1):
                    own_rows[kind].append(jnp.where(c == 0, sides[0][kind], sides[1][kind]))
                    give_rows[kind].append(jnp.where(c == 0, sides[1][kind], sides[0][kind]))
                WD[l, z, p] = r["w_down"][l]
            for kind in (0, 1):
                r["S0"][kind] = jnp.concatenate(give_rows[kind], axis=0).astype(BF16)
            SP[z, p, c] = jnp.zeros((8, 128), F32)
            widths = []
            for at, name in ((0, "biases"), (2, "gains"), (4, "mask_logits")):
                part = r[name][...].astype(F32)
                widths.append(part.shape[1])
                SP[z, p, c, at : at + 2, 0 : part.shape[1]] = part

        barrier = pltpu.get_barrier_semaphore()
        greeted = 0
        for m in range(n_blk):
            for other in (0, 1):
                if m or other:
                    pl.semaphore_signal(barrier, inc=1, device_id=(z ^ m, w ^ other), device_id_type=MESH)
                    greeted += 1
        if gather:
            for m in range(1, n_plane):
                pl.semaphore_signal(barrier, inc=1, device_id=(z, w ^ (2 * m)), device_id_type=MESH)
                greeted += 1
        pl.semaphore_wait(barrier, greeted)

        place_in = links.recv_sem()
        links.push(PGV.at[c], PGV.at[c], links.send_sem(PGV.at[0]), place_in, partner)
        if gather:
            rows_in = links.recv_sem()
            links.push(r["S0"], r["R0"], links.send_sem(r["S0"]), rows_in, partner)
            small_in = links.recv_sem()
            links.push(SP.at[z, p, c], SP.at[z, p, c], links.send_sem(SP.at[0, 0, 0]), small_in, partner)

        at_home = c == group

        def move(here, source, target, send_sem, recv_sem, local_sem, device):
            @pl.when(jnp.logical_not(here))
            def _():
                remote(source, target, send_sem, recv_sem, device).start()

            @pl.when(here)
            def _():
                pltpu.make_async_copy(source, target, local_sem).start()

        def wait_pieces(pieces, count, sem, local_sem, sending):
            def wait(n):
                copy = remote(pieces(n), pieces(n), sem, sem, partner)
                if sending:
                    copy.wait_send()
                else:
                    copy.wait_recv()

            @pl.when(jnp.logical_not(at_home))
            def _():
                wait(count)

            @pl.when(at_home)
            def _():
                wait(count - 1)
                if not sending:
                    pltpu.make_async_copy(pieces(1), pieces(1), local_sem).wait()

        def token_pieces(kind):
            def pieces(n):
                return (TOK.at[pl.ds(0, n), 0], MG.at[pl.ds(0, n), 0], MR.at[pl.ds(0, n)])[kind]

            return pieces

        def send_kind(kind, sequences=range(n_seq)):
            for s in sequences:
                chip = c * n_seq + s
                for core in (0, 1):
                    here = jnp.logical_and(chip == z, c == core)
                    source = (r["tokens"].at[pl.ds(2 * core, 2)], MGS.at[core], MRS)[kind]
                    target = (TOK.at[z, core], MG.at[z, core], MR.at[z])[kind]
                    sems = (r["tok_send"].at[kind], r["tok_recv"].at[kind])
                    move(here, source, target, *sems, local_sems.at[kind], (chip, p * 2 + core))

        def take_kind(kind):
            wait_pieces(token_pieces(kind), n_blk, r["tok_recv"].at[kind], local_sems.at[kind], False)

        if gather:
            weight_refs = (WA, WI, WD)
            ag_recv = {}
            ag_send = {}
            for kind in (0, 1, 2):
                ref = weight_refs[kind]
                likes = (ref.at[:, 0, 0:3], ref.at[0], ref.at[0, 0:2])
                ag_send[kind] = [links.send_sem(like) for like in likes]
            ag_send["small"] = [links.send_sem(like) for like in (SP.at[0, 0:3], SP.at[:, 0:2], SP.at[0:2, 0:2])]

            def rows_at(name, z_at, p_at):
                if name == "small":
                    return SP.at[z_at, p_at]
                return weight_refs[name[0]].at[name[1], z_at, p_at]

            def ag_push(name, stage, z_at, p_at, device):
                ref = rows_at(name, z_at, p_at)
                send_sem = ag_send[name if name == "small" else name[0]][stage]
                links.push(ref, ref, send_sem, ag_recv[name][stage], device)

            every, z_low, z_high = slice(0, 4), slice(0, 2), slice(2, 4)

            def ag_z(name):
                ag_recv[name] = [links.recv_sem() for _ in range(3)]
                for m in range(1, n_blk):
                    ag_push(name, 0, z, p, (z ^ m, w))

            def ag_xy(name):
                links.arrived(rows_at(name, 0, slice(0, 3)), ag_recv[name][0])
                ag_push(name, 1, every, p, x_peer)
                ag_push(name, 1, every, p, y_peer)

            def ag_pass(name):
                links.arrived(rows_at(name, every, z_low), ag_recv[name][1])
                ag_push(name, 2, z_low, p ^ 1, y_peer)
                ag_push(name, 2, z_high, p ^ 2, x_peer)

            def ag_ready(name):
                links.arrived(rows_at(name, z_low, z_low), ag_recv[name][2])

            def merge_rows(kind, l):
                own = own_rows[kind][l]
                other = r["R0"][kind].astype(F32)[8 * l : 8 * l + 8]
                merged = jnp.concatenate([jnp.where(c == 0, own, other), jnp.where(c == 0, other, own)], axis=0)
                weight_refs[kind][l, z, p] = merged.astype(BF16)

        if gather:
            links.arrived(r["R0"], rows_in)
            merge_rows(0, 0)
            ag_z((0, 0))
            links.arrived(SP.at[0, 0, 0], small_in)
            ag_z("small")
            merge_rows(1, 0)
            ag_z((1, 0))
            ag_z((2, 0))
        send_kind(0)
        if gather:
            merge_rows(0, 1)
            merge_rows(1, 1)
            ag_xy((0, 0))
            ag_xy("small")
            ag_xy((1, 0))
            ag_xy((2, 0))
            ag_z((0, 1))
            ag_pass((0, 0))
            ag_pass("small")
            ag_z((1, 1))
            ag_z((2, 1))
            ag_pass((1, 0))
            ag_pass((2, 0))

        take_kind(0)
        tokens_in = links.recv_sem()
        links.push(TOK.at[:, c], TOK.at[:, c], links.send_sem(TOK.at[:, 0]), tokens_in, partner)
        if gather:
            ag_xy((0, 1))
        links.arrived(PGV.at[0], place_in)
        to_scalars = pltpu.make_async_copy(PGV, PGS, local_sems.at[3])
        to_scalars.start()
        to_scalars.wait()
        links.arrived(TOK.at[:, 0], tokens_in)
        X, XL = r["X"], r["XL"]
        for b in range(NB):
            at = jnp.int32(0)
            for j in range(n_slots):
                at = jnp.where(PGS[group, 0, j] == seq * NB + b, j, at)
            block = TOK[lax.div(at, 4), lax.rem(lax.div(at, 2), 2), lax.rem(at, 2)]
            X[b * BS : (b + 1) * BS] = block.astype(F32)
            XL[0, b * BS : (b + 1) * BS] = block

        send_kind(1)
        send_kind(2)

        PV, LG = r["PV"], r["LG"]
        if gather:
            ag_ready("small")
            lane = lanes((1, 128))
            for l in range(LAYERS):
                for first_row, count, width, kind_row in ((0, 20, widths[0], 0), (20, 4, widths[1], 2)):
                    tiles = [jnp.zeros((1, 128), F32)] * count
                    for device in range(n_blk * n_wa):
                        t, offset = divmod(device * width, 128)
                        dz, dw = divmod(device, n_wa)
                        piece = SP[dz, dw // 2, dw % 2, kind_row + l : kind_row + l + 1, :]
                        if offset:
                            piece = turn(piece, offset)
                        if offset + width <= 128:
                            tiles[t] = tiles[t] + piece
                        else:
                            tiles[t] = tiles[t] + jnp.where(lane >= offset, piece, 0.0)
                            tiles[t + 1] = tiles[t + 1] + jnp.where(lane < offset, piece, 0.0)
                    for t in range(count):
                        PV[l, first_row + t : first_row + t + 1, :] = tiles[t]
                for h in range(H):
                    for i in range(NB):
                        LG[l, h, i : i + 1, :] = SP[h, i // 2, i % 2, 4 + l : 5 + l, :]

        def wide(l, row):
            return jnp.concatenate([PV[l, row : row + 1, :], PV[l, row + 1 : row + 2, :]], axis=1)

        def mine(l, row):
            return jnp.where(c == 0, PV[l, row : row + 1, :], PV[l, row + 1 : row + 2, :])

        BIAS = r["BIAS"]
        spread = lax.broadcasted_iota(jnp.int32, (16, SEQ), 1) // BS
        spread = (spread == lax.broadcasted_iota(jnp.int32, (16, SEQ), 0)).astype(F32).astype(BF16)

        def over_rows(table):
            table = jnp.concatenate([table, jnp.zeros_like(table)], axis=0).astype(BF16)
            return tn(table, spread)[0:NB]

        for h in (0, 1):
            allowed = over_rows(r["block_mask"][2 * c + h].astype(F32)) > 0.5
            for l in range(LAYERS):
                logit = over_rows(LG[l, 2 * c + h])
                log_sig = jnp.minimum(logit, 0.0) - jnp.log1p(jnp.exp(-jnp.abs(logit)))
                BIAS[l, h] = jnp.where(allowed, log_sig, NEG)

        PSEND, PRECV = r["PSEND"], r["PRECV"]
        exchange_out = links.send_sem(PSEND)
        exchange_in = [links.recv_sem() for _ in range(4)]

        def give(step, chunk, value):
            PSEND[step, chunk] = value.astype(BF16)
            sem = exchange_in[2 * (step % 2) + chunk]
            links.push(PSEND.at[step, chunk], PRECV.at[step, chunk], exchange_out, sem, partner)

        def take(step, chunk):
            links.arrived(PRECV.at[step, chunk], exchange_in[2 * (step % 2) + chunk])

        def of_head(value, h):
            keep = (lanes(value.shape) // HD) == h
            return jnp.where(keep, value, jnp.zeros_like(value))

        def rows_of(chunk):
            return slice(chunk * HALF, (chunk + 1) * HALF)

        YB, SND, RET = ((r[name + "0"], r[name + "1"]) for name in ("YB", "SND", "RET"))

        def send_back(which):
            for dest in range(n_blk):
                for j in range(2):
                    position = lax.rem(PGS[group, 0, dest * BLK_DEV + 2 * c + j], NB)
                    SND[which][dest, j] = YB[which][position]
                here = jnp.logical_and(dest == z, c == group)
                sems = (r["ret_send"].at[which], r["ret_recv"].at[which])
                target = RET[which].at[seq, c]
                move(here, SND[which].at[dest], target, *sems, local_sems.at[4 + which], (dest, p * 2 + group))

        def return_pieces(which):
            return lambda n: SND[which].at[pl.ds(0, n)]

        def take_back(which, target_ref):
            wait_pieces(return_pieces(which), 2 * n_seq, r["ret_recv"].at[which], local_sems.at[4 + which], False)
            for j in range(BLK_DEV):
                from_seq = lax.div(place_smem[0, z * BLK_DEV + j], NB)
                target_ref[j] = RET[which][from_seq, j // 2, j % 2].astype(F32)

        QKV, KT, VT, PR, AT, AN, AX = (r[n] for n in ("QKV", "KT", "VT", "PR", "AT", "AN", "AX"))
        ST, DS, PO, FS, G, GP, Y1B = (r[n] for n in ("ST", "DS", "PO", "FS", "G", "GP", "Y1B"))
        U1, R1, U2, R2 = (r[n] for n in ("U1", "R1", "U2", "R2"))
        WO = r["WO"]
        attended_out, attended_in = links.send_sem(AX), links.recv_sem()
        if gather:
            wo_out = links.send_sem(r["WOX"])

        def weight(kind, l):
            if gather:
                ref = weight_refs[kind]
                return ref[l].reshape(ref.shape[1] * ref.shape[2] * ref.shape[3], ref.shape[4])
            return (r["WA"], r["WI"], r["WD"])[kind][l]

        def weight_qkv(l):
            if gather:
                return WA[l, :, :, :, 0:384].reshape(D, 384)
            return r["WA"][l, :, 0:384]

        for l in range(LAYERS):
            step = 2 * l
            if gather:
                ag_ready((0, l))
                part = n_blk // 2
                wo_in = links.recv_sem()
                theirs = WA.at[l, pl.ds((1 - c) * part, part), :, :, pl.ds(384, 128)]
                links.push(theirs, r["WOX"].at[l], wo_out, wo_in, partner)
                WO[l, :, my_cols] = WA[l, pl.ds(c * part, part), :, :, 384:512].reshape(128, 128)
            bias = jnp.concatenate([mine(l, ROW_BQ), jnp.zeros((1, 128), F32), mine(l, ROW_BV)], axis=1)
            scale = jnp.where(lanes((1, 384)) < 128, 0.125, 1.0)
            for chunk in range(2):
                rows = rows_of(chunk)
                QKV[l, rows] = ((nn(XL[l, rows], weight_qkv(l)) + bias) * scale).astype(BF16)
            keys = QKV[l, :, 128:256]
            KT[l] = keys.astype(F32).T.astype(BF16)
            VT[...] = QKV[l, :, 256:384].astype(F32).T.astype(BF16)
            if gather:
                if l + 1 < LAYERS:
                    ag_xy((1, l + 1))
                    ag_xy((2, l + 1))
                links.arrived(r["WOX"].at[l], wo_in)
                WO[l, :, other_cols] = r["WOX"][l].reshape(128, 128)
            for chunk in range(2):
                rows = rows_of(chunk)
                for h in (0, 1):
                    queries = of_head(QKV[l, rows, 0:128], h)
                    ST[...] = nt(keys, queries)
                    top = jnp.full((8, HALF), NEG, F32)
                    for kb in range(NB):
                        score = ST[kb * BS : (kb + 1) * BS] + BIAS[l, h, kb : kb + 1, rows]
                        top = jnp.maximum(top, jnp.max(score.reshape(8, 8, HALF), axis=0))
                    top = jnp.max(top, axis=0, keepdims=True)
                    total = jnp.zeros((8, HALF), F32)
                    for kb in range(NB):
                        score = ST[kb * BS : (kb + 1) * BS] + BIAS[l, h, kb : kb + 1, rows]
                        weight_of = jnp.exp(score - top)
                        ST[kb * BS : (kb + 1) * BS] = weight_of
                        total = total + fold(weight_of)
                    inverse = 1.0 / column_sum(total)
                    for kb in range(NB):
                        PR[l, h, kb * BS : (kb + 1) * BS, rows] = (ST[kb * BS : (kb + 1) * BS] * inverse).astype(BF16)
                    AT[l, h * HD : (h + 1) * HD, rows] = nn(VT[h * HD : (h + 1) * HD], PR[l, h, :, rows])
                AN[l, rows] = AT[l, :, rows].T.astype(BF16)
                branch = nn(AN[l, rows], WO[l])
                give(step, chunk, branch)
                PO[rows] = X[rows] + branch + wide(l, ROW_BO)
                part = pl.ds(chunk * HALF, HALF)
                links.push(AN.at[l, part], AX.at[l, part], attended_out, attended_in, partner)
            if gather:
                if l + 1 < LAYERS:
                    ag_pass((0, l + 1))
                    ag_pass((1, l + 1))
                    ag_pass((2, l + 1))
                ag_ready((1, l))
                ag_ready((2, l))
            for chunk in range(2):
                rows = rows_of(chunk)
                take(step, chunk)
                gain, shift = wide(l, ROW_G1), wide(l, ROW_S1)
                for t in range(0, HALF, BS):
                    tile = slice(chunk * HALF + t, chunk * HALF + t + BS)
                    hidden = PO[tile] + PRECV[step, chunk, t : t + BS].astype(F32)
                    normed, unit, rstd = layer_norm(hidden, gain, shift)
                    U1[l, tile] = unit
                    R1[l, tile] = rstd
                    X[tile] = normed
                    Y1B[l, tile] = normed.astype(BF16)
                FS[...] = nn(Y1B[l, rows], weight(1, l))
                inner_bias = []
                for t in range(4):
                    row = ROW_BI + 2 * t
                    inner_bias.append(pick_groups(PV[l, row : row + 1, :], PV[l, row + 1 : row + 2, :], c))
                inner_bias = jnp.concatenate(inner_bias, axis=1)
                for t in range(0, HALF, 32):
                    tile = slice(chunk * HALF + t, chunk * HALF + t + 32)
                    inner = FS[t : t + 32] + inner_bias
                    below = 0.5 + 0.5 * lax.erf(inner * 0.7071067811865476)
                    G[l, tile] = (inner * below).astype(BF16)
                    slope = below + inner * (jnp.exp(inner * inner * -0.5) * 0.3989422804014327)
                    GP[l, tile] = slope.astype(BF16)
                branch = nn(G[l, rows], weight(2, l))
                give(step + 1, chunk, branch)
                PO[rows] = X[rows] + branch + wide(l, ROW_BD)
            for chunk in range(2):
                take(step + 1, chunk)
                gain, shift = wide(l, ROW_G2), wide(l, ROW_S2)
                for t in range(0, HALF, BS):
                    tile = slice(chunk * HALF + t, chunk * HALF + t + BS)
                    hidden = PO[tile] + PRECV[step + 1, chunk, t : t + BS].astype(F32)
                    normed, unit, rstd = layer_norm(hidden, gain, shift)
                    U2[l, tile] = unit
                    R2[l, tile] = rstd
                    X[tile] = normed
                    if l + 1 < LAYERS:
                        XL[l + 1, tile] = normed.astype(BF16)
                    else:
                        YB[0][chunk * 4 + t // BS] = normed.astype(BF16)
        send_back(0)

        DY, DD, DF, DH, DO, DA, DAT, DQKV = (r[n] for n in ("DY", "DD", "DF", "DH", "DO", "DA", "DAT", "DQKV"))
        LR, SGL = r["LR"], r["SGL"]
        take_kind(1)
        take_kind(2)
        grads_in = links.recv_sem()
        links.push(MG.at[:, c], MG.at[:, c], links.send_sem(MG.at[:, 0]), grads_in, partner)
        links.arrived(MG.at[:, 0], grads_in)
        wanted = []
        lane = lanes((1, 128))
        for t in range(n_blk // 2):
            wanted.append(jnp.where(lane < 64, MR[2 * t, 0:1, :], MR[2 * t + 1, 0:1, :]))
        wanted = jnp.concatenate(wanted, axis=1) - seq * SEQ
        listed = MG[...].reshape(n_blk * 64, D)
        for chunk in range(2):
            row_ids = lax.broadcasted_iota(jnp.int32, (HALF, n_blk * 64), 0) + chunk * HALF
            DY[rows_of(chunk)] = nn((row_ids == wanted).astype(F32).astype(BF16), listed)

        rs_recv = {}
        if gather:
            rs_out = {kind: (links.send_sem(r["RP_" + kind]), links.send_sem(r["RZ_" + kind])) for kind in RS_KINDS}

        def rs_start(kind, l):
            if not gather:
                return
            rs_recv[kind, l] = [links.recv_sem() for _ in range(3)]
            grad, parts, sem = r["G_" + kind], r["RP_" + kind], rs_recv[kind, l][0]
            out = rs_out[kind][0]
            links.push(grad.at[l, z_low, p ^ 3], parts.at[l, 0, 1], out, sem, x_peer)
            links.push(grad.at[l, z_high, p ^ 3], parts.at[l, 1, 1], out, sem, y_peer)
            links.push(grad.at[l, z_low, p ^ 1], parts.at[l, 0, 0], out, sem, x_peer)
            links.push(grad.at[l, z_high, p ^ 2], parts.at[l, 1, 0], out, sem, y_peer)

        def rs_pass(kind, l):
            if not gather:
                return
            grad, parts, sem = r["G_" + kind], r["RP_" + kind], rs_recv[kind, l][1]
            links.arrived(parts.at[l, :, 0:2], rs_recv[kind, l][0])
            parts[l, 0, 1] = (grad[l, z_low, p ^ 2].astype(F32) + parts[l, 0, 1].astype(F32)).astype(BF16)
            links.push(parts.at[l, 0, 1], parts.at[l, 1, 2], rs_out[kind][0], sem, y_peer)
            parts[l, 1, 1] = (grad[l, z_high, p ^ 1].astype(F32) + parts[l, 1, 1].astype(F32)).astype(BF16)
            links.push(parts.at[l, 1, 1], parts.at[l, 0, 2], rs_out[kind][0], sem, x_peer)

        def rs_z(kind, l):
            if not gather:
                return
            grad, parts, total = r["G_" + kind], r["RP_" + kind], r["SZ_" + kind]
            links.arrived(parts.at[l, :, 2], rs_recv[kind, l][1])
            for half, straight, passed in ((z_low, 0, 1), (z_high, 1, 0)):
                value = grad[l, half, p].astype(F32) + parts[l, straight, 0].astype(F32) + parts[l, passed, 2].astype(F32)
                total[l, half] = value.astype(BF16)
            for m in range(1, n_blk):
                links.push(total.at[l, z ^ m], r["RZ_" + kind].at[l, m - 1], rs_out[kind][1], rs_recv[kind, l][2], (z ^ m, w))

        def rs_end(kind, l):
            total = r["SZ_" + kind][l, z].astype(F32)
            links.arrived(r["RZ_" + kind].at[l], rs_recv[kind, l][2])
            for m in range(1, n_blk):
                total = total + r["RZ_" + kind][l, m - 1].astype(F32)
            return total

        sg_recv = {}
        if gather:
            sg_out = (links.send_sem(r["SGP"]), links.send_sem(r["SGZ"]))

        def small_start(l):
            if not gather:
                return
            sg_recv[l] = [links.recv_sem() for _ in range(2)]
            for m in range(1, n_plane):
                links.push(SGL.at[l], r["SGP"].at[l, m - 1], sg_out[0], sg_recv[l][0], (z, w ^ (2 * m)))

        def small_z(l):
            if not gather:
                return
            links.arrived(r["SGP"].at[l], sg_recv[l][0])
            total = SGL[l]
            for m in range(1, n_plane):
                total = total + r["SGP"][l, m - 1]
            r["SGS"][l] = total
            for m in range(1, n_blk):
                links.push(r["SGS"].at[l], r["SGZ"].at[l, m - 1], sg_out[1], sg_recv[l][1], (z ^ m, w))

        def small_end(l):
            links.arrived(r["SGZ"].at[l], sg_recv[l][1])
            total = r["SGS"][l]
            for m in range(1, n_blk):
                total = total + r["SGZ"][l, m - 1]
            return total

        def store_grad(kind, l, value):
            if gather:
                shape = r["G_" + kind].shape
                r["G_" + kind][l] = value.astype(BF16).reshape(shape[1:])
            else:
                r["G_" + kind][l] = value

        def two_rows(l, row, value):
            SGL[l, row : row + 1, :] = value[:, 0:128]
            SGL[l, row + 1 : row + 2, :] = value[:, 128:256]

        SGL[...] = jnp.zeros_like(SGL)
        for l in reversed(range(LAYERS)):
            step = 4 + 2 * (LAYERS - 1 - l)
            gain = wide(l, ROW_G2)
            sums = [jnp.zeros((8, D), F32) for _ in range(3)]
            inner_sum = jnp.zeros((8, MY_FF), F32)
            for chunk in range(2):
                rows = rows_of(chunk)
                for t in range(0, HALF, BS):
                    tile = slice(chunk * HALF + t, chunk * HALF + t + BS)
                    grad, unit = DY[tile], U2[l, tile]
                    if l < LAYERS - 1:
                        if t == 0:
                            take(step - 1, chunk)
                        grad = grad + PRECV[step - 1, chunk, t : t + BS].astype(F32)
                    d_hidden = layer_norm_back(grad, unit, R2[l, tile], gain)
                    low = d_hidden.astype(BF16)
                    DH[tile] = d_hidden
                    DD[tile] = low
                    sums[0] = sums[0] + fold(grad * unit)
                    sums[1] = sums[1] + fold(grad)
                    sums[2] = sums[2] + fold(low.astype(F32))
                FS[...] = nt(DD[rows], weight(2, l))
                for t in range(0, HALF, 32):
                    tile = slice(chunk * HALF + t, chunk * HALF + t + 32)
                    d_inner = (FS[t : t + 32] * GP[l, tile].astype(F32)).astype(BF16)
                    DF[tile] = d_inner
                    inner_sum = inner_sum + fold(d_inner.astype(F32))
                branch = nt(DF[rows], weight(1, l))
                give(step, chunk, branch)
                DH[rows] = DH[rows] + branch
            two_rows(l, SG_G2, column_sum(sums[0]))
            two_rows(l, SG_S2, column_sum(sums[1]))
            two_rows(l, SG_BD, column_sum(sums[2]))
            inner_sum = column_sum(inner_sum)
            for t in range(4):
                SGL[l, SG_BI + t : SG_BI + t + 1, :] = inner_sum[:, 128 * t : 128 * t + 128]
            store_grad("d", l, tn(G[l], DD[...]))
            rs_start("d", l)
            store_grad("i", l, tn(Y1B[l], DF[...]))
            rs_start("i", l)
            if l < LAYERS - 1:
                rs_pass("q", l + 1)
                rs_z("d", l + 1)
            gain = wide(l, ROW_G1)
            sums = [jnp.zeros((8, D), F32) for _ in range(3)]
            for chunk in range(2):
                rows = rows_of(chunk)
                take(step, chunk)
                for t in range(0, HALF, BS):
                    tile = slice(chunk * HALF + t, chunk * HALF + t + BS)
                    grad = DH[tile] + PRECV[step, chunk, t : t + BS].astype(F32)
                    unit = U1[l, tile]
                    d_hidden = layer_norm_back(grad, unit, R1[l, tile], gain)
                    low = d_hidden.astype(BF16)
                    DH[tile] = d_hidden
                    DO[tile] = low
                    sums[0] = sums[0] + fold(grad * unit)
                    sums[1] = sums[1] + fold(grad)
                    sums[2] = sums[2] + fold(low.astype(F32))
                DA[rows] = nt(DO[rows], WO[l]).astype(BF16)
                DAT[:, rows] = nt(WO[l], DO[rows]).astype(BF16).astype(F32)
            two_rows(l, SG_G1, column_sum(sums[0]))
            two_rows(l, SG_S1, column_sum(sums[1]))
            two_rows(l, SG_BO, column_sum(sums[2]))
            if l == LAYERS - 1:
                links.arrived(AX, attended_in)
            own_part = tn(AN[l], DO[:, my_cols])
            other_part = tn(AX[l], DO[:, my_cols])
            if gather:
                part = n_blk // 2
                shape = (part, n_plane, 16, 128)
                r["G_o"][l, pl.ds(c * part, part)] = own_part.astype(BF16).reshape(shape)
                r["G_o"][l, pl.ds((1 - c) * part, part)] = other_part.astype(BF16).reshape(shape)
            else:
                r["G_o"][l, c] = own_part
                r["G_o"][l, 1 - c] = other_part
            rs_start("o", l)
            if l < LAYERS - 1:
                rs_z("i", l + 1)
                small_z(l + 1)
            keys, values = QKV[l, :, 128:256], QKV[l, :, 256:384]
            for chunk in range(2):
                rows = rows_of(chunk)
                d_query = []
                for h in (0, 1):
                    head = slice(h * HD, (h + 1) * HD)
                    ST[...] = nt(values, of_head(DA[rows], h))
                    inner = column_sum(DAT[head, rows] * AT[l, head, rows])
                    for kb in range(NB):
                        block = slice(kb * BS, (kb + 1) * BS)
                        d_score = PR[l, h, block, rows].astype(F32) * (ST[block] - inner)
                        DS[h, block, rows] = d_score.astype(BF16)
                        LR[h, kb : kb + 1, rows] = column_sum(fold(d_score))
                    d_query.append(nn(KT[l, head], DS[h, :, rows]))
                d_query = jnp.concatenate(d_query, axis=0) * 0.125
                DQKV[rows, 0:128] = d_query.T.astype(BF16)
                if l == LAYERS - 1:
                    if chunk == 1:
                        rs_pass("d", l)
                else:
                    rs_z("oq"[chunk], l + 1)
                    rs_pass("di"[chunk], l)
            d_keys = jnp.zeros((SEQ, 128), F32)
            d_values = jnp.zeros((SEQ, 128), F32)
            for h in (0, 1):
                d_keys = d_keys + nn(DS[h], of_head(QKV[l, :, 0:128], h))
                d_values = d_values + nn(PR[l, h], of_head(DA[...], h))
            DQKV[:, 128:256] = d_keys.astype(BF16)
            DQKV[:, 256:384] = d_values.astype(BF16)
            by_block = lax.broadcasted_iota(jnp.int32, (128, SEQ), 1) // BS
            by_block = (by_block == lax.broadcasted_iota(jnp.int32, (128, SEQ), 0)).astype(F32)
            for h in (0, 1):
                table = lax.dot_general(
                    LR[h], by_block, (((1,), (1,)), ((), ())), preferred_element_type=F32, precision=HIGHEST
                )
                SGL[l, SG_LG + 8 * h : SG_LG + 8 * h + 8, :] = table
            for chunk in range(2):
                rows = rows_of(chunk)
                branch = nt(DQKV[rows], weight_qkv(l))
                give(step + 1, chunk, branch)
                DY[rows] = DH[rows] + branch
            store_grad("q", l, tn(XL[l], DQKV[...]))
            rs_start("q", l)
            SGL[l, SG_BQ : SG_BQ + 1, :] = column_sum(fold(DQKV[:, 0:128].astype(F32)))
            SGL[l, SG_BV : SG_BV + 1, :] = column_sum(fold(DQKV[:, 256:384].astype(F32)))
            small_start(l)
            if l == LAYERS - 1:
                rs_pass("i", l)
            rs_pass("o", l)
        for chunk in range(2):
            take(step + 1, chunk)
            for t in range(0, HALF, BS):
                tile = slice(chunk * HALF + t, chunk * HALF + t + BS)
                grad = DY[tile] + PRECV[step + 1, chunk, t : t + BS].astype(F32)
                YB[1][chunk * 4 + t // BS] = grad.astype(BF16)
        send_back(1)
        SGF = r["SGF"]
        if gather:
            rs_z("d", 0)
            rs_z("i", 0)
            rs_pass("q", 0)
            rs_z("o", 0)
            small_z(0)
            FX, RX = r["FX"], r["RX"]
            kept = {}

            def finish(kind, l, at):
                total = rs_end(kind, l)
                width = total.shape[1]
                kept[kind, l] = jnp.where(c == 0, total[0:8], total[8:16])
                FX[l, :, at : at + width] = jnp.where(c == 0, total[8:16], total[0:8])

            for l in reversed(range(LAYERS)):
                r["gdown"][l] = rs_end("d", l)
                finish("i", l, 512)
                if l > 0:
                    finish("o", l, 384)
                    finish("q", l, 0)
                    SGF[c, l] = small_end(l)
                if l == LAYERS - 1:
                    rs_z("q", 0)
        take_back(0, r["out"])
        if gather:
            finish("o", 0, 384)
            SGF[c, 0] = small_end(0)
            sgf_in = links.recv_sem()
            links.push(SGF.at[c], SGF.at[c], links.send_sem(SGF.at[0]), sgf_in, partner)
            finish("q", 0, 0)
            fx_in = links.recv_sem()
            links.push(FX, RX, links.send_sem(FX), fx_in, partner)
            links.arrived(SGF.at[0], sgf_in)
        else:
            SGF[c] = SGL[...]
            SGF[1 - c] = jnp.zeros(SGL.shape, F32)
        for l in range(LAYERS):

            def put(at, value):
                if gather:
                    r["BT"][l, at : at + 1, :] = value
                elif at < ROW_G1:
                    r["gbias"][l : l + 1, 128 * at : 128 * at + 128] = value
                else:
                    at -= ROW_G1
                    r["ggain"][l : l + 1, 128 * at : 128 * at + 128] = value

            def row(core, at):
                return SGF[core, l, at : at + 1, :]

            for core in (0, 1):
                put(ROW_BQ + core, row(core, SG_BQ))
                put(ROW_BV + core, row(core, SG_BV))
                if not gather:
                    for h in (0, 1):
                        r["glog"][l, 2 * core + h] = SGF[core, l, SG_LG + 8 * h : SG_LG + 8 * h + 8, :]
            singles = ((ROW_BO, SG_BO), (ROW_S1, SG_S1), (ROW_BD, SG_BD), (ROW_S2, SG_S2), (ROW_G1, SG_G1), (ROW_G2, SG_G2))
            for at, source in singles:
                for j in (0, 1):
                    put(at + j, row(0, source + j))
            for t in range(4):
                first, second = weave_groups(row(0, SG_BI + t), row(1, SG_BI + t))
                put(ROW_BI + 2 * t, first)
                put(ROW_BI + 2 * t + 1, second)
            if gather:
                index = z * n_wa + w
                lane = lanes((1, 128))

                def entries(first_row, width):
                    start = index * width
                    tile, offset = lax.div(start, 128), lax.rem(start, 128)
                    shift = lax.rem(128 - offset, 128)
                    first = pltpu.roll(r["BT"][l, pl.ds(first_row + tile, 1), :], shift, 1)
                    if 128 % width == 0:
                        return first[:, 0:width]
                    second = pltpu.roll(r["BT"][l, pl.ds(first_row + tile + 1, 1), :], shift, 1)
                    return jnp.where(lane < 128 - offset, first, second)[:, 0:width]

                r["gbias"][l : l + 1, :] = entries(0, widths[0])
                r["ggain"][l : l + 1, :] = entries(ROW_G1, widths[1])
                table = SGF[lax.div(z, 2), l, pl.ds(SG_LG + 8 * lax.rem(z, 2), 8), :]
                wide_lane = lanes((8, 128))
                column = jnp.sum(jnp.where(wide_lane == w, table, 0.0), axis=1, keepdims=True)
                diagonal = wide_lane == lax.broadcasted_iota(jnp.int32, (8, 128), 0)
                values_row = column_sum(jnp.where(diagonal, column, 0.0))[:, 0:NB]
                logit = r["mask_logits"][...].astype(F32)[l : l + 1]
                r["glog"][l : l + 1, :] = values_row / (1.0 + jnp.exp(logit))
        if gather:
            links.arrived(RX, fx_in)
            for l in range(LAYERS):
                own = jnp.concatenate([kept[kind, l] for kind in ("q", "o", "i")], axis=1)
                other = RX[l]
                zero = jnp.where(c == 0, own, other)
                one = jnp.where(c == 0, other, own)
                for j in range(3):
                    r["gqkv"][l, :, 256 * j : 256 * j + 128] = zero[:, 128 * j : 128 * j + 128]
                    r["gqkv"][l, :, 256 * j + 128 : 256 * j + 256] = one[:, 128 * j : 128 * j + 128]
                r["gout"][l, :, 0:128] = zero[:, 384:512]
                r["gout"][l, :, 128:256] = one[:, 384:512]
                for t in range(4):
                    at = 512 + 128 * t
                    first, second = weave_groups(zero[:, at : at + 128], one[:, at : at + 128])
                    r["gin"][l, :, 256 * t : 256 * t + 128] = first
                    r["gin"][l, :, 256 * t + 128 : 256 * t + 256] = second
        take_back(1, r["gtok"])
        links.drain()
        for kind in range(3):
            wait_pieces(token_pieces(kind), 2 * n_seq, r["tok_send"].at[kind], None, True)
        for which in range(2):
            wait_pieces(return_pieces(which), n_blk, r["ret_send"].at[which], None, True)

    return kernel


def call_kernel(n_blk, n_wa, gather, named):
    vmem = pl.BlockSpec(memory_space=pltpu.VMEM)
    smem = pl.BlockSpec(memory_space=pltpu.SMEM)
    in_names = list(named)
    shapes = dict(out=(BLK_DEV, BS, D), gtok=(BLK_DEV, BS, D))
    if gather:
        sources = ("w_qkv", "w_out", "w_in", "w_down", "biases", "gains", "mask_logits")
        results = ("gqkv", "gout", "gin", "gdown", "gbias", "ggain", "glog")
        shapes.update({result: named[source].shape for result, source in zip(results, sources)})
    else:
        shapes.update(
            gbias=(LAYERS, 6 * D + FF),
            ggain=(LAYERS, 2 * D),
            glog=(LAYERS, H, NB, 128),
            G_d=(LAYERS, MY_FF, D),
            G_i=(LAYERS, D, MY_FF),
            G_o=(LAYERS, 2, 128, 128),
            G_q=(LAYERS, D, 384),
        )
    hold = pltpu.VMEM if gather else jax.ShapeDtypeStruct
    scratch = scratch_shapes(n_blk, n_wa, gather)
    kernel = make_kernel(n_blk, n_wa, gather, in_names, list(shapes), list(scratch))
    results = pl.pallas_call(
        kernel,
        out_shape=[hold(shape, F32) for shape in shapes.values()],
        in_specs=[smem if name in ("place_smem", "masked_count") else vmem for name in in_names],
        out_specs=[vmem] * len(shapes),
        scratch_shapes=list(scratch.values()),
        compiler_params=pltpu.CompilerParams(
            collective_id=0, has_side_effects=True, vmem_limit_bytes=60 * 2**20
        ),
        name="encoder",
    )(*named.values())
    if gather:
        results = pl.pallas_call(
            write_out,
            out_shape=[jax.ShapeDtypeStruct(shape, F32) for shape in shapes.values()],
            in_specs=[vmem] * len(shapes),
            out_specs=[pl.BlockSpec(memory_space=pl.ANY)] * len(shapes),
            scratch_shapes=[pltpu.SemaphoreType.DMA((len(shapes),))],
            name="write_out",
        )(*[pltpu.with_memory_space_constraint(result, pltpu.VMEM) for result in results])
    return dict(zip(shapes, results))


def write_out(*refs):
    count = (len(refs) - 1) // 2
    sems = refs[-1]
    copies = [pltpu.make_async_copy(refs[k], refs[count + k], sems.at[k]) for k in range(count)]
    for copy in copies:
        copy.start()
    for copy in copies:
        copy.wait()


def local(
    tokens,
    placement,
    block_mask,
    w_qkv,
    w_out,
    w_in,
    w_down,
    biases,
    gains,
    mask_logits,
    masked_pos,
    masked_count,
    masked_grad,
):
    n_blk, n_wa = lax.axis_size("blk"), lax.axis_size("wa")
    both = ("blk", "wa")
    core = lax.rem(lax.axis_index("wa"), 2)
    gather = w_qkv.shape[1] == 8 and n_blk == H and n_wa == NB
    named = dict(
        tokens=tokens.reshape(BLK_DEV, BS, D),
        place_smem=placement,
        place_vmem=placement,
        block_mask=block_mask,
        masked_pos=masked_pos.reshape(1, -1),
        masked_count=masked_count,
        masked_grad=masked_grad.reshape(-1, D),
    )
    if gather:
        named.update(
            w_qkv=w_qkv, w_out=w_out, w_in=w_in, w_down=w_down, biases=biases, gains=gains, mask_logits=mask_logits
        )
    else:
        shards = (w_qkv, w_out, w_in, w_down, biases, gains, mask_logits)
        whole = [lax.all_gather(shard, both, axis=1, tiled=True) for shard in shards]
        qkv = lax.dynamic_index_in_dim(whole[0].reshape(LAYERS, D, 3, 2, 128), core, 3, False)
        qkv = qkv.reshape(LAYERS, D, 384)
        inner = lax.dynamic_index_in_dim(whole[2].reshape(LAYERS, D, 16, 2, 32), core, 3, False)
        down = lax.dynamic_index_in_dim(whole[3].reshape(LAYERS, 16, 2, 32, D), core, 2, False)
        vectors = jnp.concatenate([whole[4], whole[5]], axis=1).astype(F32)
        logits = whole[6].astype(F32).reshape(LAYERS, H, NB, NB)
        named.update(
            WA=qkv,
            WO=lax.dynamic_slice_in_dim(whole[1], core * 128, 128, axis=1),
            WI=inner.reshape(LAYERS, D, MY_FF),
            WD=down.reshape(LAYERS, MY_FF, D),
            PV=vectors.reshape(LAYERS, PV_ROWS, 128),
            LG=jnp.pad(logits, ((0, 0), (0, 0), (0, 0), (0, 128 - NB))),
        )
    got = call_kernel(n_blk, n_wa, gather, named)
    if gather:
        weight_grads = (got["gqkv"], got["gout"], got["gin"], got["gdown"])
        small = (got["gbias"], got["ggain"], got["glog"])
    else:
        grad_logits = jnp.swapaxes(got["glog"][..., 0:NB], 2, 3).reshape(LAYERS, H * NB * NB)

        def one_core(part, axis):
            halves = [jnp.where(core == side, part, 0.0) for side in (0, 1)]
            return jnp.stack(halves, axis=axis)

        whole = (
            one_core(got["G_q"].reshape(LAYERS, D, 3, 128), 3).reshape(LAYERS, D, 3 * D),
            one_core(got["G_o"].reshape(LAYERS, D, 128), 2).reshape(LAYERS, D, D),
            one_core(got["G_i"].reshape(LAYERS, D, 16, 32), 3).reshape(LAYERS, D, FF),
            one_core(got["G_d"].reshape(LAYERS, 16, 32, D), 2).reshape(LAYERS, FF, D),
            got["gbias"],
            got["ggain"],
            grad_logits,
        )
        summed = [lax.psum_scatter(part, both, scatter_dimension=1, tiled=True) for part in whole]
        grad_mask = summed[6] * jax.nn.sigmoid(-mask_logits.astype(F32))
        weight_grads, small = tuple(summed[:4]), (summed[4], summed[5], grad_mask)
    return (
        got["out"].reshape(tokens.shape),
        got["gtok"].reshape(tokens.shape),
        *weight_grads,
        *small,
    )


def solution(mesh):
    placed = (
        P("wa", "blk", None, None),
        P("wa", None),
        P(),
        P(None, ("blk", "wa"), None),
        P(None, ("blk", "wa"), None),
        P(None, ("blk", "wa"), None),
        P(None, ("blk", "wa"), None),
        P(None, ("blk", "wa")),
        P(None, ("blk", "wa")),
        P(None, ("blk", "wa")),
        P("wa", "blk", None),
        P("wa", "blk"),
        P("wa", "blk", None, None),
    )
    return jax.shard_map(
        local,
        mesh=mesh,
        in_specs=placed,
        out_specs=(
            P("wa", "blk", None, None),
            P("wa", "blk", None, None),
            P(None, ("blk", "wa"), None),
            P(None, ("blk", "wa"), None),
            P(None, ("blk", "wa"), None),
            P(None, ("blk", "wa"), None),
            P(None, ("blk", "wa")),
            P(None, ("blk", "wa")),
            P(None, ("blk", "wa")),
        ),
        check_vma=False,
    )
```

```python
import functools

import jax
import jax.numpy as jnp
from jax import lax
from jax.experimental import pallas as pl
from jax.experimental.pallas import tpu as pltpu
from jax.sharding import PartitionSpec as P

D = 256
H = 4
HD = 64
FF = 1024
NB = 8
BS = 64
SEQ = 512
LAYERS = 2
BLK_DEV = 4
HALF = 512
CHUNKS = SEQ // HALF
FWD = 512
FWD_CHUNKS = SEQ // FWD
MY_FF = FF // 2
NEG = -1e30
EPS = 1e-05
MESH = pl.DeviceIdType.MESH
F32 = jnp.float32
BF16 = jnp.bfloat16
HIGHEST = lax.Precision.HIGHEST

ROW_BQ, ROW_BV, ROW_BO, ROW_S1, ROW_BI, ROW_BD, ROW_S2, ROW_G1, ROW_G2 = 0, 2, 4, 6, 8, 16, 18, 20, 22
PV_ROWS = 24
SG_BQ, SG_BV, SG_BI, SG_BO, SG_S1, SG_BD, SG_S2, SG_G1, SG_G2, SG_LG = 0, 1, 2, 6, 8, 10, 12, 14, 16, 24
SG_ROWS = 40
SLAB = 16
SLAB_ROWS = (
    (SG_BQ, SG_BV, SG_BO),
    (SG_BO + 1, SG_S1, SG_S1 + 1, SG_BI),
    (SG_BI + 1, SG_BI + 2, SG_BI + 3),
    (SG_BI + 3, SG_BD, SG_BD + 1, SG_S2, SG_S2 + 1),
)
SLAB_GAINS = (SG_G1, SG_G1 + 1, SG_G2, SG_G2 + 1)


def nn(left, right):
    return jnp.dot(left, right, preferred_element_type=F32)


def nt(left, right):
    return lax.dot_general(left, right, (((1,), (1,)), ((), ())), preferred_element_type=F32)


def tn(left, right):
    return lax.dot_general(left, right, (((0,), (0,)), ((), ())), preferred_element_type=F32)


def lanes(shape):
    return lax.broadcasted_iota(jnp.int32, shape, len(shape) - 1)


def turn(value, shift):
    return pltpu.roll(value, shift % 128, 1)


def pick_groups(first, second, core):
    if isinstance(core, int):
        if core == 1:
            first, second = turn(first, -32), turn(second, -32)
    else:
        first = jnp.where(core == 1, turn(first, -32), first)
        second = jnp.where(core == 1, turn(second, -32), second)
    group = lanes(first.shape) // 32
    return jnp.where(
        group == 0,
        first,
        jnp.where(group == 1, turn(first, -32), jnp.where(group == 2, turn(second, 64), turn(second, 32))),
    )


def weave_groups(zero, one):
    group = lanes(zero.shape) // 32
    first = jnp.where(
        group == 0, zero, jnp.where(group == 1, turn(one, 32), jnp.where(group == 2, turn(zero, 32), turn(one, 64)))
    )
    second = jnp.where(
        group == 0,
        turn(zero, -64),
        jnp.where(group == 1, turn(one, -32), jnp.where(group == 2, turn(zero, -32), one)),
    )
    return first, second


class Links:
    def __init__(self, send, recv, anyone):
        self.send, self.recv, self.anyone = send, recv, anyone
        self.send_used = self.recv_used = 0
        self.pending = {}
        self.pending_if = []

    def recv_sem(self):
        self.recv_used += 1
        return self.recv_used - 1

    def send_sem(self, bytes_like):
        self.send_used += 1
        self.pending[self.send_used - 1] = bytes_like
        return self.send_used - 1

    def send_sem_if(self, condition, bytes_like):
        self.send_used += 1
        self.pending_if.append((condition, self.send_used - 1, bytes_like))
        return self.send_used - 1

    def push(self, source, target, send_sem, recv_sem, device):
        remote(source, target, self.send.at[send_sem], self.recv.at[recv_sem], device).start()

    def arrived(self, bytes_like, recv_sem):
        remote(bytes_like, bytes_like, self.send.at[0], self.recv.at[recv_sem], self.anyone).wait_recv()

    def drain(self):
        for send_sem, bytes_like in self.pending.items():
            remote(bytes_like, bytes_like, self.send.at[send_sem], self.recv.at[0], self.anyone).wait_send()
        for condition, send_sem, bytes_like in self.pending_if:

            @pl.when(condition)
            def _():
                remote(bytes_like, bytes_like, self.send.at[send_sem], self.recv.at[0], self.anyone).wait_send()


def remote(source, target, send_sem, recv_sem, device):
    return pltpu.make_async_remote_copy(
        src_ref=source,
        dst_ref=target,
        send_sem=send_sem,
        recv_sem=recv_sem,
        device_id=device,
        device_id_type=MESH,
    )


def layer_norm(hidden, gain, shift):
    mean = jnp.sum(hidden, axis=1, keepdims=True) * (1.0 / D)
    centred = hidden - mean
    var = jnp.sum(centred * centred, axis=1, keepdims=True) * (1.0 / D)
    rstd = lax.rsqrt(var + EPS)
    unit = centred * rstd
    return unit * gain + shift, unit, rstd


def layer_norm_back(grad, unit, rstd, gain):
    scaled = grad * gain
    mean_one = jnp.sum(scaled, axis=1, keepdims=True) * (1.0 / D)
    mean_two = jnp.sum(scaled * unit, axis=1, keepdims=True) * (1.0 / D)
    return rstd * (scaled - mean_one - unit * mean_two)


def fold(value):
    rows, cols = value.shape
    return jnp.sum(value.reshape(rows // 8, 8, cols), axis=0)


def column_sum(value):
    return jnp.sum(value, axis=0, keepdims=True)


SEND_SEMS, RECV_SEMS = 46, 82


def scratch_shapes(n_blk, n_wa, gather):
    n_plane, n_seq = n_wa // 2, n_blk // 2
    vmem = pltpu.VMEM
    shapes = dict(
        TOK=vmem((n_blk, 2, 2, BS, D), BF16),
        MGS=vmem((2, 32, D), BF16),
        MRS=vmem((8, 128), jnp.int32),
        MG=vmem((n_blk, 2, 32, D), BF16),
        MR=vmem((n_blk, 8, 128), jnp.int32),
        PGV=vmem((2, 8, 128), jnp.int32),
        PGS=pltpu.SMEM((2, 8, 128), jnp.int32),
        YB0=vmem((NB, BS, D), BF16),
        YB1=vmem((NB, BS, D), BF16),
        SND0=vmem((n_blk, 2, BS, D), BF16),
        SND1=vmem((n_blk, 2, BS, D), BF16),
        RET0=vmem((n_seq, 2, 2, BS, D), BF16),
        RET1=vmem((n_seq, 2, 2, BS, D), BF16),
        PSEND=vmem((4 * LAYERS, SEQ, D), BF16),
        PRECV=vmem((4 * LAYERS, SEQ, D), BF16),
        X=vmem((SEQ, D), F32),
        XL=vmem((LAYERS, SEQ, D), BF16),
        QKV=vmem((LAYERS, SEQ, 384), BF16),
        KT=vmem((LAYERS, 128, SEQ), BF16),
        VT=vmem((128, SEQ), BF16),
        PR=vmem((LAYERS, 2, SEQ, SEQ), BF16),
        AT=vmem((LAYERS, 128, SEQ), F32),
        AN=vmem((LAYERS, SEQ, 128), BF16),
        AX=vmem((LAYERS, SEQ, 128), BF16),
        ST=vmem((SEQ, HALF), F32),
        DS=vmem((2, SEQ, SEQ), BF16),
        PO=vmem((SEQ, D), F32),
        U1=vmem((LAYERS, SEQ, D), F32),
        R1=vmem((LAYERS, SEQ, 1), F32),
        U2=vmem((LAYERS, SEQ, D), F32),
        R2=vmem((LAYERS, SEQ, 1), F32),
        Y1B=vmem((LAYERS, SEQ, D), BF16),
        FS=vmem((HALF, MY_FF), F32),
        G=vmem((LAYERS, SEQ, MY_FF), BF16),
        GP=vmem((LAYERS, SEQ, MY_FF), BF16),
        DY=vmem((SEQ, D), F32),
        DD=vmem((SEQ, D), BF16),
        DF=vmem((SEQ, MY_FF), BF16),
        DH=vmem((SEQ, D), F32),
        DO=vmem((SEQ, D), BF16),
        DA=vmem((SEQ, 128), BF16),
        DAT=vmem((128, SEQ), F32),
        DQKV=vmem((SEQ, 384), BF16),
        BIAS=vmem((LAYERS, 2, NB, SEQ), F32),
        LR=vmem((2, NB, SEQ), F32),
        SGL=vmem((LAYERS, SG_ROWS, 128), F32),
        SGF=vmem((2, LAYERS, SLAB if gather else SG_ROWS, 128), F32),
        link_send=pltpu.SemaphoreType.DMA((SEND_SEMS if gather else 8,)),
        link_recv=pltpu.SemaphoreType.DMA((RECV_SEMS if gather else 16,)),
        tok_send=pltpu.SemaphoreType.DMA((3,)),
        tok_recv=pltpu.SemaphoreType.DMA((3,)),
        ret_send=pltpu.SemaphoreType.DMA((2,)),
        ret_recv=pltpu.SemaphoreType.DMA((2,)),
        local_sems=pltpu.SemaphoreType.DMA((6,)),
    )
    if gather:
        shapes.update(
            WA=vmem((LAYERS, n_blk, n_plane, 16, 512), BF16),
            WI=vmem((LAYERS, n_blk, n_plane, 16, MY_FF), BF16),
            WD=vmem((LAYERS, n_blk, n_plane, 32, D), BF16),
            WO=vmem((LAYERS, 128, D), BF16),
            WOX=vmem((LAYERS, n_blk // 2, n_plane, 16, 128), BF16),
            PV=vmem((LAYERS, PV_ROWS, 128), F32),
            LG=vmem((LAYERS, H, NB, 128), F32),
            S0=vmem((2, 16, 512), BF16),
            R0=vmem((2, 16, 512), BF16),
            SP=vmem((n_blk, n_plane, 2, 8, 128), F32),
            FX=vmem((LAYERS, 8, 1024), F32),
            RX=vmem((LAYERS, 8, 1024), F32),
            SLO=vmem((LAYERS, n_blk, SLAB, 128), BF16),
            SLP=vmem((LAYERS, n_plane - 1, n_blk, SLAB, 128), BF16),
            SLS=vmem((LAYERS, n_blk, SLAB, 128), BF16),
            SLZ=vmem((LAYERS, n_blk - 1, SLAB, 128), BF16),
            BT=vmem((LAYERS, 8, 128), F32),
        )
        for kind, (rows, cols) in RS_KINDS.items():
            shapes["G_" + kind] = vmem((LAYERS, n_blk, n_plane, rows, cols), BF16)
            shapes["RP_" + kind] = vmem((LAYERS, 2, 3, n_blk // 2, rows, cols), BF16)
            shapes["SZ_" + kind] = vmem((LAYERS, n_blk, rows, cols), BF16)
            shapes["RZ_" + kind] = vmem((LAYERS, n_blk - 1, rows, cols), BF16)
    return shapes


RS_STRAIGHT = {("q", 0)}
RS_KINDS = {"d": (32, D), "i": (16, MY_FF), "o": (16, 128), "q": (16, 384)}


def make_kernel(n_blk, n_wa, gather, in_names, out_names, scratch_names):
    n_plane = n_wa // 2
    n_seq = n_blk // 2
    n_slots = n_blk * BLK_DEV

    def kernel(*refs):
        r = dict(zip(in_names + out_names + scratch_names, refs))
        place_smem = r["place_smem"]
        z = lax.axis_index("blk")
        w = lax.axis_index("wa")
        c = lax.rem(w, 2)
        p = lax.div(w, 2)
        group = lax.div(z, n_seq)
        seq = lax.rem(z, n_seq)
        partner = (z, p * 2 + (1 - c))
        links = Links(r["link_send"], r["link_recv"], partner)
        x_peer, y_peer = (z, w ^ 2), (z, w ^ 4)
        in_middle = jnp.logical_or(z == 1, z == 2)
        z_next, z_far = (z ^ 1, w), (2 - lax.div(z, 2), w)
        far_pair = pl.ds(2 - 2 * lax.div(z, 2), 2)
        local_sems = r["local_sems"]
        my_cols = pl.ds(pl.multiple_of(c * 128, 128), 128)
        other_cols = pl.ds(pl.multiple_of((1 - c) * 128, 128), 128)

        TOK, MGS, MRS, MG, MR = (r[name] for name in ("TOK", "MGS", "MRS", "MG", "MR"))
        PGV, PGS = r["PGV"], r["PGS"]
        PGV[c, 0:1, 0:n_slots] = r["place_vmem"][...]
        MGS[...] = r["masked_grad"][...].astype(BF16).reshape(2, 32, D)
        chosen = r["masked_pos"][...]
        slot_of = lax.shift_right_logical(chosen, 6)
        block_of = jnp.zeros_like(chosen)
        for j in range(BLK_DEV):
            block_of = jnp.where(slot_of == j, place_smem[0, z * BLK_DEV + j], block_of)
        target_row = block_of * BS + (chosen & (BS - 1))
        target_row = jnp.where(lanes(chosen.shape) < r["masked_count"][0, 0], target_row, -1)
        MRS[0:1, 0:64] = target_row
        MRS[0:1, 64:128] = target_row
        if gather:
            WA, WI, WD, SP = r["WA"], r["WI"], r["WD"], r["SP"]
            own_rows = ([], [])
            give_rows = ([], [])
            for l in range(LAYERS):
                qkv = r["w_qkv"][l].astype(F32)
                out_part = r["w_out"][l].astype(F32)
                inner = r["w_in"][l].astype(F32)
                sides = []
                for side in (0, 1):
                    at = 128 * side
                    attn = [qkv[:, 256 * j + at : 256 * j + at + 128] for j in range(3)]
                    attn = jnp.concatenate(attn + [out_part[:, at : at + 128]], axis=1)
                    feed = []
                    for t in range(4):
                        first = inner[:, 256 * t : 256 * t + 128]
                        second = inner[:, 256 * t + 128 : 256 * t + 256]
                        feed.append(pick_groups(first, second, side))
                    sides.append((attn, jnp.concatenate(feed, axis=1)))
                for kind in (0, 1):
                    own_rows[kind].append(jnp.where(c == 0, sides[0][kind], sides[1][kind]))
                    give_rows[kind].append(jnp.where(c == 0, sides[1][kind], sides[0][kind]))
                WD[l, z, p] = r["w_down"][l]
            for kind in (0, 1):
                r["S0"][kind] = jnp.concatenate(give_rows[kind], axis=0).astype(BF16)
            SP[z, p, c] = jnp.zeros((8, 128), F32)
            widths = []
            for at, name in ((0, "biases"), (2, "gains"), (4, "mask_logits")):
                part = r[name][...].astype(F32)
                widths.append(part.shape[1])
                SP[z, p, c, at : at + 2, 0 : part.shape[1]] = part

        barrier = pltpu.get_barrier_semaphore()
        greeted = 0
        for m in range(n_blk):
            for other in (0, 1):
                if m or other:
                    pl.semaphore_signal(barrier, inc=1, device_id=(z ^ m, w ^ other), device_id_type=MESH)
                    greeted += 1
        if gather:
            for m in range(1, n_plane):
                pl.semaphore_signal(barrier, inc=1, device_id=(z, w ^ (2 * m)), device_id_type=MESH)
                greeted += 1
        pl.semaphore_wait(barrier, greeted)

        place_in = links.recv_sem()
        links.push(PGV.at[c], PGV.at[c], links.send_sem(PGV.at[0]), place_in, partner)
        if gather:
            rows_in = links.recv_sem()
            links.push(r["S0"], r["R0"], links.send_sem(r["S0"]), rows_in, partner)
            small_in = links.recv_sem()
            links.push(SP.at[z, p, c], SP.at[z, p, c], links.send_sem(SP.at[0, 0, 0]), small_in, partner)

        at_home = c == group

        def move(here, source, target, send_sem, recv_sem, local_sem, device):
            @pl.when(jnp.logical_not(here))
            def _():
                remote(source, target, send_sem, recv_sem, device).start()

            @pl.when(here)
            def _():
                pltpu.make_async_copy(source, target, local_sem).start()

        def wait_pieces(pieces, count, sem, local_sem, sending):
            def wait(n):
                copy = remote(pieces(n), pieces(n), sem, sem, partner)
                if sending:
                    copy.wait_send()
                else:
                    copy.wait_recv()

            @pl.when(jnp.logical_not(at_home))
            def _():
                wait(count)

            @pl.when(at_home)
            def _():
                wait(count - 1)
                if not sending:
                    pltpu.make_async_copy(pieces(1), pieces(1), local_sem).wait()

        def token_pieces(kind):
            def pieces(n):
                return (TOK.at[pl.ds(0, n), 0], MG.at[pl.ds(0, n), 0], MR.at[pl.ds(0, n)])[kind]

            return pieces

        def send_kind(kind, sequences=range(n_seq)):
            for s in sequences:
                chip = c * n_seq + s
                for core in (0, 1):
                    here = jnp.logical_and(chip == z, c == core)
                    source = (r["tokens"].at[pl.ds(2 * core, 2)], MGS.at[core], MRS)[kind]
                    target = (TOK.at[z, core], MG.at[z, core], MR.at[z])[kind]
                    sems = (r["tok_send"].at[kind], r["tok_recv"].at[kind])
                    move(here, source, target, *sems, local_sems.at[kind], (chip, p * 2 + core))

        def take_kind(kind):
            wait_pieces(token_pieces(kind), n_blk, r["tok_recv"].at[kind], local_sems.at[kind], False)

        if gather:
            weight_refs = (WA, WI, WD)
            ag_recv = {}
            ag_send = {}
            for kind in (0, 1, 2):
                ref = weight_refs[kind]
                likes = (ref.at[:, 0:2, 0], ref.at[0], ref.at[0, 0:2])
                ag_send[kind] = [links.send_sem(like) for like in likes]
                ag_send[kind].append(links.send_sem_if(in_middle, likes[0]))
            ag_send["small"] = [links.send_sem(like) for like in (SP.at[0:2, 0], SP.at[:, 0:2], SP.at[0:2, 0:2])]
            ag_send["small"].append(links.send_sem_if(in_middle, SP.at[0:2, 0]))

            def rows_at(name, z_at, p_at):
                if name == "small":
                    return SP.at[z_at, p_at]
                return weight_refs[name[0]].at[name[1], z_at, p_at]

            def ag_push(name, stage, z_at, p_at, device):
                ref = rows_at(name, z_at, p_at)
                send_sem = ag_send[name if name == "small" else name[0]][stage]
                links.push(ref, ref, send_sem, ag_recv[name][stage % 3], device)

            every, z_low, z_high = slice(0, 4), slice(0, 2), slice(2, 4)

            def ag_z(name):
                ag_recv[name] = [links.recv_sem() for _ in range(3)]
                ag_push(name, 0, z, p, z_far)
                ag_push(name, 0, z, p, z_next)

            def ag_xy(name):
                links.arrived(rows_at(name, 0, slice(0, 3)), ag_recv[name][0])

                @pl.when(in_middle)
                def _():
                    ag_push(name, 3, far_pair, p, z_next)

                ag_push(name, 1, every, p, x_peer)
                ag_push(name, 1, every, p, y_peer)

            def ag_pass(name):
                links.arrived(rows_at(name, every, z_low), ag_recv[name][1])
                ag_push(name, 2, z_low, p ^ 1, y_peer)
                ag_push(name, 2, z_high, p ^ 2, x_peer)

            def ag_ready(name):
                links.arrived(rows_at(name, z_low, z_low), ag_recv[name][2])

            def merge_rows(kind, l):
                own = own_rows[kind][l]
                other = r["R0"][kind].astype(F32)[8 * l : 8 * l + 8]
                merged = jnp.concatenate([jnp.where(c == 0, own, other), jnp.where(c == 0, other, own)], axis=0)
                weight_refs[kind][l, z, p] = merged.astype(BF16)

        if gather:
            links.arrived(r["R0"], rows_in)
            merge_rows(0, 0)
            ag_z((0, 0))
            links.arrived(SP.at[0, 0, 0], small_in)
            ag_z("small")
            merge_rows(1, 0)
            ag_z((1, 0))
            ag_z((2, 0))
        send_kind(0)
        if gather:
            merge_rows(0, 1)
            merge_rows(1, 1)
            ag_z((0, 1))
            ag_z((1, 1))
            ag_z((2, 1))
            ag_xy((0, 0))
            ag_xy("small")
            ag_xy((1, 0))
            ag_xy((2, 0))
            ag_pass((0, 0))
            ag_pass("small")
            ag_pass((1, 0))
            ag_pass((2, 0))

        take_kind(0)
        tokens_in = links.recv_sem()
        links.push(TOK.at[:, c], TOK.at[:, c], links.send_sem(TOK.at[:, 0]), tokens_in, partner)
        links.arrived(PGV.at[0], place_in)
        to_scalars = pltpu.make_async_copy(PGV, PGS, local_sems.at[3])
        to_scalars.start()
        to_scalars.wait()
        links.arrived(TOK.at[:, 0], tokens_in)
        X, XL = r["X"], r["XL"]
        for b in range(NB):
            at = jnp.int32(0)
            for j in range(n_slots):
                at = jnp.where(PGS[group, 0, j] == seq * NB + b, j, at)
            block = TOK[lax.div(at, 4), lax.rem(lax.div(at, 2), 2), lax.rem(at, 2)]
            X[b * BS : (b + 1) * BS] = block.astype(F32)
            XL[0, b * BS : (b + 1) * BS] = block

        send_kind(1)
        send_kind(2)

        PV, LG = r["PV"], r["LG"]
        if gather:
            ag_ready("small")
            lane = lanes((1, 128))
            for l in range(LAYERS):
                for first_row, count, width, kind_row in ((0, 20, widths[0], 0), (20, 4, widths[1], 2)):
                    tiles = [jnp.zeros((1, 128), F32)] * count
                    for device in range(n_blk * n_wa):
                        t, offset = divmod(device * width, 128)
                        dz, dw = divmod(device, n_wa)
                        piece = SP[dz, dw // 2, dw % 2, kind_row + l : kind_row + l + 1, :]
                        if offset:
                            piece = turn(piece, offset)
                        if offset + width <= 128:
                            tiles[t] = tiles[t] + piece
                        else:
                            tiles[t] = tiles[t] + jnp.where(lane >= offset, piece, 0.0)
                            tiles[t + 1] = tiles[t + 1] + jnp.where(lane < offset, piece, 0.0)
                    for t in range(count):
                        PV[l, first_row + t : first_row + t + 1, :] = tiles[t]
                for h in range(H):
                    for i in range(NB):
                        LG[l, h, i : i + 1, :] = SP[h, i // 2, i % 2, 4 + l : 5 + l, :]

        def wide(l, row):
            return jnp.concatenate([PV[l, row : row + 1, :], PV[l, row + 1 : row + 2, :]], axis=1)

        def mine(l, row):
            return jnp.where(c == 0, PV[l, row : row + 1, :], PV[l, row + 1 : row + 2, :])

        BIAS = r["BIAS"]
        spread = lax.broadcasted_iota(jnp.int32, (16, SEQ), 1) // BS
        spread = (spread == lax.broadcasted_iota(jnp.int32, (16, SEQ), 0)).astype(F32).astype(BF16)

        def over_rows(table):
            table = jnp.concatenate([table, jnp.zeros_like(table)], axis=0).astype(BF16)
            return tn(table, spread)[0:NB]

        for h in (0, 1):
            allowed = over_rows(r["block_mask"][2 * c + h].astype(F32)) > 0.5
            for l in range(LAYERS):
                logit = over_rows(LG[l, 2 * c + h])
                log_sig = jnp.minimum(logit, 0.0) - jnp.log1p(jnp.exp(-jnp.abs(logit)))
                BIAS[l, h] = jnp.where(allowed, log_sig, NEG)

        PSEND, PRECV = r["PSEND"], r["PRECV"]
        exchange_out = links.send_sem(PSEND)
        most = max(CHUNKS, FWD_CHUNKS)
        exchange_in = [links.recv_sem() for _ in range(2 * most)]

        def part_of(step, chunk):
            size = FWD if step < 2 * LAYERS else HALF
            return pl.ds(chunk * size, size)

        def give(step, chunk, value):
            part = part_of(step, chunk)
            PSEND[step, part] = value.astype(BF16)
            sem = exchange_in[most * (step % 2) + chunk]
            links.push(PSEND.at[step, part], PRECV.at[step, part], exchange_out, sem, partner)

        def take(step, chunk):
            links.arrived(PRECV.at[step, part_of(step, chunk)], exchange_in[most * (step % 2) + chunk])

        def of_head(value, h):
            keep = (lanes(value.shape) // HD) == h
            return jnp.where(keep, value, jnp.zeros_like(value))

        def fwd_rows(chunk):
            return slice(chunk * FWD, (chunk + 1) * FWD)

        def rows_of(chunk):
            return slice(chunk * HALF, (chunk + 1) * HALF)

        YB, SND, RET = ((r[name + "0"], r[name + "1"]) for name in ("YB", "SND", "RET"))

        def send_back(which):
            for dest in range(n_blk):
                for j in range(2):
                    position = lax.rem(PGS[group, 0, dest * BLK_DEV + 2 * c + j], NB)
                    SND[which][dest, j] = YB[which][position]
                here = jnp.logical_and(dest == z, c == group)
                sems = (r["ret_send"].at[which], r["ret_recv"].at[which])
                target = RET[which].at[seq, c]
                move(here, SND[which].at[dest], target, *sems, local_sems.at[4 + which], (dest, p * 2 + group))

        def return_pieces(which):
            return lambda n: SND[which].at[pl.ds(0, n)]

        def take_back(which, target_ref):
            wait_pieces(return_pieces(which), 2 * n_seq, r["ret_recv"].at[which], local_sems.at[4 + which], False)
            for j in range(BLK_DEV):
                from_seq = lax.div(place_smem[0, z * BLK_DEV + j], NB)
                target_ref[j] = RET[which][from_seq, j // 2, j % 2].astype(F32)

        QKV, KT, VT, PR, AT, AN, AX = (r[n] for n in ("QKV", "KT", "VT", "PR", "AT", "AN", "AX"))
        ST, DS, PO, FS, G, GP, Y1B = (r[n] for n in ("ST", "DS", "PO", "FS", "G", "GP", "Y1B"))
        U1, R1, U2, R2 = (r[n] for n in ("U1", "R1", "U2", "R2"))
        WO = r["WO"]
        attended_out, attended_in = links.send_sem(AX), links.recv_sem()
        if gather:
            wo_out = links.send_sem(r["WOX"])

        def weight(kind, l):
            if gather:
                ref = weight_refs[kind]
                return ref[l].reshape(ref.shape[1] * ref.shape[2] * ref.shape[3], ref.shape[4])
            return (r["WA"], r["WI"], r["WD"])[kind][l]

        def weight_qkv(l):
            if gather:
                return WA[l, :, :, :, 0:384].reshape(D, 384)
            return r["WA"][l, :, 0:384]

        for l in range(LAYERS):
            step = 2 * l
            if gather:
                ag_ready((0, l))
                part = n_blk // 2
                wo_in = links.recv_sem()
                theirs = WA.at[l, pl.ds((1 - c) * part, part), :, :, pl.ds(384, 128)]
                links.push(theirs, r["WOX"].at[l], wo_out, wo_in, partner)
                WO[l, :, my_cols] = WA[l, pl.ds(c * part, part), :, :, 384:512].reshape(128, 128)
            bias = jnp.concatenate([mine(l, ROW_BQ), jnp.zeros((1, 128), F32), mine(l, ROW_BV)], axis=1)
            scale = jnp.where(lanes((1, 384)) < 128, 0.125, 1.0)
            for chunk in range(FWD_CHUNKS):
                rows = fwd_rows(chunk)
                QKV[l, rows] = ((nn(XL[l, rows], weight_qkv(l)) + bias) * scale).astype(BF16)
            keys = QKV[l, :, 128:256]
            VT[...] = QKV[l, :, 256:384].astype(F32).T.astype(BF16)
            if gather:
                if l + 1 < LAYERS:
                    ag_xy((0, l + 1))
                links.arrived(r["WOX"].at[l], wo_in)
                WO[l, :, other_cols] = r["WOX"][l].reshape(128, 128)
            for chunk in range(FWD_CHUNKS):
                rows = fwd_rows(chunk)
                for h in (0, 1):
                    queries = of_head(QKV[l, rows, 0:128], h)
                    ST[:, 0:FWD] = nt(keys, queries)
                    top = jnp.full((8, FWD), NEG, F32)
                    for kb in range(NB):
                        score = ST[kb * BS : (kb + 1) * BS, 0:FWD] + BIAS[l, h, kb : kb + 1, rows]
                        top = jnp.maximum(top, jnp.max(score.reshape(8, 8, FWD), axis=0))
                    top = jnp.max(top, axis=0, keepdims=True)
                    total = jnp.zeros((8, FWD), F32)
                    for kb in range(NB):
                        score = ST[kb * BS : (kb + 1) * BS, 0:FWD] + BIAS[l, h, kb : kb + 1, rows]
                        weight_of = jnp.exp(score - top)
                        ST[kb * BS : (kb + 1) * BS, 0:FWD] = weight_of
                        total = total + fold(weight_of)
                    inverse = 1.0 / column_sum(total)
                    for kb in range(NB):
                        PR[l, h, kb * BS : (kb + 1) * BS, rows] = (ST[kb * BS : (kb + 1) * BS, 0:FWD] * inverse).astype(BF16)
                    AT[l, h * HD : (h + 1) * HD, rows] = nn(VT[h * HD : (h + 1) * HD], PR[l, h, :, rows])
                AN[l, rows] = AT[l, :, rows].T.astype(BF16)
                branch = nn(AN[l, rows], WO[l])
                give(step, chunk, branch)
                PO[rows] = X[rows] + branch + wide(l, ROW_BO)
                part = pl.ds(chunk * FWD, FWD)
                links.push(AN.at[l, part], AX.at[l, part], attended_out, attended_in, partner)
            KT[l] = keys.astype(F32).T.astype(BF16)
            if l == LAYERS - 1:
                take_kind(1)
                take_kind(2)
                grads_in = links.recv_sem()
                links.push(MG.at[:, c], MG.at[:, c], links.send_sem(MG.at[:, 0]), grads_in, partner)
            if gather:
                if l + 1 < LAYERS:
                    ag_xy((1, l + 1))
                    ag_xy((2, l + 1))
                ag_ready((1, l))
                ag_ready((2, l))
            for chunk in range(FWD_CHUNKS):
                rows = fwd_rows(chunk)
                take(step, chunk)
                gain, shift = wide(l, ROW_G1), wide(l, ROW_S1)
                for t in range(0, FWD, BS):
                    tile = slice(chunk * FWD + t, chunk * FWD + t + BS)
                    hidden = PO[tile] + PRECV[step, tile].astype(F32)
                    normed, unit, rstd = layer_norm(hidden, gain, shift)
                    U1[l, tile] = unit
                    R1[l, tile] = rstd
                    X[tile] = normed
                    Y1B[l, tile] = normed.astype(BF16)
                FS[0:FWD] = nn(Y1B[l, rows], weight(1, l))
                inner_bias = []
                for t in range(4):
                    row = ROW_BI + 2 * t
                    inner_bias.append(pick_groups(PV[l, row : row + 1, :], PV[l, row + 1 : row + 2, :], c))
                inner_bias = jnp.concatenate(inner_bias, axis=1)
                for t in range(0, FWD, 32):
                    tile = slice(chunk * FWD + t, chunk * FWD + t + 32)
                    inner = FS[t : t + 32] + inner_bias
                    below = 0.5 + 0.5 * lax.erf(inner * 0.7071067811865476)
                    G[l, tile] = (inner * below).astype(BF16)
                    slope = below + inner * (jnp.exp(inner * inner * -0.5) * 0.3989422804014327)
                    GP[l, tile] = slope.astype(BF16)
                branch = nn(G[l, rows], weight(2, l))
                give(step + 1, chunk, branch)
                PO[rows] = X[rows] + branch + wide(l, ROW_BD)
                if gather and l + 1 < LAYERS and chunk == 0:
                    ag_pass((0, l + 1))
            if gather and l + 1 < LAYERS:
                ag_pass((1, l + 1))
                ag_pass((2, l + 1))
            for chunk in range(FWD_CHUNKS):
                take(step + 1, chunk)
                gain, shift = wide(l, ROW_G2), wide(l, ROW_S2)
                for t in range(0, FWD, BS):
                    tile = slice(chunk * FWD + t, chunk * FWD + t + BS)
                    hidden = PO[tile] + PRECV[step + 1, tile].astype(F32)
                    normed, unit, rstd = layer_norm(hidden, gain, shift)
                    U2[l, tile] = unit
                    R2[l, tile] = rstd
                    X[tile] = normed
                    if l + 1 < LAYERS:
                        XL[l + 1, tile] = normed.astype(BF16)
                    else:
                        YB[0][(chunk * FWD + t) // BS] = normed.astype(BF16)
        send_back(0)

        DY, DD, DF, DH, DO, DA, DAT, DQKV = (r[n] for n in ("DY", "DD", "DF", "DH", "DO", "DA", "DAT", "DQKV"))
        LR, SGL = r["LR"], r["SGL"]
        links.arrived(MG.at[:, 0], grads_in)
        wanted = []
        lane = lanes((1, 128))
        for t in range(n_blk // 2):
            wanted.append(jnp.where(lane < 64, MR[2 * t, 0:1, :], MR[2 * t + 1, 0:1, :]))
        wanted = jnp.concatenate(wanted, axis=1) - seq * SEQ
        listed = MG[...].reshape(n_blk * 64, D)
        for chunk in range(CHUNKS):
            row_ids = lax.broadcasted_iota(jnp.int32, (HALF, n_blk * 64), 0) + chunk * HALF
            DY[rows_of(chunk)] = nn((row_ids == wanted).astype(F32).astype(BF16), listed)

        rs_recv = {}
        if gather:
            rs_out = {kind: (links.send_sem(r["RP_" + kind]), links.send_sem(r["RZ_" + kind])) for kind in RS_KINDS}

        def rs_start(kind, l):
            if not gather:
                return
            rs_recv[kind, l] = [links.recv_sem() for _ in range(3)]
            grad, parts, sem = r["G_" + kind], r["RP_" + kind], rs_recv[kind, l][0]
            out = rs_out[kind][0]
            if (kind, l) in RS_STRAIGHT:
                devices = (x_peer, y_peer, (z, w ^ 6))
                for m in range(3):
                    links.push(grad.at[l, z_low, p ^ (m + 1)], parts.at[l, 0, m], out, sem, devices[m])
                    links.push(grad.at[l, z_high, p ^ (m + 1)], parts.at[l, 1, m], out, sem, devices[m])
                return
            links.push(grad.at[l, z_low, p ^ 3], parts.at[l, 0, 1], out, sem, x_peer)
            links.push(grad.at[l, z_high, p ^ 3], parts.at[l, 1, 1], out, sem, y_peer)
            links.push(grad.at[l, z_low, p ^ 1], parts.at[l, 0, 0], out, sem, x_peer)
            links.push(grad.at[l, z_high, p ^ 2], parts.at[l, 1, 0], out, sem, y_peer)

        def rs_pass(kind, l):
            if not gather or (kind, l) in RS_STRAIGHT:
                return
            grad, parts, sem = r["G_" + kind], r["RP_" + kind], rs_recv[kind, l][1]
            links.arrived(parts.at[l, :, 0:2], rs_recv[kind, l][0])
            parts[l, 0, 1] = (grad[l, z_low, p ^ 2].astype(F32) + parts[l, 0, 1].astype(F32)).astype(BF16)
            links.push(parts.at[l, 0, 1], parts.at[l, 1, 2], rs_out[kind][0], sem, y_peer)
            parts[l, 1, 1] = (grad[l, z_high, p ^ 1].astype(F32) + parts[l, 1, 1].astype(F32)).astype(BF16)
            links.push(parts.at[l, 1, 1], parts.at[l, 0, 2], rs_out[kind][0], sem, x_peer)

        def rs_z(kind, l):
            if not gather:
                return
            grad, parts, total = r["G_" + kind], r["RP_" + kind], r["SZ_" + kind]
            if (kind, l) in RS_STRAIGHT:
                links.arrived(parts.at[l], rs_recv[kind, l][0])
            else:
                links.arrived(parts.at[l, :, 2], rs_recv[kind, l][1])
            for at, half in enumerate((z_low, z_high)):
                value = grad[l, half, p].astype(F32)
                if (kind, l) in RS_STRAIGHT:
                    for m in range(3):
                        value = value + parts[l, at, m].astype(F32)
                else:
                    value = value + parts[l, at, 0].astype(F32) + parts[l, 1 - at, 2].astype(F32)
                total[l, half] = value.astype(BF16)
            for m in range(1, n_blk):
                links.push(total.at[l, z ^ m], r["RZ_" + kind].at[l, m - 1], rs_out[kind][1], rs_recv[kind, l][2], (z ^ m, w))

        def rs_end(kind, l):
            total = r["SZ_" + kind][l, z].astype(F32)
            links.arrived(r["RZ_" + kind].at[l], rs_recv[kind, l][2])
            for m in range(1, n_blk):
                total = total + r["RZ_" + kind][l, m - 1].astype(F32)
            return total

        sg_recv = {}
        if gather:
            SLO, SLP, SLS, SLZ = (r[name] for name in ("SLO", "SLP", "SLS", "SLZ"))
            sg_out = (links.send_sem(SLP), links.send_sem(SLZ))

        def small_start(l):
            if not gather:
                return
            for owner in range(n_blk):
                parts = [SGL[l, at : at + 1, :] for at in SLAB_ROWS[owner]]
                parts += [jnp.zeros((1, 128), F32)] * (5 - len(parts))
                parts += [SGL[l, SLAB_GAINS[owner] : SLAB_GAINS[owner] + 1, :], jnp.zeros((2, 128), F32)]
                at = SG_LG + 8 * (owner % 2)
                slab = jnp.concatenate(parts + [SGL[l, at : at + 8, :]], axis=0)
                SLO[l, owner] = slab.astype(BF16)
            sg_recv[l] = [links.recv_sem() for _ in range(2)]
            for m in range(1, n_plane):
                links.push(SLO.at[l], SLP.at[l, m - 1], sg_out[0], sg_recv[l][0], (z, w ^ (2 * m)))

        def small_z(l):
            if not gather:
                return
            links.arrived(SLP.at[l], sg_recv[l][0])
            total = SLO[l].astype(F32)
            for m in range(1, n_plane):
                total = total + SLP[l, m - 1].astype(F32)
            SLS[l] = total.astype(BF16)
            for m in range(1, n_blk):
                links.push(SLS.at[l, z ^ m], SLZ.at[l, m - 1], sg_out[1], sg_recv[l][1], (z ^ m, w))

        def small_end(l):
            links.arrived(SLZ.at[l], sg_recv[l][1])
            total = SLS[l, z].astype(F32)
            for m in range(1, n_blk):
                total = total + SLZ[l, m - 1].astype(F32)
            return total

        def store_grad(kind, l, value):
            if gather:
                shape = r["G_" + kind].shape
                r["G_" + kind][l] = value.astype(BF16).reshape(shape[1:])
            else:
                r["G_" + kind][l] = value

        def two_rows(l, row, value):
            SGL[l, row : row + 1, :] = value[:, 0:128]
            SGL[l, row + 1 : row + 2, :] = value[:, 128:256]

        SGL[...] = jnp.zeros_like(SGL)
        for l in reversed(range(LAYERS)):
            step = 4 + 2 * (LAYERS - 1 - l)
            gain = wide(l, ROW_G2)
            sums = [jnp.zeros((8, D), F32) for _ in range(3)]
            inner_sum = jnp.zeros((8, MY_FF), F32)
            for chunk in range(CHUNKS):
                rows = rows_of(chunk)
                for t in range(0, HALF, BS):
                    tile = slice(chunk * HALF + t, chunk * HALF + t + BS)
                    grad, unit = DY[tile], U2[l, tile]
                    if l < LAYERS - 1:
                        if t == 0:
                            take(step - 1, chunk)
                        grad = grad + PRECV[step - 1, tile].astype(F32)
                    d_hidden = layer_norm_back(grad, unit, R2[l, tile], gain)
                    low = d_hidden.astype(BF16)
                    DH[tile] = d_hidden
                    DD[tile] = low
                    sums[0] = sums[0] + fold(grad * unit)
                    sums[1] = sums[1] + fold(grad)
                    sums[2] = sums[2] + fold(low.astype(F32))
                FS[...] = nt(DD[rows], weight(2, l))
                for t in range(0, HALF, 32):
                    tile = slice(chunk * HALF + t, chunk * HALF + t + 32)
                    d_inner = (FS[t : t + 32] * GP[l, tile].astype(F32)).astype(BF16)
                    DF[tile] = d_inner
                    inner_sum = inner_sum + fold(d_inner.astype(F32))
                branch = nt(DF[rows], weight(1, l))
                give(step, chunk, branch)
                DH[rows] = DH[rows] + branch
            two_rows(l, SG_G2, column_sum(sums[0]))
            two_rows(l, SG_S2, column_sum(sums[1]))
            two_rows(l, SG_BD, column_sum(sums[2]))
            inner_sum = column_sum(inner_sum)
            for t in range(4):
                SGL[l, SG_BI + t : SG_BI + t + 1, :] = inner_sum[:, 128 * t : 128 * t + 128]
            store_grad("d", l, tn(G[l], DD[...]))
            rs_start("d", l)
            store_grad("i", l, tn(Y1B[l], DF[...]))
            rs_start("i", l)
            if l < LAYERS - 1:
                rs_pass("q", l + 1)
                rs_z("d", l + 1)
            gain = wide(l, ROW_G1)
            sums = [jnp.zeros((8, D), F32) for _ in range(3)]
            for chunk in range(CHUNKS):
                rows = rows_of(chunk)
                take(step, chunk)
                for t in range(0, HALF, BS):
                    tile = slice(chunk * HALF + t, chunk * HALF + t + BS)
                    grad = DH[tile] + PRECV[step, tile].astype(F32)
                    unit = U1[l, tile]
                    d_hidden = layer_norm_back(grad, unit, R1[l, tile], gain)
                    low = d_hidden.astype(BF16)
                    DH[tile] = d_hidden
                    DO[tile] = low
                    sums[0] = sums[0] + fold(grad * unit)
                    sums[1] = sums[1] + fold(grad)
                    sums[2] = sums[2] + fold(low.astype(F32))
                DA[rows] = nt(DO[rows], WO[l]).astype(BF16)
                DAT[:, rows] = nt(WO[l], DO[rows]).astype(BF16).astype(F32)
            two_rows(l, SG_G1, column_sum(sums[0]))
            two_rows(l, SG_S1, column_sum(sums[1]))
            two_rows(l, SG_BO, column_sum(sums[2]))
            if l == LAYERS - 1:
                links.arrived(AX, attended_in)
            own_part = tn(AN[l], DO[:, my_cols])
            other_part = tn(AX[l], DO[:, my_cols])
            if gather:
                part = n_blk // 2
                shape = (part, n_plane, 16, 128)
                r["G_o"][l, pl.ds(c * part, part)] = own_part.astype(BF16).reshape(shape)
                r["G_o"][l, pl.ds((1 - c) * part, part)] = other_part.astype(BF16).reshape(shape)
            else:
                r["G_o"][l, c] = own_part
                r["G_o"][l, 1 - c] = other_part
            rs_start("o", l)
            if l < LAYERS - 1:
                rs_z("i", l + 1)
                small_z(l + 1)
            keys, values = QKV[l, :, 128:256], QKV[l, :, 256:384]
            for chunk in range(CHUNKS):
                rows = rows_of(chunk)
                d_query = []
                for h in (0, 1):
                    head = slice(h * HD, (h + 1) * HD)
                    ST[...] = nt(values, of_head(DA[rows], h))
                    inner = column_sum(DAT[head, rows] * AT[l, head, rows])
                    for kb in range(NB):
                        block = slice(kb * BS, (kb + 1) * BS)
                        d_score = PR[l, h, block, rows].astype(F32) * (ST[block] - inner)
                        DS[h, block, rows] = d_score.astype(BF16)
                        LR[h, kb : kb + 1, rows] = column_sum(fold(d_score))
                    d_query.append(nn(KT[l, head], DS[h, :, rows]))
                d_query = jnp.concatenate(d_query, axis=0) * 0.125
                DQKV[rows, 0:128] = d_query.T.astype(BF16)
                if l == LAYERS - 1:
                    if chunk == CHUNKS - 1:
                        rs_pass("d", l)
                elif chunk == -1:
                    rs_z("o", l + 1)
                    rs_pass("d", l)
                elif chunk == CHUNKS - 1:
                    rs_z("o", l + 1)
                    rs_pass("d", l)
                    rs_z("q", l + 1)
                    rs_pass("i", l)
            d_keys = jnp.zeros((SEQ, 128), F32)
            d_values = jnp.zeros((SEQ, 128), F32)
            for h in (0, 1):
                d_keys = d_keys + nn(DS[h], of_head(QKV[l, :, 0:128], h))
                d_values = d_values + nn(PR[l, h], of_head(DA[...], h))
            DQKV[:, 128:256] = d_keys.astype(BF16)
            DQKV[:, 256:384] = d_values.astype(BF16)
            by_block = lax.broadcasted_iota(jnp.int32, (128, SEQ), 1) // BS
            by_block = (by_block == lax.broadcasted_iota(jnp.int32, (128, SEQ), 0)).astype(F32)
            for h in (0, 1):
                table = lax.dot_general(
                    LR[h], by_block, (((1,), (1,)), ((), ())), preferred_element_type=F32, precision=HIGHEST
                )
                SGL[l, SG_LG + 8 * h : SG_LG + 8 * h + 8, :] = table
            for chunk in range(CHUNKS):
                rows = rows_of(chunk)
                branch = nt(DQKV[rows], weight_qkv(l))
                give(step + 1, chunk, branch)
                DY[rows] = DH[rows] + branch
            store_grad("q", l, tn(XL[l], DQKV[...]))
            rs_start("q", l)
            SGL[l, SG_BQ : SG_BQ + 1, :] = column_sum(fold(DQKV[:, 0:128].astype(F32)))
            SGL[l, SG_BV : SG_BV + 1, :] = column_sum(fold(DQKV[:, 256:384].astype(F32)))
            small_start(l)
            if l == LAYERS - 1:
                rs_pass("i", l)
            rs_pass("o", l)
        for chunk in range(CHUNKS):
            take(step + 1, chunk)
            for t in range(0, HALF, BS):
                tile = slice(chunk * HALF + t, chunk * HALF + t + BS)
                grad = DY[tile] + PRECV[step + 1, tile].astype(F32)
                YB[1][(chunk * HALF + t) // BS] = grad.astype(BF16)
        rs_z("d", 0)
        rs_z("i", 0)
        send_back(1)
        SGF = r["SGF"]
        if gather:
            rs_pass("q", 0)
            rs_z("o", 0)
            small_z(0)
            FX, RX = r["FX"], r["RX"]
            kept = {}

            def finish(kind, l, at):
                total = rs_end(kind, l)
                width = total.shape[1]
                kept[kind, l] = jnp.where(c == 0, total[0:8], total[8:16])
                FX[l, :, at : at + width] = jnp.where(c == 0, total[8:16], total[0:8])

            for l in reversed(range(LAYERS)):
                r["gdown"][l] = rs_end("d", l)
                finish("i", l, 512)
                if l > 0:
                    finish("o", l, 384)
                    finish("q", l, 0)
                    SGF[c, l] = small_end(l)
                if l == LAYERS - 1:
                    rs_z("q", 0)
        take_back(0, r["out"])
        if gather:
            finish("o", 0, 384)
            SGF[c, 0] = small_end(0)
            sgf_in = links.recv_sem()
            links.push(SGF.at[c], SGF.at[c], links.send_sem(SGF.at[0]), sgf_in, partner)
            finish("q", 0, 0)
            fx_in = links.recv_sem()
            links.push(FX, RX, links.send_sem(FX), fx_in, partner)
            links.arrived(SGF.at[0], sgf_in)
        else:
            SGF[c] = SGL[...]
            SGF[1 - c] = jnp.zeros(SGL.shape, F32)
        for l in range(LAYERS):

            def row(core, at):
                return SGF[core, l, at : at + 1, :]

            if gather:
                woven = [weave_groups(row(0, at), row(1, at)) for at in (0, 1, 2, 3)]
                tiles = (
                    (row(0, 0), row(1, 0), row(0, 1), row(1, 1), row(0, 2)),
                    (row(0, 0), row(0, 1), row(0, 2), *woven[3]),
                    (*woven[0], *woven[1], woven[2][0]),
                    (woven[0][1], row(0, 1), row(0, 2), row(0, 3), row(0, 4)),
                )
                for t in range(5):
                    choice = tiles[0][t]
                    for owner in range(1, n_blk):
                        choice = jnp.where(z == owner, tiles[owner][t], choice)
                    r["BT"][l, t : t + 1, :] = choice
                lane = lanes((1, 128))
                start = w * widths[0]
                tile, offset = lax.div(start, 128), lax.rem(start, 128)
                shift = lax.rem(128 - offset, 128)
                first = pltpu.roll(r["BT"][l, pl.ds(tile, 1), :], shift, 1)
                second = pltpu.roll(r["BT"][l, pl.ds(tile + 1, 1), :], shift, 1)
                r["gbias"][l : l + 1, :] = jnp.where(lane < 128 - offset, first, second)[:, 0 : widths[0]]
                gain = pltpu.roll(row(0, 5), lax.rem(128 - w * widths[1], 128), 1)
                r["ggain"][l : l + 1, :] = gain[:, 0 : widths[1]]
                table = SGF[lax.div(z, 2), l, 8:16, :]
                wide_lane = lanes((8, 128))
                column = jnp.sum(jnp.where(wide_lane == w, table, 0.0), axis=1, keepdims=True)
                diagonal = wide_lane == lax.broadcasted_iota(jnp.int32, (8, 128), 0)
                values_row = column_sum(jnp.where(diagonal, column, 0.0))[:, 0:NB]
                logit = r["mask_logits"][...].astype(F32)[l : l + 1]
                r["glog"][l : l + 1, :] = values_row / (1.0 + jnp.exp(logit))
                continue

            def put(at, value):
                if at < ROW_G1:
                    r["gbias"][l : l + 1, 128 * at : 128 * at + 128] = value
                else:
                    at -= ROW_G1
                    r["ggain"][l : l + 1, 128 * at : 128 * at + 128] = value

            for core in (0, 1):
                put(ROW_BQ + core, row(core, SG_BQ))
                put(ROW_BV + core, row(core, SG_BV))
                for h in (0, 1):
                    r["glog"][l, 2 * core + h] = SGF[core, l, SG_LG + 8 * h : SG_LG + 8 * h + 8, :]
            singles = ((ROW_BO, SG_BO), (ROW_S1, SG_S1), (ROW_BD, SG_BD), (ROW_S2, SG_S2), (ROW_G1, SG_G1), (ROW_G2, SG_G2))
            for at, source in singles:
                for j in (0, 1):
                    put(at + j, row(0, source + j))
            for t in range(4):
                first, second = weave_groups(row(0, SG_BI + t), row(1, SG_BI + t))
                put(ROW_BI + 2 * t, first)
                put(ROW_BI + 2 * t + 1, second)
        if gather:
            links.arrived(RX, fx_in)
            for l in range(LAYERS):
                own = jnp.concatenate([kept[kind, l] for kind in ("q", "o", "i")], axis=1)
                other = RX[l]
                zero = jnp.where(c == 0, own, other)
                one = jnp.where(c == 0, other, own)
                for j in range(3):
                    r["gqkv"][l, :, 256 * j : 256 * j + 128] = zero[:, 128 * j : 128 * j + 128]
                    r["gqkv"][l, :, 256 * j + 128 : 256 * j + 256] = one[:, 128 * j : 128 * j + 128]
                r["gout"][l, :, 0:128] = zero[:, 384:512]
                r["gout"][l, :, 128:256] = one[:, 384:512]
                for t in range(4):
                    at = 512 + 128 * t
                    first, second = weave_groups(zero[:, at : at + 128], one[:, at : at + 128])
                    r["gin"][l, :, 256 * t : 256 * t + 128] = first
                    r["gin"][l, :, 256 * t + 128 : 256 * t + 256] = second
        take_back(1, r["gtok"])
        links.drain()
        for kind in range(3):
            wait_pieces(token_pieces(kind), 2 * n_seq, r["tok_send"].at[kind], None, True)
        for which in range(2):
            wait_pieces(return_pieces(which), n_blk, r["ret_send"].at[which], None, True)

    return kernel


def call_kernel(n_blk, n_wa, gather, named):
    vmem = pl.BlockSpec(memory_space=pltpu.VMEM)
    smem = pl.BlockSpec(memory_space=pltpu.SMEM)
    in_names = list(named)
    shapes = dict(out=(BLK_DEV, BS, D), gtok=(BLK_DEV, BS, D))
    if gather:
        sources = ("w_qkv", "w_out", "w_in", "w_down", "biases", "gains", "mask_logits")
        results = ("gqkv", "gout", "gin", "gdown", "gbias", "ggain", "glog")
        shapes.update({result: named[source].shape for result, source in zip(results, sources)})
    else:
        shapes.update(
            gbias=(LAYERS, 6 * D + FF),
            ggain=(LAYERS, 2 * D),
            glog=(LAYERS, H, NB, 128),
            G_d=(LAYERS, MY_FF, D),
            G_i=(LAYERS, D, MY_FF),
            G_o=(LAYERS, 2, 128, 128),
            G_q=(LAYERS, D, 384),
        )
    hold = pltpu.VMEM if gather else jax.ShapeDtypeStruct
    scratch = scratch_shapes(n_blk, n_wa, gather)
    kernel = make_kernel(n_blk, n_wa, gather, in_names, list(shapes), list(scratch))
    results = pl.pallas_call(
        kernel,
        out_shape=[hold(shape, F32) for shape in shapes.values()],
        in_specs=[smem if name in ("place_smem", "masked_count") else vmem for name in in_names],
        out_specs=[vmem] * len(shapes),
        scratch_shapes=list(scratch.values()),
        compiler_params=pltpu.CompilerParams(
            collective_id=0, has_side_effects=True, vmem_limit_bytes=60 * 2**20
        ),
        name="encoder",
    )(*named.values())
    if gather:
        results = pl.pallas_call(
            write_out,
            out_shape=[jax.ShapeDtypeStruct(shape, F32) for shape in shapes.values()],
            in_specs=[vmem] * len(shapes),
            out_specs=[pl.BlockSpec(memory_space=pl.ANY)] * len(shapes),
            scratch_shapes=[pltpu.SemaphoreType.DMA((len(shapes),))],
            name="write_out",
        )(*[pltpu.with_memory_space_constraint(result, pltpu.VMEM) for result in results])
    return dict(zip(shapes, results))


def write_out(*refs):
    count = (len(refs) - 1) // 2
    sems = refs[-1]
    copies = [pltpu.make_async_copy(refs[k], refs[count + k], sems.at[k]) for k in range(count)]
    for copy in copies:
        copy.start()
    for copy in copies:
        copy.wait()


def local(
    tokens,
    placement,
    block_mask,
    w_qkv,
    w_out,
    w_in,
    w_down,
    biases,
    gains,
    mask_logits,
    masked_pos,
    masked_count,
    masked_grad,
):
    n_blk, n_wa = lax.axis_size("blk"), lax.axis_size("wa")
    both = ("blk", "wa")
    core = lax.rem(lax.axis_index("wa"), 2)
    gather = w_qkv.shape[1] == 8 and n_blk == H and n_wa == NB
    named = dict(
        tokens=tokens.reshape(BLK_DEV, BS, D),
        place_smem=placement,
        place_vmem=placement,
        block_mask=block_mask,
        masked_pos=masked_pos.reshape(1, -1),
        masked_count=masked_count,
        masked_grad=masked_grad.reshape(-1, D),
    )
    if gather:
        named.update(
            w_qkv=w_qkv, w_out=w_out, w_in=w_in, w_down=w_down, biases=biases, gains=gains, mask_logits=mask_logits
        )
    else:
        shards = (w_qkv, w_out, w_in, w_down, biases, gains, mask_logits)
        whole = [lax.all_gather(shard, both, axis=1, tiled=True) for shard in shards]
        qkv = lax.dynamic_index_in_dim(whole[0].reshape(LAYERS, D, 3, 2, 128), core, 3, False)
        qkv = qkv.reshape(LAYERS, D, 384)
        inner = lax.dynamic_index_in_dim(whole[2].reshape(LAYERS, D, 16, 2, 32), core, 3, False)
        down = lax.dynamic_index_in_dim(whole[3].reshape(LAYERS, 16, 2, 32, D), core, 2, False)
        vectors = jnp.concatenate([whole[4], whole[5]], axis=1).astype(F32)
        logits = whole[6].astype(F32).reshape(LAYERS, H, NB, NB)
        named.update(
            WA=qkv,
            WO=lax.dynamic_slice_in_dim(whole[1], core * 128, 128, axis=1),
            WI=inner.reshape(LAYERS, D, MY_FF),
            WD=down.reshape(LAYERS, MY_FF, D),
            PV=vectors.reshape(LAYERS, PV_ROWS, 128),
            LG=jnp.pad(logits, ((0, 0), (0, 0), (0, 0), (0, 128 - NB))),
        )
    got = call_kernel(n_blk, n_wa, gather, named)
    if gather:
        weight_grads = (got["gqkv"], got["gout"], got["gin"], got["gdown"])
        small = (got["gbias"], got["ggain"], got["glog"])
    else:
        grad_logits = jnp.swapaxes(got["glog"][..., 0:NB], 2, 3).reshape(LAYERS, H * NB * NB)

        def one_core(part, axis):
            halves = [jnp.where(core == side, part, 0.0) for side in (0, 1)]
            return jnp.stack(halves, axis=axis)

        whole = (
            one_core(got["G_q"].reshape(LAYERS, D, 3, 128), 3).reshape(LAYERS, D, 3 * D),
            one_core(got["G_o"].reshape(LAYERS, D, 128), 2).reshape(LAYERS, D, D),
            one_core(got["G_i"].reshape(LAYERS, D, 16, 32), 3).reshape(LAYERS, D, FF),
            one_core(got["G_d"].reshape(LAYERS, 16, 32, D), 2).reshape(LAYERS, FF, D),
            got["gbias"],
            got["ggain"],
            grad_logits,
        )
        summed = [lax.psum_scatter(part, both, scatter_dimension=1, tiled=True) for part in whole]
        grad_mask = summed[6] * jax.nn.sigmoid(-mask_logits.astype(F32))
        weight_grads, small = tuple(summed[:4]), (summed[4], summed[5], grad_mask)
    return (
        got["out"].reshape(tokens.shape),
        got["gtok"].reshape(tokens.shape),
        *weight_grads,
        *small,
    )


def solution(mesh):
    placed = (
        P("wa", "blk", None, None),
        P("wa", None),
        P(),
        P(None, ("blk", "wa"), None),
        P(None, ("blk", "wa"), None),
        P(None, ("blk", "wa"), None),
        P(None, ("blk", "wa"), None),
        P(None, ("blk", "wa")),
        P(None, ("blk", "wa")),
        P(None, ("blk", "wa")),
        P("wa", "blk", None),
        P("wa", "blk"),
        P("wa", "blk", None, None),
    )
    return jax.shard_map(
        local,
        mesh=mesh,
        in_specs=placed,
        out_specs=(
            P("wa", "blk", None, None),
            P("wa", "blk", None, None),
            P(None, ("blk", "wa"), None),
            P(None, ("blk", "wa"), None),
            P(None, ("blk", "wa"), None),
            P(None, ("blk", "wa"), None),
            P(None, ("blk", "wa")),
            P(None, ("blk", "wa")),
            P(None, ("blk", "wa")),
        ),
        check_vma=False,
    )
```

```python
import functools

import jax
import jax.numpy as jnp
from jax import lax
from jax.experimental import pallas as pl
from jax.experimental.pallas import tpu as pltpu
from jax.sharding import PartitionSpec as P

D = 256
H = 4
HD = 64
FF = 1024
NB = 8
BS = 64
SEQ = 512
LAYERS = 2
BLK_DEV = 4
HALF = 512
CHUNKS = SEQ // HALF
FWD = 512
FWD_CHUNKS = SEQ // FWD
MY_FF = FF // 2
NEG = -1e30
EPS = 1e-05
MESH = pl.DeviceIdType.MESH
F32 = jnp.float32
BF16 = jnp.bfloat16
HIGHEST = lax.Precision.HIGHEST

ROW_BQ, ROW_BV, ROW_BO, ROW_S1, ROW_BI, ROW_BD, ROW_S2, ROW_G1, ROW_G2 = 0, 2, 4, 6, 8, 16, 18, 20, 22
PV_ROWS = 24
SG_BQ, SG_BV, SG_BI, SG_BO, SG_S1, SG_BD, SG_S2, SG_G1, SG_G2, SG_LG = 0, 1, 2, 6, 8, 10, 12, 14, 16, 24
SG_ROWS = 40
SLAB = 16
SLAB_ROWS = (
    (SG_BQ, SG_BV, SG_BO),
    (SG_BO + 1, SG_S1, SG_S1 + 1, SG_BI),
    (SG_BI + 1, SG_BI + 2, SG_BI + 3),
    (SG_BI + 3, SG_BD, SG_BD + 1, SG_S2, SG_S2 + 1),
)
SLAB_GAINS = (SG_G1, SG_G1 + 1, SG_G2, SG_G2 + 1)


def nn(left, right):
    return jnp.dot(left, right, preferred_element_type=F32)


def nt(left, right):
    return lax.dot_general(left, right, (((1,), (1,)), ((), ())), preferred_element_type=F32)


def tn(left, right):
    return lax.dot_general(left, right, (((0,), (0,)), ((), ())), preferred_element_type=F32)


def lanes(shape):
    return lax.broadcasted_iota(jnp.int32, shape, len(shape) - 1)


def turn(value, shift):
    return pltpu.roll(value, shift % 128, 1)


def pick_groups(first, second, core):
    if isinstance(core, int):
        if core == 1:
            first, second = turn(first, -32), turn(second, -32)
    else:
        first = jnp.where(core == 1, turn(first, -32), first)
        second = jnp.where(core == 1, turn(second, -32), second)
    group = lanes(first.shape) // 32
    return jnp.where(
        group == 0,
        first,
        jnp.where(group == 1, turn(first, -32), jnp.where(group == 2, turn(second, 64), turn(second, 32))),
    )


def weave_groups(zero, one):
    group = lanes(zero.shape) // 32
    first = jnp.where(
        group == 0, zero, jnp.where(group == 1, turn(one, 32), jnp.where(group == 2, turn(zero, 32), turn(one, 64)))
    )
    second = jnp.where(
        group == 0,
        turn(zero, -64),
        jnp.where(group == 1, turn(one, -32), jnp.where(group == 2, turn(zero, -32), one)),
    )
    return first, second


class Links:
    def __init__(self, send, recv, anyone):
        self.send, self.recv, self.anyone = send, recv, anyone
        self.send_used = self.recv_used = 0
        self.pending = {}
        self.pending_if = []

    def recv_sem(self):
        self.recv_used += 1
        return self.recv_used - 1

    def send_sem(self, bytes_like):
        self.send_used += 1
        self.pending[self.send_used - 1] = bytes_like
        return self.send_used - 1

    def send_sem_if(self, condition, bytes_like):
        self.send_used += 1
        self.pending_if.append((condition, self.send_used - 1, bytes_like))
        return self.send_used - 1

    def push(self, source, target, send_sem, recv_sem, device):
        remote(source, target, self.send.at[send_sem], self.recv.at[recv_sem], device).start()

    def arrived(self, bytes_like, recv_sem):
        remote(bytes_like, bytes_like, self.send.at[0], self.recv.at[recv_sem], self.anyone).wait_recv()

    def drain(self):
        for send_sem, bytes_like in self.pending.items():
            remote(bytes_like, bytes_like, self.send.at[send_sem], self.recv.at[0], self.anyone).wait_send()
        for condition, send_sem, bytes_like in self.pending_if:

            @pl.when(condition)
            def _():
                remote(bytes_like, bytes_like, self.send.at[send_sem], self.recv.at[0], self.anyone).wait_send()


def remote(source, target, send_sem, recv_sem, device):
    return pltpu.make_async_remote_copy(
        src_ref=source,
        dst_ref=target,
        send_sem=send_sem,
        recv_sem=recv_sem,
        device_id=device,
        device_id_type=MESH,
    )


def layer_norm(hidden, gain, shift):
    mean = jnp.sum(hidden, axis=1, keepdims=True) * (1.0 / D)
    centred = hidden - mean
    var = jnp.sum(centred * centred, axis=1, keepdims=True) * (1.0 / D)
    rstd = lax.rsqrt(var + EPS)
    unit = centred * rstd
    return unit * gain + shift, unit, rstd


def layer_norm_back(grad, unit, rstd, gain):
    scaled = grad * gain
    mean_one = jnp.sum(scaled, axis=1, keepdims=True) * (1.0 / D)
    mean_two = jnp.sum(scaled * unit, axis=1, keepdims=True) * (1.0 / D)
    return rstd * (scaled - mean_one - unit * mean_two)


def fold(value):
    rows, cols = value.shape
    return jnp.sum(value.reshape(rows // 8, 8, cols), axis=0)


def column_sum(value):
    return jnp.sum(value, axis=0, keepdims=True)


SEND_SEMS, RECV_SEMS = 46, 82


def scratch_shapes(n_blk, n_wa, gather):
    n_plane, n_seq = n_wa // 2, n_blk // 2
    vmem = pltpu.VMEM
    shapes = dict(
        TOK=vmem((n_blk, 2, 2, BS, D), BF16),
        MGS=vmem((2, 32, D), BF16),
        MRS=vmem((8, 128), jnp.int32),
        MG=vmem((n_blk, 2, 32, D), BF16),
        MR=vmem((n_blk, 8, 128), jnp.int32),
        PGV=vmem((2, 8, 128), jnp.int32),
        PGS=pltpu.SMEM((2, 8, 128), jnp.int32),
        YB0=vmem((NB, BS, D), BF16),
        YB1=vmem((NB, BS, D), BF16),
        SND0=vmem((n_blk, 2, BS, D), BF16),
        SND1=vmem((n_blk, 2, BS, D), BF16),
        RET0=vmem((n_seq, 2, 2, BS, D), BF16),
        RET1=vmem((n_seq, 2, 2, BS, D), BF16),
        PSEND=vmem((4 * LAYERS, SEQ, D), BF16),
        PRECV=vmem((4 * LAYERS, SEQ, D), BF16),
        X=vmem((SEQ, D), F32),
        XL=vmem((LAYERS, SEQ, D), BF16),
        QKV=vmem((LAYERS, SEQ, 384), BF16),
        KT=vmem((LAYERS, 128, SEQ), BF16),
        VT=vmem((128, SEQ), BF16),
        PR=vmem((LAYERS, 2, SEQ, SEQ), BF16),
        AT=vmem((LAYERS, 128, SEQ), F32),
        AN=vmem((LAYERS, SEQ, 128), BF16),
        AX=vmem((LAYERS, SEQ, 128), BF16),
        ST=vmem((SEQ, HALF), F32),
        DS=vmem((2, SEQ, SEQ), BF16),
        PO=vmem((SEQ, D), F32),
        U1=vmem((LAYERS, SEQ, D), F32),
        R1=vmem((LAYERS, SEQ, 1), F32),
        U2=vmem((LAYERS, SEQ, D), F32),
        R2=vmem((LAYERS, SEQ, 1), F32),
        Y1B=vmem((LAYERS, SEQ, D), BF16),
        FS=vmem((HALF, MY_FF), F32),
        G=vmem((LAYERS, SEQ, MY_FF), BF16),
        GP=vmem((LAYERS, SEQ, MY_FF), BF16),
        DY=vmem((SEQ, D), F32),
        DD=vmem((SEQ, D), BF16),
        DF=vmem((SEQ, MY_FF), BF16),
        DH=vmem((SEQ, D), F32),
        DO=vmem((SEQ, D), BF16),
        DA=vmem((SEQ, 128), BF16),
        DAT=vmem((128, SEQ), F32),
        DQKV=vmem((SEQ, 384), BF16),
        BIAS=vmem((LAYERS, 2, NB, SEQ), F32),
        LR=vmem((2, NB, SEQ), F32),
        SGL=vmem((LAYERS, SG_ROWS, 128), F32),
        SGF=vmem((2, LAYERS, SLAB if gather else SG_ROWS, 128), F32),
        link_send=pltpu.SemaphoreType.DMA((SEND_SEMS if gather else 8,)),
        link_recv=pltpu.SemaphoreType.DMA((RECV_SEMS if gather else 16,)),
        tok_send=pltpu.SemaphoreType.DMA((3,)),
        tok_recv=pltpu.SemaphoreType.DMA((3,)),
        ret_send=pltpu.SemaphoreType.DMA((2,)),
        ret_recv=pltpu.SemaphoreType.DMA((2,)),
        local_sems=pltpu.SemaphoreType.DMA((6,)),
    )
    if gather:
        shapes.update(
            WA=vmem((LAYERS, n_blk, n_plane, 16, 512), BF16),
            WI=vmem((LAYERS, n_blk, n_plane, 16, MY_FF), BF16),
            WD=vmem((LAYERS, n_blk, n_plane, 32, D), BF16),
            WO=vmem((LAYERS, 128, D), BF16),
            WOX=vmem((LAYERS, n_blk // 2, n_plane, 16, 128), BF16),
            PV=vmem((LAYERS, PV_ROWS, 128), F32),
            LG=vmem((LAYERS, H, NB, 128), F32),
            S0=vmem((2, 16, 512), BF16),
            R0=vmem((2, 16, 512), BF16),
            SP=vmem((n_blk, n_plane, 2, 8, 128), F32),
            FX=vmem((LAYERS, 8, 1024), F32),
            RX=vmem((LAYERS, 8, 1024), F32),
            SLO=vmem((LAYERS, n_blk, SLAB, 128), BF16),
            SLP=vmem((LAYERS, n_plane - 1, n_blk, SLAB, 128), BF16),
            SLS=vmem((LAYERS, n_blk, SLAB, 128), BF16),
            SLZ=vmem((LAYERS, n_blk - 1, SLAB, 128), BF16),
            BT=vmem((LAYERS, 8, 128), F32),
        )
        for kind, (rows, cols) in RS_KINDS.items():
            shapes["G_" + kind] = vmem((LAYERS, n_blk, n_plane, rows, cols), BF16)
            shapes["RP_" + kind] = vmem((LAYERS, 2, 3, n_blk // 2, rows, cols), BF16)
            shapes["SZ_" + kind] = vmem((LAYERS, n_blk, rows, cols), BF16)
            shapes["RZ_" + kind] = vmem((LAYERS, n_blk - 1, rows, cols), BF16)
    return shapes


RS_KINDS = {"d": (32, D), "i": (16, MY_FF), "o": (16, 128), "q": (16, 384)}


def make_kernel(n_blk, n_wa, gather, in_names, out_names, scratch_names):
    n_plane = n_wa // 2
    n_seq = n_blk // 2
    n_slots = n_blk * BLK_DEV

    def kernel(*refs):
        r = dict(zip(in_names + out_names + scratch_names, refs))
        place_smem = r["place_smem"]
        z = lax.axis_index("blk")
        w = lax.axis_index("wa")
        c = lax.rem(w, 2)
        p = lax.div(w, 2)
        group = lax.div(z, n_seq)
        seq = lax.rem(z, n_seq)
        partner = (z, p * 2 + (1 - c))
        links = Links(r["link_send"], r["link_recv"], partner)
        x_peer, y_peer = (z, w ^ 2), (z, w ^ 4)
        in_middle = jnp.logical_or(z == 1, z == 2)
        z_next, z_far = (z ^ 1, w), (2 - lax.div(z, 2), w)
        far_pair = pl.ds(2 - 2 * lax.div(z, 2), 2)
        local_sems = r["local_sems"]
        my_cols = pl.ds(pl.multiple_of(c * 128, 128), 128)
        other_cols = pl.ds(pl.multiple_of((1 - c) * 128, 128), 128)

        TOK, MGS, MRS, MG, MR = (r[name] for name in ("TOK", "MGS", "MRS", "MG", "MR"))
        PGV, PGS = r["PGV"], r["PGS"]
        PGV[c, 0:1, 0:n_slots] = r["place_vmem"][...]
        MGS[...] = r["masked_grad"][...].astype(BF16).reshape(2, 32, D)
        chosen = r["masked_pos"][...]
        slot_of = lax.shift_right_logical(chosen, 6)
        block_of = jnp.zeros_like(chosen)
        for j in range(BLK_DEV):
            block_of = jnp.where(slot_of == j, place_smem[0, z * BLK_DEV + j], block_of)
        target_row = block_of * BS + (chosen & (BS - 1))
        target_row = jnp.where(lanes(chosen.shape) < r["masked_count"][0, 0], target_row, -1)
        MRS[0:1, 0:64] = target_row
        MRS[0:1, 64:128] = target_row
        if gather:
            WA, WI, WD, SP = r["WA"], r["WI"], r["WD"], r["SP"]
            own_rows = ([], [])
            give_rows = ([], [])
            for l in range(LAYERS):
                qkv = r["w_qkv"][l].astype(F32)
                out_part = r["w_out"][l].astype(F32)
                inner = r["w_in"][l].astype(F32)
                sides = []
                for side in (0, 1):
                    at = 128 * side
                    attn = [qkv[:, 256 * j + at : 256 * j + at + 128] for j in range(3)]
                    attn = jnp.concatenate(attn + [out_part[:, at : at + 128]], axis=1)
                    feed = []
                    for t in range(4):
                        first = inner[:, 256 * t : 256 * t + 128]
                        second = inner[:, 256 * t + 128 : 256 * t + 256]
                        feed.append(pick_groups(first, second, side))
                    sides.append((attn, jnp.concatenate(feed, axis=1)))
                for kind in (0, 1):
                    own_rows[kind].append(jnp.where(c == 0, sides[0][kind], sides[1][kind]))
                    give_rows[kind].append(jnp.where(c == 0, sides[1][kind], sides[0][kind]))
                WD[l, z, p] = r["w_down"][l]
            for kind in (0, 1):
                r["S0"][kind] = jnp.concatenate(give_rows[kind], axis=0).astype(BF16)
            SP[z, p, c] = jnp.zeros((8, 128), F32)
            widths = []
            for at, name in ((0, "biases"), (2, "gains"), (4, "mask_logits")):
                part = r[name][...].astype(F32)
                widths.append(part.shape[1])
                SP[z, p, c, at : at + 2, 0 : part.shape[1]] = part

        barrier = pltpu.get_barrier_semaphore()
        greeted = 0
        for m in range(n_blk):
            for other in (0, 1):
                if m or other:
                    pl.semaphore_signal(barrier, inc=1, device_id=(z ^ m, w ^ other), device_id_type=MESH)
                    greeted += 1
        if gather:
            for m in range(1, n_plane):
                pl.semaphore_signal(barrier, inc=1, device_id=(z, w ^ (2 * m)), device_id_type=MESH)
                greeted += 1
        pl.semaphore_wait(barrier, greeted)

        place_in = links.recv_sem()
        links.push(PGV.at[c], PGV.at[c], links.send_sem(PGV.at[0]), place_in, partner)
        if gather:
            rows_in = links.recv_sem()
            links.push(r["S0"], r["R0"], links.send_sem(r["S0"]), rows_in, partner)
            small_in = links.recv_sem()
            links.push(SP.at[z, p, c], SP.at[z, p, c], links.send_sem(SP.at[0, 0, 0]), small_in, partner)

        at_home = c == group

        def move(here, source, target, send_sem, recv_sem, local_sem, device):
            @pl.when(jnp.logical_not(here))
            def _():
                remote(source, target, send_sem, recv_sem, device).start()

            @pl.when(here)
            def _():
                pltpu.make_async_copy(source, target, local_sem).start()

        def wait_pieces(pieces, count, sem, local_sem, sending):
            def wait(n):
                copy = remote(pieces(n), pieces(n), sem, sem, partner)
                if sending:
                    copy.wait_send()
                else:
                    copy.wait_recv()

            @pl.when(jnp.logical_not(at_home))
            def _():
                wait(count)

            @pl.when(at_home)
            def _():
                wait(count - 1)
                if not sending:
                    pltpu.make_async_copy(pieces(1), pieces(1), local_sem).wait()

        def token_pieces(kind):
            def pieces(n):
                return (TOK.at[pl.ds(0, n), 0], MG.at[pl.ds(0, n), 0], MR.at[pl.ds(0, n)])[kind]

            return pieces

        def send_kind(kind, sequences=range(n_seq)):
            for s in sequences:
                chip = c * n_seq + s
                for core in (0, 1):
                    here = jnp.logical_and(chip == z, c == core)
                    source = (r["tokens"].at[pl.ds(2 * core, 2)], MGS.at[core], MRS)[kind]
                    target = (TOK.at[z, core], MG.at[z, core], MR.at[z])[kind]
                    sems = (r["tok_send"].at[kind], r["tok_recv"].at[kind])
                    move(here, source, target, *sems, local_sems.at[kind], (chip, p * 2 + core))

        def take_kind(kind):
            wait_pieces(token_pieces(kind), n_blk, r["tok_recv"].at[kind], local_sems.at[kind], False)

        if gather:
            weight_refs = (WA, WI, WD)
            ag_recv = {}
            ag_send = {}
            for kind in (0, 1, 2):
                ref = weight_refs[kind]
                likes = (ref.at[:, 0:2, 0], ref.at[0], ref.at[0, 0:2])
                ag_send[kind] = [links.send_sem(like) for like in likes]
                ag_send[kind].append(links.send_sem_if(in_middle, likes[0]))
            ag_send["small"] = [links.send_sem(like) for like in (SP.at[0:2, 0], SP.at[:, 0:2], SP.at[0:2, 0:2])]
            ag_send["small"].append(links.send_sem_if(in_middle, SP.at[0:2, 0]))

            def rows_at(name, z_at, p_at):
                if name == "small":
                    return SP.at[z_at, p_at]
                return weight_refs[name[0]].at[name[1], z_at, p_at]

            def ag_push(name, stage, z_at, p_at, device):
                ref = rows_at(name, z_at, p_at)
                send_sem = ag_send[name if name == "small" else name[0]][stage]
                links.push(ref, ref, send_sem, ag_recv[name][stage % 3], device)

            every, z_low, z_high = slice(0, 4), slice(0, 2), slice(2, 4)

            def ag_z(name):
                ag_recv[name] = [links.recv_sem() for _ in range(3)]
                ag_push(name, 0, z, p, z_far)
                ag_push(name, 0, z, p, z_next)

            def ag_xy(name):
                links.arrived(rows_at(name, 0, slice(0, 3)), ag_recv[name][0])

                @pl.when(in_middle)
                def _():
                    ag_push(name, 3, far_pair, p, z_next)

                ag_push(name, 1, every, p, x_peer)
                ag_push(name, 1, every, p, y_peer)

            def ag_pass(name):
                links.arrived(rows_at(name, every, z_low), ag_recv[name][1])
                ag_push(name, 2, z_low, p ^ 1, y_peer)
                ag_push(name, 2, z_high, p ^ 2, x_peer)

            def ag_ready(name):
                links.arrived(rows_at(name, z_low, z_low), ag_recv[name][2])

            def merge_rows(kind, l):
                own = own_rows[kind][l]
                other = r["R0"][kind].astype(F32)[8 * l : 8 * l + 8]
                merged = jnp.concatenate([jnp.where(c == 0, own, other), jnp.where(c == 0, other, own)], axis=0)
                weight_refs[kind][l, z, p] = merged.astype(BF16)

        if gather:
            links.arrived(r["R0"], rows_in)
            merge_rows(0, 0)
            ag_z((0, 0))
            links.arrived(SP.at[0, 0, 0], small_in)
            ag_z("small")
            merge_rows(1, 0)
            ag_z((1, 0))
            ag_z((2, 0))
        send_kind(0)
        if gather:
            merge_rows(0, 1)
            merge_rows(1, 1)
            ag_z((0, 1))
            ag_z((1, 1))
            ag_z((2, 1))
            ag_xy((0, 0))
            ag_xy("small")
            ag_xy((1, 0))
            ag_xy((2, 0))
            ag_pass((0, 0))
            ag_pass("small")
            ag_pass((1, 0))
            ag_pass((2, 0))

        take_kind(0)
        tokens_in = links.recv_sem()
        links.push(TOK.at[:, c], TOK.at[:, c], links.send_sem(TOK.at[:, 0]), tokens_in, partner)
        links.arrived(PGV.at[0], place_in)
        to_scalars = pltpu.make_async_copy(PGV, PGS, local_sems.at[3])
        to_scalars.start()
        to_scalars.wait()
        links.arrived(TOK.at[:, 0], tokens_in)
        X, XL = r["X"], r["XL"]
        for b in range(NB):
            at = jnp.int32(0)
            for j in range(n_slots):
                at = jnp.where(PGS[group, 0, j] == seq * NB + b, j, at)
            block = TOK[lax.div(at, 4), lax.rem(lax.div(at, 2), 2), lax.rem(at, 2)]
            X[b * BS : (b + 1) * BS] = block.astype(F32)
            XL[0, b * BS : (b + 1) * BS] = block

        send_kind(1)
        send_kind(2)

        PV, LG = r["PV"], r["LG"]
        if gather:
            ag_ready("small")
            lane = lanes((1, 128))
            for l in range(LAYERS):
                for first_row, count, width, kind_row in ((0, 20, widths[0], 0), (20, 4, widths[1], 2)):
                    tiles = [jnp.zeros((1, 128), F32)] * count
                    for device in range(n_blk * n_wa):
                        t, offset = divmod(device * width, 128)
                        dz, dw = divmod(device, n_wa)
                        piece = SP[dz, dw // 2, dw % 2, kind_row + l : kind_row + l + 1, :]
                        if offset:
                            piece = turn(piece, offset)
                        if offset + width <= 128:
                            tiles[t] = tiles[t] + piece
                        else:
                            tiles[t] = tiles[t] + jnp.where(lane >= offset, piece, 0.0)
                            tiles[t + 1] = tiles[t + 1] + jnp.where(lane < offset, piece, 0.0)
                    for t in range(count):
                        PV[l, first_row + t : first_row + t + 1, :] = tiles[t]
                for h in range(H):
                    for i in range(NB):
                        LG[l, h, i : i + 1, :] = SP[h, i // 2, i % 2, 4 + l : 5 + l, :]

        def wide(l, row):
            return jnp.concatenate([PV[l, row : row + 1, :], PV[l, row + 1 : row + 2, :]], axis=1)

        def mine(l, row):
            return jnp.where(c == 0, PV[l, row : row + 1, :], PV[l, row + 1 : row + 2, :])

        BIAS = r["BIAS"]
        spread = lax.broadcasted_iota(jnp.int32, (16, SEQ), 1) // BS
        spread = (spread == lax.broadcasted_iota(jnp.int32, (16, SEQ), 0)).astype(F32).astype(BF16)

        def over_rows(table):
            table = jnp.concatenate([table, jnp.zeros_like(table)], axis=0).astype(BF16)
            return tn(table, spread)[0:NB]

        for h in (0, 1):
            allowed = over_rows(r["block_mask"][2 * c + h].astype(F32)) > 0.5
            for l in range(LAYERS):
                logit = over_rows(LG[l, 2 * c + h])
                log_sig = jnp.minimum(logit, 0.0) - jnp.log1p(jnp.exp(-jnp.abs(logit)))
                BIAS[l, h] = jnp.where(allowed, log_sig, NEG)

        PSEND, PRECV = r["PSEND"], r["PRECV"]
        exchange_out = links.send_sem(PSEND)
        most = max(CHUNKS, FWD_CHUNKS)
        exchange_in = [links.recv_sem() for _ in range(2 * most)]

        def part_of(step, chunk):
            size = FWD if step < 2 * LAYERS else HALF
            return pl.ds(chunk * size, size)

        def give(step, chunk, value):
            part = part_of(step, chunk)
            PSEND[step, part] = value.astype(BF16)
            sem = exchange_in[most * (step % 2) + chunk]
            links.push(PSEND.at[step, part], PRECV.at[step, part], exchange_out, sem, partner)

        def take(step, chunk):
            links.arrived(PRECV.at[step, part_of(step, chunk)], exchange_in[most * (step % 2) + chunk])

        def of_head(value, h):
            keep = (lanes(value.shape) // HD) == h
            return jnp.where(keep, value, jnp.zeros_like(value))

        def fwd_rows(chunk):
            return slice(chunk * FWD, (chunk + 1) * FWD)

        def rows_of(chunk):
            return slice(chunk * HALF, (chunk + 1) * HALF)

        YB, SND, RET = ((r[name + "0"], r[name + "1"]) for name in ("YB", "SND", "RET"))

        def send_back(which):
            for dest in range(n_blk):
                for j in range(2):
                    position = lax.rem(PGS[group, 0, dest * BLK_DEV + 2 * c + j], NB)
                    SND[which][dest, j] = YB[which][position]
                here = jnp.logical_and(dest == z, c == group)
                sems = (r["ret_send"].at[which], r["ret_recv"].at[which])
                target = RET[which].at[seq, c]
                move(here, SND[which].at[dest], target, *sems, local_sems.at[4 + which], (dest, p * 2 + group))

        def return_pieces(which):
            return lambda n: SND[which].at[pl.ds(0, n)]

        def take_back(which, target_ref):
            wait_pieces(return_pieces(which), 2 * n_seq, r["ret_recv"].at[which], local_sems.at[4 + which], False)
            for j in range(BLK_DEV):
                from_seq = lax.div(place_smem[0, z * BLK_DEV + j], NB)
                target_ref[j] = RET[which][from_seq, j // 2, j % 2].astype(F32)

        QKV, KT, VT, PR, AT, AN, AX = (r[n] for n in ("QKV", "KT", "VT", "PR", "AT", "AN", "AX"))
        ST, DS, PO, FS, G, GP, Y1B = (r[n] for n in ("ST", "DS", "PO", "FS", "G", "GP", "Y1B"))
        U1, R1, U2, R2 = (r[n] for n in ("U1", "R1", "U2", "R2"))
        WO = r["WO"]
        attended_out, attended_in = links.send_sem(AX), links.recv_sem()
        if gather:
            wo_out = links.send_sem(r["WOX"])

        def weight(kind, l):
            if gather:
                ref = weight_refs[kind]
                return ref[l].reshape(ref.shape[1] * ref.shape[2] * ref.shape[3], ref.shape[4])
            return (r["WA"], r["WI"], r["WD"])[kind][l]

        def weight_qkv(l):
            if gather:
                return WA[l, :, :, :, 0:384].reshape(D, 384)
            return r["WA"][l, :, 0:384]

        for l in range(LAYERS):
            step = 2 * l
            if gather:
                ag_ready((0, l))
                part = n_blk // 2
                wo_in = links.recv_sem()
                theirs = WA.at[l, pl.ds((1 - c) * part, part), :, :, pl.ds(384, 128)]
                links.push(theirs, r["WOX"].at[l], wo_out, wo_in, partner)
                WO[l, :, my_cols] = WA[l, pl.ds(c * part, part), :, :, 384:512].reshape(128, 128)
            bias = jnp.concatenate([mine(l, ROW_BQ), jnp.zeros((1, 128), F32), mine(l, ROW_BV)], axis=1)
            scale = jnp.where(lanes((1, 384)) < 128, 0.125, 1.0)
            for chunk in range(FWD_CHUNKS):
                rows = fwd_rows(chunk)
                QKV[l, rows] = ((nn(XL[l, rows], weight_qkv(l)) + bias) * scale).astype(BF16)
            keys = QKV[l, :, 128:256]
            VT[...] = QKV[l, :, 256:384].astype(F32).T.astype(BF16)
            if gather:
                if l + 1 < LAYERS:
                    ag_xy((0, l + 1))
                    ag_xy((1, l + 1))
                    ag_xy((2, l + 1))
                links.arrived(r["WOX"].at[l], wo_in)
                WO[l, :, other_cols] = r["WOX"][l].reshape(128, 128)
            for chunk in range(FWD_CHUNKS):
                rows = fwd_rows(chunk)
                for h in (0, 1):
                    queries = of_head(QKV[l, rows, 0:128], h)
                    ST[:, 0:FWD] = nt(keys, queries)
                    top = jnp.full((8, FWD), NEG, F32)
                    for kb in range(NB):
                        score = ST[kb * BS : (kb + 1) * BS, 0:FWD] + BIAS[l, h, kb : kb + 1, rows]
                        top = jnp.maximum(top, jnp.max(score.reshape(8, 8, FWD), axis=0))
                    top = jnp.max(top, axis=0, keepdims=True)
                    total = jnp.zeros((8, FWD), F32)
                    for kb in range(NB):
                        score = ST[kb * BS : (kb + 1) * BS, 0:FWD] + BIAS[l, h, kb : kb + 1, rows]
                        weight_of = jnp.exp(score - top)
                        ST[kb * BS : (kb + 1) * BS, 0:FWD] = weight_of
                        total = total + fold(weight_of)
                    inverse = 1.0 / column_sum(total)
                    for kb in range(NB):
                        PR[l, h, kb * BS : (kb + 1) * BS, rows] = (ST[kb * BS : (kb + 1) * BS, 0:FWD] * inverse).astype(BF16)
                    AT[l, h * HD : (h + 1) * HD, rows] = nn(VT[h * HD : (h + 1) * HD], PR[l, h, :, rows])
                AN[l, rows] = AT[l, :, rows].T.astype(BF16)
                branch = nn(AN[l, rows], WO[l])
                give(step, chunk, branch)
                PO[rows] = X[rows] + branch + wide(l, ROW_BO)
                part = pl.ds(chunk * FWD, FWD)
                links.push(AN.at[l, part], AX.at[l, part], attended_out, attended_in, partner)
            KT[l] = keys.astype(F32).T.astype(BF16)
            if l == LAYERS - 1:
                take_kind(1)
                take_kind(2)
                grads_in = links.recv_sem()
                links.push(MG.at[:, c], MG.at[:, c], links.send_sem(MG.at[:, 0]), grads_in, partner)
            if gather:
                if l + 1 < LAYERS:
                    ag_pass((0, l + 1))
                ag_ready((1, l))
                ag_ready((2, l))
            for chunk in range(FWD_CHUNKS):
                rows = fwd_rows(chunk)
                take(step, chunk)
                gain, shift = wide(l, ROW_G1), wide(l, ROW_S1)
                for t in range(0, FWD, BS):
                    tile = slice(chunk * FWD + t, chunk * FWD + t + BS)
                    hidden = PO[tile] + PRECV[step, tile].astype(F32)
                    normed, unit, rstd = layer_norm(hidden, gain, shift)
                    U1[l, tile] = unit
                    R1[l, tile] = rstd
                    X[tile] = normed
                    Y1B[l, tile] = normed.astype(BF16)
                FS[0:FWD] = nn(Y1B[l, rows], weight(1, l))
                inner_bias = []
                for t in range(4):
                    row = ROW_BI + 2 * t
                    inner_bias.append(pick_groups(PV[l, row : row + 1, :], PV[l, row + 1 : row + 2, :], c))
                inner_bias = jnp.concatenate(inner_bias, axis=1)
                for t in range(0, FWD, 32):
                    tile = slice(chunk * FWD + t, chunk * FWD + t + 32)
                    inner = FS[t : t + 32] + inner_bias
                    below = 0.5 + 0.5 * lax.erf(inner * 0.7071067811865476)
                    G[l, tile] = (inner * below).astype(BF16)
                    slope = below + inner * (jnp.exp(inner * inner * -0.5) * 0.3989422804014327)
                    GP[l, tile] = slope.astype(BF16)
                branch = nn(G[l, rows], weight(2, l))
                give(step + 1, chunk, branch)
                PO[rows] = X[rows] + branch + wide(l, ROW_BD)
            if gather and l + 1 < LAYERS:
                ag_pass((1, l + 1))
                ag_pass((2, l + 1))
            for chunk in range(FWD_CHUNKS):
                take(step + 1, chunk)
                gain, shift = wide(l, ROW_G2), wide(l, ROW_S2)
                for t in range(0, FWD, BS):
                    tile = slice(chunk * FWD + t, chunk * FWD + t + BS)
                    hidden = PO[tile] + PRECV[step + 1, tile].astype(F32)
                    normed, unit, rstd = layer_norm(hidden, gain, shift)
                    U2[l, tile] = unit
                    R2[l, tile] = rstd
                    X[tile] = normed
                    if l + 1 < LAYERS:
                        XL[l + 1, tile] = normed.astype(BF16)
                    else:
                        YB[0][(chunk * FWD + t) // BS] = normed.astype(BF16)
        send_back(0)

        DY, DD, DF, DH, DO, DA, DAT, DQKV = (r[n] for n in ("DY", "DD", "DF", "DH", "DO", "DA", "DAT", "DQKV"))
        LR, SGL = r["LR"], r["SGL"]
        links.arrived(MG.at[:, 0], grads_in)
        wanted = []
        lane = lanes((1, 128))
        for t in range(n_blk // 2):
            wanted.append(jnp.where(lane < 64, MR[2 * t, 0:1, :], MR[2 * t + 1, 0:1, :]))
        wanted = jnp.concatenate(wanted, axis=1) - seq * SEQ
        listed = MG[...].reshape(n_blk * 64, D)
        for chunk in range(CHUNKS):
            row_ids = lax.broadcasted_iota(jnp.int32, (HALF, n_blk * 64), 0) + chunk * HALF
            DY[rows_of(chunk)] = nn((row_ids == wanted).astype(F32).astype(BF16), listed)

        rs_recv = {}
        if gather:
            rs_out = {kind: (links.send_sem(r["RP_" + kind]), links.send_sem(r["RZ_" + kind])) for kind in RS_KINDS}

        def rs_start(kind, l):
            if not gather:
                return
            rs_recv[kind, l] = [links.recv_sem() for _ in range(2)]
            grad, parts, sem = r["G_" + kind], r["RP_" + kind], rs_recv[kind, l][0]
            out = rs_out[kind][0]
            devices = (x_peer, y_peer, (z, w ^ 6))
            for m in range(3):
                links.push(grad.at[l, z_low, p ^ (m + 1)], parts.at[l, 0, m], out, sem, devices[m])
                links.push(grad.at[l, z_high, p ^ (m + 1)], parts.at[l, 1, m], out, sem, devices[m])

        def rs_z(kind, l):
            if not gather:
                return
            grad, parts, total = r["G_" + kind], r["RP_" + kind], r["SZ_" + kind]
            links.arrived(parts.at[l], rs_recv[kind, l][0])
            for at, half in enumerate((z_low, z_high)):
                value = grad[l, half, p].astype(F32)
                for m in range(3):
                    value = value + parts[l, at, m].astype(F32)
                total[l, half] = value.astype(BF16)
            for m in range(1, n_blk):
                links.push(total.at[l, z ^ m], r["RZ_" + kind].at[l, m - 1], rs_out[kind][1], rs_recv[kind, l][1], (z ^ m, w))

        def rs_end(kind, l):
            total = r["SZ_" + kind][l, z].astype(F32)
            links.arrived(r["RZ_" + kind].at[l], rs_recv[kind, l][1])
            for m in range(1, n_blk):
                total = total + r["RZ_" + kind][l, m - 1].astype(F32)
            return total

        sg_recv = {}
        if gather:
            SLO, SLP, SLS, SLZ = (r[name] for name in ("SLO", "SLP", "SLS", "SLZ"))
            sg_out = (links.send_sem(SLP), links.send_sem(SLZ))

        def small_start(l):
            if not gather:
                return
            for owner in range(n_blk):
                parts = [SGL[l, at : at + 1, :] for at in SLAB_ROWS[owner]]
                parts += [jnp.zeros((1, 128), F32)] * (5 - len(parts))
                parts += [SGL[l, SLAB_GAINS[owner] : SLAB_GAINS[owner] + 1, :], jnp.zeros((2, 128), F32)]
                at = SG_LG + 8 * (owner % 2)
                slab = jnp.concatenate(parts + [SGL[l, at : at + 8, :]], axis=0)
                SLO[l, owner] = slab.astype(BF16)
            sg_recv[l] = [links.recv_sem() for _ in range(2)]
            for m in range(1, n_plane):
                links.push(SLO.at[l], SLP.at[l, m - 1], sg_out[0], sg_recv[l][0], (z, w ^ (2 * m)))

        def small_z(l):
            if not gather:
                return
            links.arrived(SLP.at[l], sg_recv[l][0])
            total = SLO[l].astype(F32)
            for m in range(1, n_plane):
                total = total + SLP[l, m - 1].astype(F32)
            SLS[l] = total.astype(BF16)
            for m in range(1, n_blk):
                links.push(SLS.at[l, z ^ m], SLZ.at[l, m - 1], sg_out[1], sg_recv[l][1], (z ^ m, w))

        def small_end(l):
            links.arrived(SLZ.at[l], sg_recv[l][1])
            total = SLS[l, z].astype(F32)
            for m in range(1, n_blk):
                total = total + SLZ[l, m - 1].astype(F32)
            return total

        def store_grad(kind, l, value):
            if gather:
                shape = r["G_" + kind].shape
                r["G_" + kind][l] = value.astype(BF16).reshape(shape[1:])
            else:
                r["G_" + kind][l] = value

        def two_rows(l, row, value):
            SGL[l, row : row + 1, :] = value[:, 0:128]
            SGL[l, row + 1 : row + 2, :] = value[:, 128:256]

        SGL[...] = jnp.zeros_like(SGL)
        for l in reversed(range(LAYERS)):
            step = 4 + 2 * (LAYERS - 1 - l)
            gain = wide(l, ROW_G2)
            sums = [jnp.zeros((8, D), F32) for _ in range(3)]
            inner_sum = jnp.zeros((8, MY_FF), F32)
            for chunk in range(CHUNKS):
                rows = rows_of(chunk)
                for t in range(0, HALF, BS):
                    tile = slice(chunk * HALF + t, chunk * HALF + t + BS)
                    grad, unit = DY[tile], U2[l, tile]
                    if l < LAYERS - 1:
                        if t == 0:
                            take(step - 1, chunk)
                        grad = grad + PRECV[step - 1, tile].astype(F32)
                    d_hidden = layer_norm_back(grad, unit, R2[l, tile], gain)
                    low = d_hidden.astype(BF16)
                    DH[tile] = d_hidden
                    DD[tile] = low
                    sums[0] = sums[0] + fold(grad * unit)
                    sums[1] = sums[1] + fold(grad)
                    sums[2] = sums[2] + fold(low.astype(F32))
                FS[...] = nt(DD[rows], weight(2, l))
                for t in range(0, HALF, 32):
                    tile = slice(chunk * HALF + t, chunk * HALF + t + 32)
                    d_inner = (FS[t : t + 32] * GP[l, tile].astype(F32)).astype(BF16)
                    DF[tile] = d_inner
                    inner_sum = inner_sum + fold(d_inner.astype(F32))
                branch = nt(DF[rows], weight(1, l))
                give(step, chunk, branch)
                DH[rows] = DH[rows] + branch
            two_rows(l, SG_G2, column_sum(sums[0]))
            two_rows(l, SG_S2, column_sum(sums[1]))
            two_rows(l, SG_BD, column_sum(sums[2]))
            inner_sum = column_sum(inner_sum)
            for t in range(4):
                SGL[l, SG_BI + t : SG_BI + t + 1, :] = inner_sum[:, 128 * t : 128 * t + 128]
            store_grad("d", l, tn(G[l], DD[...]))
            rs_start("d", l)
            store_grad("i", l, tn(Y1B[l], DF[...]))
            rs_start("i", l)
            gain = wide(l, ROW_G1)
            sums = [jnp.zeros((8, D), F32) for _ in range(3)]
            for chunk in range(CHUNKS):
                rows = rows_of(chunk)
                take(step, chunk)
                for t in range(0, HALF, BS):
                    tile = slice(chunk * HALF + t, chunk * HALF + t + BS)
                    grad = DH[tile] + PRECV[step, tile].astype(F32)
                    unit = U1[l, tile]
                    d_hidden = layer_norm_back(grad, unit, R1[l, tile], gain)
                    low = d_hidden.astype(BF16)
                    DH[tile] = d_hidden
                    DO[tile] = low
                    sums[0] = sums[0] + fold(grad * unit)
                    sums[1] = sums[1] + fold(grad)
                    sums[2] = sums[2] + fold(low.astype(F32))
                DA[rows] = nt(DO[rows], WO[l]).astype(BF16)
                DAT[:, rows] = nt(WO[l], DO[rows]).astype(BF16).astype(F32)
            two_rows(l, SG_G1, column_sum(sums[0]))
            two_rows(l, SG_S1, column_sum(sums[1]))
            two_rows(l, SG_BO, column_sum(sums[2]))
            if l == LAYERS - 1:
                links.arrived(AX, attended_in)
            own_part = tn(AN[l], DO[:, my_cols])
            other_part = tn(AX[l], DO[:, my_cols])
            if gather:
                part = n_blk // 2
                shape = (part, n_plane, 16, 128)
                r["G_o"][l, pl.ds(c * part, part)] = own_part.astype(BF16).reshape(shape)
                r["G_o"][l, pl.ds((1 - c) * part, part)] = other_part.astype(BF16).reshape(shape)
            else:
                r["G_o"][l, c] = own_part
                r["G_o"][l, 1 - c] = other_part
            rs_start("o", l)
            keys, values = QKV[l, :, 128:256], QKV[l, :, 256:384]
            for chunk in range(CHUNKS):
                rows = rows_of(chunk)
                d_query = []
                for h in (0, 1):
                    head = slice(h * HD, (h + 1) * HD)
                    ST[...] = nt(values, of_head(DA[rows], h))
                    inner = column_sum(DAT[head, rows] * AT[l, head, rows])
                    for kb in range(NB):
                        block = slice(kb * BS, (kb + 1) * BS)
                        d_score = PR[l, h, block, rows].astype(F32) * (ST[block] - inner)
                        DS[h, block, rows] = d_score.astype(BF16)
                        LR[h, kb : kb + 1, rows] = column_sum(fold(d_score))
                    d_query.append(nn(KT[l, head], DS[h, :, rows]))
                d_query = jnp.concatenate(d_query, axis=0) * 0.125
                DQKV[rows, 0:128] = d_query.T.astype(BF16)
                if l < LAYERS - 1:
                    rs_z("d", 1)
                    rs_z("i", 1)
            d_keys = jnp.zeros((SEQ, 128), F32)
            d_values = jnp.zeros((SEQ, 128), F32)
            for h in (0, 1):
                d_keys = d_keys + nn(DS[h], of_head(QKV[l, :, 0:128], h))
                d_values = d_values + nn(PR[l, h], of_head(DA[...], h))
            DQKV[:, 128:256] = d_keys.astype(BF16)
            DQKV[:, 256:384] = d_values.astype(BF16)
            by_block = lax.broadcasted_iota(jnp.int32, (128, SEQ), 1) // BS
            by_block = (by_block == lax.broadcasted_iota(jnp.int32, (128, SEQ), 0)).astype(F32)
            for h in (0, 1):
                table = lax.dot_general(
                    LR[h], by_block, (((1,), (1,)), ((), ())), preferred_element_type=F32, precision=HIGHEST
                )
                SGL[l, SG_LG + 8 * h : SG_LG + 8 * h + 8, :] = table
            for chunk in range(CHUNKS):
                rows = rows_of(chunk)
                branch = nt(DQKV[rows], weight_qkv(l))
                give(step + 1, chunk, branch)
                DY[rows] = DH[rows] + branch
            store_grad("q", l, tn(XL[l], DQKV[...]))
            rs_start("q", l)
            SGL[l, SG_BQ : SG_BQ + 1, :] = column_sum(fold(DQKV[:, 0:128].astype(F32)))
            SGL[l, SG_BV : SG_BV + 1, :] = column_sum(fold(DQKV[:, 256:384].astype(F32)))
            small_start(l)
            if l < LAYERS - 1:
                rs_z("o", 1)
                rs_z("q", 1)
                small_z(1)
        for chunk in range(CHUNKS):
            take(step + 1, chunk)
            for t in range(0, HALF, BS):
                tile = slice(chunk * HALF + t, chunk * HALF + t + BS)
                grad = DY[tile] + PRECV[step + 1, tile].astype(F32)
                YB[1][(chunk * HALF + t) // BS] = grad.astype(BF16)
        send_back(1)
        SGF = r["SGF"]
        if gather:
            rs_z("d", 0)
            rs_z("i", 0)
            rs_z("o", 0)
            small_z(0)
            FX, RX = r["FX"], r["RX"]
            kept = {}

            def finish(kind, l, at):
                total = rs_end(kind, l)
                width = total.shape[1]
                kept[kind, l] = jnp.where(c == 0, total[0:8], total[8:16])
                FX[l, :, at : at + width] = jnp.where(c == 0, total[8:16], total[0:8])

            for l in reversed(range(LAYERS)):
                r["gdown"][l] = rs_end("d", l)
                finish("i", l, 512)
                if l > 0:
                    finish("o", l, 384)
                    finish("q", l, 0)
                    SGF[c, l] = small_end(l)
                if l == LAYERS - 1:
                    rs_z("q", 0)
        take_back(0, r["out"])
        if gather:
            finish("o", 0, 384)
            SGF[c, 0] = small_end(0)
            sgf_in = links.recv_sem()
            links.push(SGF.at[c], SGF.at[c], links.send_sem(SGF.at[0]), sgf_in, partner)
            finish("q", 0, 0)
            fx_in = links.recv_sem()
            links.push(FX, RX, links.send_sem(FX), fx_in, partner)
            links.arrived(SGF.at[0], sgf_in)
        else:
            SGF[c] = SGL[...]
            SGF[1 - c] = jnp.zeros(SGL.shape, F32)
        for l in range(LAYERS):

            def row(core, at):
                return SGF[core, l, at : at + 1, :]

            if gather:
                woven = [weave_groups(row(0, at), row(1, at)) for at in (0, 1, 2, 3)]
                tiles = (
                    (row(0, 0), row(1, 0), row(0, 1), row(1, 1), row(0, 2)),
                    (row(0, 0), row(0, 1), row(0, 2), *woven[3]),
                    (*woven[0], *woven[1], woven[2][0]),
                    (woven[0][1], row(0, 1), row(0, 2), row(0, 3), row(0, 4)),
                )
                for t in range(5):
                    choice = tiles[0][t]
                    for owner in range(1, n_blk):
                        choice = jnp.where(z == owner, tiles[owner][t], choice)
                    r["BT"][l, t : t + 1, :] = choice
                lane = lanes((1, 128))
                start = w * widths[0]
                tile, offset = lax.div(start, 128), lax.rem(start, 128)
                shift = lax.rem(128 - offset, 128)
                first = pltpu.roll(r["BT"][l, pl.ds(tile, 1), :], shift, 1)
                second = pltpu.roll(r["BT"][l, pl.ds(tile + 1, 1), :], shift, 1)
                r["gbias"][l : l + 1, :] = jnp.where(lane < 128 - offset, first, second)[:, 0 : widths[0]]
                gain = pltpu.roll(row(0, 5), lax.rem(128 - w * widths[1], 128), 1)
                r["ggain"][l : l + 1, :] = gain[:, 0 : widths[1]]
                table = SGF[lax.div(z, 2), l, 8:16, :]
                wide_lane = lanes((8, 128))
                column = jnp.sum(jnp.where(wide_lane == w, table, 0.0), axis=1, keepdims=True)
                diagonal = wide_lane == lax.broadcasted_iota(jnp.int32, (8, 128), 0)
                values_row = column_sum(jnp.where(diagonal, column, 0.0))[:, 0:NB]
                logit = r["mask_logits"][...].astype(F32)[l : l + 1]
                r["glog"][l : l + 1, :] = values_row / (1.0 + jnp.exp(logit))
                continue

            def put(at, value):
                if at < ROW_G1:
                    r["gbias"][l : l + 1, 128 * at : 128 * at + 128] = value
                else:
                    at -= ROW_G1
                    r["ggain"][l : l + 1, 128 * at : 128 * at + 128] = value

            for core in (0, 1):
                put(ROW_BQ + core, row(core, SG_BQ))
                put(ROW_BV + core, row(core, SG_BV))
                for h in (0, 1):
                    r["glog"][l, 2 * core + h] = SGF[core, l, SG_LG + 8 * h : SG_LG + 8 * h + 8, :]
            singles = ((ROW_BO, SG_BO), (ROW_S1, SG_S1), (ROW_BD, SG_BD), (ROW_S2, SG_S2), (ROW_G1, SG_G1), (ROW_G2, SG_G2))
            for at, source in singles:
                for j in (0, 1):
                    put(at + j, row(0, source + j))
            for t in range(4):
                first, second = weave_groups(row(0, SG_BI + t), row(1, SG_BI + t))
                put(ROW_BI + 2 * t, first)
                put(ROW_BI + 2 * t + 1, second)
        if gather:
            links.arrived(RX, fx_in)
            for l in range(LAYERS):
                own = jnp.concatenate([kept[kind, l] for kind in ("q", "o", "i")], axis=1)
                other = RX[l]
                zero = jnp.where(c == 0, own, other)
                one = jnp.where(c == 0, other, own)
                for j in range(3):
                    r["gqkv"][l, :, 256 * j : 256 * j + 128] = zero[:, 128 * j : 128 * j + 128]
                    r["gqkv"][l, :, 256 * j + 128 : 256 * j + 256] = one[:, 128 * j : 128 * j + 128]
                r["gout"][l, :, 0:128] = zero[:, 384:512]
                r["gout"][l, :, 128:256] = one[:, 384:512]
                for t in range(4):
                    at = 512 + 128 * t
                    first, second = weave_groups(zero[:, at : at + 128], one[:, at : at + 128])
                    r["gin"][l, :, 256 * t : 256 * t + 128] = first
                    r["gin"][l, :, 256 * t + 128 : 256 * t + 256] = second
        take_back(1, r["gtok"])
        links.drain()
        for kind in range(3):
            wait_pieces(token_pieces(kind), 2 * n_seq, r["tok_send"].at[kind], None, True)
        for which in range(2):
            wait_pieces(return_pieces(which), n_blk, r["ret_send"].at[which], None, True)

    return kernel


def call_kernel(n_blk, n_wa, gather, named):
    vmem = pl.BlockSpec(memory_space=pltpu.VMEM)
    smem = pl.BlockSpec(memory_space=pltpu.SMEM)
    in_names = list(named)
    shapes = dict(out=(BLK_DEV, BS, D), gtok=(BLK_DEV, BS, D))
    if gather:
        sources = ("w_qkv", "w_out", "w_in", "w_down", "biases", "gains", "mask_logits")
        results = ("gqkv", "gout", "gin", "gdown", "gbias", "ggain", "glog")
        shapes.update({result: named[source].shape for result, source in zip(results, sources)})
    else:
        shapes.update(
            gbias=(LAYERS, 6 * D + FF),
            ggain=(LAYERS, 2 * D),
            glog=(LAYERS, H, NB, 128),
            G_d=(LAYERS, MY_FF, D),
            G_i=(LAYERS, D, MY_FF),
            G_o=(LAYERS, 2, 128, 128),
            G_q=(LAYERS, D, 384),
        )
    hold = pltpu.VMEM if gather else jax.ShapeDtypeStruct
    scratch = scratch_shapes(n_blk, n_wa, gather)
    kernel = make_kernel(n_blk, n_wa, gather, in_names, list(shapes), list(scratch))
    results = pl.pallas_call(
        kernel,
        out_shape=[hold(shape, F32) for shape in shapes.values()],
        in_specs=[smem if name in ("place_smem", "masked_count") else vmem for name in in_names],
        out_specs=[vmem] * len(shapes),
        scratch_shapes=list(scratch.values()),
        compiler_params=pltpu.CompilerParams(
            collective_id=0, has_side_effects=True, vmem_limit_bytes=60 * 2**20
        ),
        name="encoder",
    )(*named.values())
    if gather:
        results = pl.pallas_call(
            write_out,
            out_shape=[jax.ShapeDtypeStruct(shape, F32) for shape in shapes.values()],
            in_specs=[vmem] * len(shapes),
            out_specs=[pl.BlockSpec(memory_space=pl.ANY)] * len(shapes),
            scratch_shapes=[pltpu.SemaphoreType.DMA((len(shapes),))],
            name="write_out",
        )(*[pltpu.with_memory_space_constraint(result, pltpu.VMEM) for result in results])
    return dict(zip(shapes, results))


def write_out(*refs):
    count = (len(refs) - 1) // 2
    sems = refs[-1]
    copies = [pltpu.make_async_copy(refs[k], refs[count + k], sems.at[k]) for k in range(count)]
    for copy in copies:
        copy.start()
    for copy in copies:
        copy.wait()


def local(
    tokens,
    placement,
    block_mask,
    w_qkv,
    w_out,
    w_in,
    w_down,
    biases,
    gains,
    mask_logits,
    masked_pos,
    masked_count,
    masked_grad,
):
    n_blk, n_wa = lax.axis_size("blk"), lax.axis_size("wa")
    both = ("blk", "wa")
    core = lax.rem(lax.axis_index("wa"), 2)
    gather = w_qkv.shape[1] == 8 and n_blk == H and n_wa == NB
    named = dict(
        tokens=tokens.reshape(BLK_DEV, BS, D),
        place_smem=placement,
        place_vmem=placement,
        block_mask=block_mask,
        masked_pos=masked_pos.reshape(1, -1),
        masked_count=masked_count,
        masked_grad=masked_grad.reshape(-1, D),
    )
    if gather:
        named.update(
            w_qkv=w_qkv, w_out=w_out, w_in=w_in, w_down=w_down, biases=biases, gains=gains, mask_logits=mask_logits
        )
    else:
        shards = (w_qkv, w_out, w_in, w_down, biases, gains, mask_logits)
        whole = [lax.all_gather(shard, both, axis=1, tiled=True) for shard in shards]
        qkv = lax.dynamic_index_in_dim(whole[0].reshape(LAYERS, D, 3, 2, 128), core, 3, False)
        qkv = qkv.reshape(LAYERS, D, 384)
        inner = lax.dynamic_index_in_dim(whole[2].reshape(LAYERS, D, 16, 2, 32), core, 3, False)
        down = lax.dynamic_index_in_dim(whole[3].reshape(LAYERS, 16, 2, 32, D), core, 2, False)
        vectors = jnp.concatenate([whole[4], whole[5]], axis=1).astype(F32)
        logits = whole[6].astype(F32).reshape(LAYERS, H, NB, NB)
        named.update(
            WA=qkv,
            WO=lax.dynamic_slice_in_dim(whole[1], core * 128, 128, axis=1),
            WI=inner.reshape(LAYERS, D, MY_FF),
            WD=down.reshape(LAYERS, MY_FF, D),
            PV=vectors.reshape(LAYERS, PV_ROWS, 128),
            LG=jnp.pad(logits, ((0, 0), (0, 0), (0, 0), (0, 128 - NB))),
        )
    got = call_kernel(n_blk, n_wa, gather, named)
    if gather:
        weight_grads = (got["gqkv"], got["gout"], got["gin"], got["gdown"])
        small = (got["gbias"], got["ggain"], got["glog"])
    else:
        grad_logits = jnp.swapaxes(got["glog"][..., 0:NB], 2, 3).reshape(LAYERS, H * NB * NB)

        def one_core(part, axis):
            halves = [jnp.where(core == side, part, 0.0) for side in (0, 1)]
            return jnp.stack(halves, axis=axis)

        whole = (
            one_core(got["G_q"].reshape(LAYERS, D, 3, 128), 3).reshape(LAYERS, D, 3 * D),
            one_core(got["G_o"].reshape(LAYERS, D, 128), 2).reshape(LAYERS, D, D),
            one_core(got["G_i"].reshape(LAYERS, D, 16, 32), 3).reshape(LAYERS, D, FF),
            one_core(got["G_d"].reshape(LAYERS, 16, 32, D), 2).reshape(LAYERS, FF, D),
            got["gbias"],
            got["ggain"],
            grad_logits,
        )
        summed = [lax.psum_scatter(part, both, scatter_dimension=1, tiled=True) for part in whole]
        grad_mask = summed[6] * jax.nn.sigmoid(-mask_logits.astype(F32))
        weight_grads, small = tuple(summed[:4]), (summed[4], summed[5], grad_mask)
    return (
        got["out"].reshape(tokens.shape),
        got["gtok"].reshape(tokens.shape),
        *weight_grads,
        *small,
    )


def solution(mesh):
    placed = (
        P("wa", "blk", None, None),
        P("wa", None),
        P(),
        P(None, ("blk", "wa"), None),
        P(None, ("blk", "wa"), None),
        P(None, ("blk", "wa"), None),
        P(None, ("blk", "wa"), None),
        P(None, ("blk", "wa")),
        P(None, ("blk", "wa")),
        P(None, ("blk", "wa")),
        P("wa", "blk", None),
        P("wa", "blk"),
        P("wa", "blk", None, None),
    )
    return jax.shard_map(
        local,
        mesh=mesh,
        in_specs=placed,
        out_specs=(
            P("wa", "blk", None, None),
            P("wa", "blk", None, None),
            P(None, ("blk", "wa"), None),
            P(None, ("blk", "wa"), None),
            P(None, ("blk", "wa"), None),
            P(None, ("blk", "wa"), None),
            P(None, ("blk", "wa")),
            P(None, ("blk", "wa")),
            P(None, ("blk", "wa")),
        ),
        check_vma=False,
    )
```

```python
import functools

import jax
import jax.numpy as jnp
from jax import lax
from jax.experimental import pallas as pl
from jax.experimental.pallas import tpu as pltpu
from jax.sharding import PartitionSpec as P

D = 256
H = 4
HD = 64
FF = 1024
NB = 8
BS = 64
SEQ = 512
LAYERS = 2
BLK_DEV = 4
HALF = 512
CHUNKS = SEQ // HALF
FWD = 512
FWD_CHUNKS = SEQ // FWD
MY_FF = FF // 2
NEG = -1e30
EPS = 1e-05
MESH = pl.DeviceIdType.MESH
F32 = jnp.float32
BF16 = jnp.bfloat16
HIGHEST = lax.Precision.HIGHEST

ROW_BQ, ROW_BV, ROW_BO, ROW_S1, ROW_BI, ROW_BD, ROW_S2, ROW_G1, ROW_G2 = 0, 2, 4, 6, 8, 16, 18, 20, 22
PV_ROWS = 24
SG_BQ, SG_BV, SG_BI, SG_BO, SG_S1, SG_BD, SG_S2, SG_G1, SG_G2, SG_LG = 0, 1, 2, 6, 8, 10, 12, 14, 16, 24
SG_ROWS = 40
SLAB = 16
SLAB_ROWS = (
    (SG_BQ, SG_BV, SG_BO),
    (SG_BO + 1, SG_S1, SG_S1 + 1, SG_BI),
    (SG_BI + 1, SG_BI + 2, SG_BI + 3),
    (SG_BI + 3, SG_BD, SG_BD + 1, SG_S2, SG_S2 + 1),
)
SLAB_GAINS = (SG_G1, SG_G1 + 1, SG_G2, SG_G2 + 1)


def nn(left, right):
    return jnp.dot(left, right, preferred_element_type=F32)


def nt(left, right):
    return lax.dot_general(left, right, (((1,), (1,)), ((), ())), preferred_element_type=F32)


def tn(left, right):
    return lax.dot_general(left, right, (((0,), (0,)), ((), ())), preferred_element_type=F32)


def lanes(shape):
    return lax.broadcasted_iota(jnp.int32, shape, len(shape) - 1)


def turn(value, shift):
    return pltpu.roll(value, shift % 128, 1)


def pick_groups(first, second, core):
    if isinstance(core, int):
        if core == 1:
            first, second = turn(first, -32), turn(second, -32)
    else:
        first = jnp.where(core == 1, turn(first, -32), first)
        second = jnp.where(core == 1, turn(second, -32), second)
    group = lanes(first.shape) // 32
    return jnp.where(
        group == 0,
        first,
        jnp.where(group == 1, turn(first, -32), jnp.where(group == 2, turn(second, 64), turn(second, 32))),
    )


def weave_groups(zero, one):
    group = lanes(zero.shape) // 32
    first = jnp.where(
        group == 0, zero, jnp.where(group == 1, turn(one, 32), jnp.where(group == 2, turn(zero, 32), turn(one, 64)))
    )
    second = jnp.where(
        group == 0,
        turn(zero, -64),
        jnp.where(group == 1, turn(one, -32), jnp.where(group == 2, turn(zero, -32), one)),
    )
    return first, second


class Links:
    def __init__(self, send, recv, anyone):
        self.send, self.recv, self.anyone = send, recv, anyone
        self.send_used = self.recv_used = 0
        self.pending = {}
        self.pending_if = []

    def recv_sem(self):
        self.recv_used += 1
        return self.recv_used - 1

    def send_sem(self, bytes_like):
        self.send_used += 1
        self.pending[self.send_used - 1] = bytes_like
        return self.send_used - 1

    def send_sem_if(self, condition, bytes_like):
        self.send_used += 1
        self.pending_if.append((condition, self.send_used - 1, bytes_like))
        return self.send_used - 1

    def push(self, source, target, send_sem, recv_sem, device):
        remote(source, target, self.send.at[send_sem], self.recv.at[recv_sem], device).start()

    def arrived(self, bytes_like, recv_sem):
        remote(bytes_like, bytes_like, self.send.at[0], self.recv.at[recv_sem], self.anyone).wait_recv()

    def drain(self):
        for send_sem, bytes_like in self.pending.items():
            remote(bytes_like, bytes_like, self.send.at[send_sem], self.recv.at[0], self.anyone).wait_send()
        for condition, send_sem, bytes_like in self.pending_if:

            @pl.when(condition)
            def _():
                remote(bytes_like, bytes_like, self.send.at[send_sem], self.recv.at[0], self.anyone).wait_send()


def remote(source, target, send_sem, recv_sem, device):
    return pltpu.make_async_remote_copy(
        src_ref=source,
        dst_ref=target,
        send_sem=send_sem,
        recv_sem=recv_sem,
        device_id=device,
        device_id_type=MESH,
    )


def layer_norm(hidden, gain, shift):
    mean = jnp.sum(hidden, axis=1, keepdims=True) * (1.0 / D)
    centred = hidden - mean
    var = jnp.sum(centred * centred, axis=1, keepdims=True) * (1.0 / D)
    rstd = lax.rsqrt(var + EPS)
    unit = centred * rstd
    return unit * gain + shift, unit, rstd


def layer_norm_back(grad, unit, rstd, gain):
    scaled = grad * gain
    mean_one = jnp.sum(scaled, axis=1, keepdims=True) * (1.0 / D)
    mean_two = jnp.sum(scaled * unit, axis=1, keepdims=True) * (1.0 / D)
    return rstd * (scaled - mean_one - unit * mean_two)


def fold(value):
    rows, cols = value.shape
    return jnp.sum(value.reshape(rows // 8, 8, cols), axis=0)


def column_sum(value):
    return jnp.sum(value, axis=0, keepdims=True)


SEND_SEMS, RECV_SEMS = 46, 82


def scratch_shapes(n_blk, n_wa, gather):
    n_plane, n_seq = n_wa // 2, n_blk // 2
    vmem = pltpu.VMEM
    shapes = dict(
        TOK=vmem((n_blk, 2, 2, BS, D), BF16),
        MGS=vmem((2, 32, D), BF16),
        MRS=vmem((8, 128), jnp.int32),
        MG=vmem((n_blk, 2, 32, D), BF16),
        MR=vmem((n_blk, 8, 128), jnp.int32),
        PGV=vmem((2, 8, 128), jnp.int32),
        PGS=pltpu.SMEM((2, 8, 128), jnp.int32),
        YB0=vmem((NB, BS, D), BF16),
        YB1=vmem((NB, BS, D), BF16),
        SND0=vmem((n_blk, 2, BS, D), BF16),
        SND1=vmem((n_blk, 2, BS, D), BF16),
        RET0=vmem((n_seq, 2, 2, BS, D), BF16),
        RET1=vmem((n_seq, 2, 2, BS, D), BF16),
        PSEND=vmem((4 * LAYERS, SEQ, D), BF16),
        PRECV=vmem((4 * LAYERS, SEQ, D), BF16),
        X=vmem((SEQ, D), F32),
        XL=vmem((LAYERS, SEQ, D), BF16),
        QKV=vmem((LAYERS, SEQ, 384), BF16),
        KT=vmem((LAYERS, 128, SEQ), BF16),
        VT=vmem((128, SEQ), BF16),
        PR=vmem((LAYERS, 2, SEQ, SEQ), BF16),
        AT=vmem((LAYERS, 128, SEQ), F32),
        AN=vmem((LAYERS, SEQ, 128), BF16),
        AX=vmem((LAYERS, SEQ, 128), BF16),
        ST=vmem((SEQ, HALF), F32),
        DS=vmem((2, SEQ, SEQ), BF16),
        PO=vmem((SEQ, D), F32),
        U1=vmem((LAYERS, SEQ, D), F32),
        R1=vmem((LAYERS, SEQ, 1), F32),
        U2=vmem((LAYERS, SEQ, D), F32),
        R2=vmem((LAYERS, SEQ, 1), F32),
        Y1B=vmem((LAYERS, SEQ, D), BF16),
        FS=vmem((HALF, MY_FF), F32),
        CDF=vmem((HALF, MY_FF), F32),
        G=vmem((LAYERS, SEQ, MY_FF), BF16),
        GP=vmem((LAYERS, SEQ, MY_FF), BF16),
        DY=vmem((SEQ, D), F32),
        DD=vmem((SEQ, D), BF16),
        DF=vmem((SEQ, MY_FF), BF16),
        DH=vmem((SEQ, D), F32),
        DO=vmem((SEQ, D), BF16),
        DA=vmem((SEQ, 128), BF16),
        DAT=vmem((128, SEQ), F32),
        DQKV=vmem((SEQ, 384), BF16),
        BIAS=vmem((LAYERS, 2, NB, SEQ), F32),
        LR=vmem((2, NB, SEQ), F32),
        SGL=vmem((LAYERS, SG_ROWS, 128), F32),
        SGF=vmem((2, LAYERS, SLAB if gather else SG_ROWS, 128), F32),
        link_send=pltpu.SemaphoreType.DMA((SEND_SEMS if gather else 8,)),
        link_recv=pltpu.SemaphoreType.DMA((RECV_SEMS if gather else 16,)),
        tok_send=pltpu.SemaphoreType.DMA((3,)),
        tok_recv=pltpu.SemaphoreType.DMA((3,)),
        ret_send=pltpu.SemaphoreType.DMA((2,)),
        ret_recv=pltpu.SemaphoreType.DMA((2,)),
        local_sems=pltpu.SemaphoreType.DMA((6,)),
    )
    if gather:
        shapes.update(
            WA=vmem((LAYERS, n_blk, n_plane, 16, 512), BF16),
            WI=vmem((LAYERS, n_blk, n_plane, 16, MY_FF), BF16),
            WD=vmem((LAYERS, n_blk, n_plane, 32, D), BF16),
            WO=vmem((LAYERS, 128, D), BF16),
            WOX=vmem((LAYERS, n_blk // 2, n_plane, 16, 128), BF16),
            PV=vmem((LAYERS, PV_ROWS, 128), F32),
            LG=vmem((LAYERS, H, NB, 128), F32),
            S0=vmem((2, 16, 512), BF16),
            R0=vmem((2, 16, 512), BF16),
            SP=vmem((n_blk, n_plane, 2, 8, 128), F32),
            FX=vmem((LAYERS, 8, 1024), F32),
            RX=vmem((LAYERS, 8, 1024), F32),
            SLO=vmem((LAYERS, n_blk, SLAB, 128), BF16),
            SLP=vmem((LAYERS, n_plane - 1, n_blk, SLAB, 128), BF16),
            SLS=vmem((LAYERS, n_blk, SLAB, 128), BF16),
            SLZ=vmem((LAYERS, n_blk - 1, SLAB, 128), BF16),
            BT=vmem((LAYERS, 8, 128), F32),
        )
        for kind, (rows, cols) in RS_KINDS.items():
            shapes["G_" + kind] = vmem((LAYERS, n_blk, n_plane, rows, cols), BF16)
            shapes["RP_" + kind] = vmem((LAYERS, 2, 3, n_blk // 2, rows, cols), BF16)
            shapes["SZ_" + kind] = vmem((LAYERS, n_blk, rows, cols), BF16)
            shapes["RZ_" + kind] = vmem((LAYERS, n_blk - 1, rows, cols), BF16)
    return shapes


RS_KINDS = {"d": (32, D), "i": (16, MY_FF), "o": (16, 128), "q": (16, 384)}


def make_kernel(n_blk, n_wa, gather, in_names, out_names, scratch_names):
    n_plane = n_wa // 2
    n_seq = n_blk // 2
    n_slots = n_blk * BLK_DEV

    def kernel(*refs):
        r = dict(zip(in_names + out_names + scratch_names, refs))
        place_smem = r["place_smem"]
        z = lax.axis_index("blk")
        w = lax.axis_index("wa")
        c = lax.rem(w, 2)
        p = lax.div(w, 2)
        group = lax.div(z, n_seq)
        seq = lax.rem(z, n_seq)
        partner = (z, p * 2 + (1 - c))
        links = Links(r["link_send"], r["link_recv"], partner)
        x_peer, y_peer = (z, w ^ 2), (z, w ^ 4)
        in_middle = jnp.logical_or(z == 1, z == 2)
        z_next, z_far = (z ^ 1, w), (2 - lax.div(z, 2), w)
        far_pair = pl.ds(2 - 2 * lax.div(z, 2), 2)
        local_sems = r["local_sems"]
        my_cols = pl.ds(pl.multiple_of(c * 128, 128), 128)
        other_cols = pl.ds(pl.multiple_of((1 - c) * 128, 128), 128)

        TOK, MGS, MRS, MG, MR = (r[name] for name in ("TOK", "MGS", "MRS", "MG", "MR"))
        PGV, PGS = r["PGV"], r["PGS"]
        PGV[c, 0:1, 0:n_slots] = r["place_vmem"][...]
        MGS[...] = r["masked_grad"][...].astype(BF16).reshape(2, 32, D)
        chosen = r["masked_pos"][...]
        slot_of = lax.shift_right_logical(chosen, 6)
        block_of = jnp.zeros_like(chosen)
        for j in range(BLK_DEV):
            block_of = jnp.where(slot_of == j, place_smem[0, z * BLK_DEV + j], block_of)
        target_row = block_of * BS + (chosen & (BS - 1))
        target_row = jnp.where(lanes(chosen.shape) < r["masked_count"][0, 0], target_row, -1)
        MRS[0:1, 0:64] = target_row
        MRS[0:1, 64:128] = target_row
        if gather:
            WA, WI, WD, SP = r["WA"], r["WI"], r["WD"], r["SP"]
            own_rows = ([], [])
            give_rows = ([], [])
            for l in range(LAYERS):
                qkv = r["w_qkv"][l].astype(F32)
                out_part = r["w_out"][l].astype(F32)
                inner = r["w_in"][l].astype(F32)
                sides = []
                for side in (0, 1):
                    at = 128 * side
                    attn = [qkv[:, 256 * j + at : 256 * j + at + 128] for j in range(3)]
                    attn = jnp.concatenate(attn + [out_part[:, at : at + 128]], axis=1)
                    feed = []
                    for t in range(4):
                        first = inner[:, 256 * t : 256 * t + 128]
                        second = inner[:, 256 * t + 128 : 256 * t + 256]
                        feed.append(pick_groups(first, second, side))
                    sides.append((attn, jnp.concatenate(feed, axis=1)))
                for kind in (0, 1):
                    own_rows[kind].append(jnp.where(c == 0, sides[0][kind], sides[1][kind]))
                    give_rows[kind].append(jnp.where(c == 0, sides[1][kind], sides[0][kind]))
                WD[l, z, p] = r["w_down"][l]
            for kind in (0, 1):
                r["S0"][kind] = jnp.concatenate(give_rows[kind], axis=0).astype(BF16)
            SP[z, p, c] = jnp.zeros((8, 128), F32)
            widths = []
            for at, name in ((0, "biases"), (2, "gains"), (4, "mask_logits")):
                part = r[name][...].astype(F32)
                widths.append(part.shape[1])
                SP[z, p, c, at : at + 2, 0 : part.shape[1]] = part

        barrier = pltpu.get_barrier_semaphore()
        greeted = 0
        for m in range(n_blk):
            for other in (0, 1):
                if m or other:
                    pl.semaphore_signal(barrier, inc=1, device_id=(z ^ m, w ^ other), device_id_type=MESH)
                    greeted += 1
        if gather:
            for m in range(1, n_plane):
                pl.semaphore_signal(barrier, inc=1, device_id=(z, w ^ (2 * m)), device_id_type=MESH)
                greeted += 1
        pl.semaphore_wait(barrier, greeted)

        place_in = links.recv_sem()
        links.push(PGV.at[c], PGV.at[c], links.send_sem(PGV.at[0]), place_in, partner)
        if gather:
            rows_in = links.recv_sem()
            links.push(r["S0"], r["R0"], links.send_sem(r["S0"]), rows_in, partner)
            small_in = links.recv_sem()
            links.push(SP.at[z, p, c], SP.at[z, p, c], links.send_sem(SP.at[0, 0, 0]), small_in, partner)

        at_home = c == group

        def move(here, source, target, send_sem, recv_sem, local_sem, device):
            @pl.when(jnp.logical_not(here))
            def _():
                remote(source, target, send_sem, recv_sem, device).start()

            @pl.when(here)
            def _():
                pltpu.make_async_copy(source, target, local_sem).start()

        def wait_pieces(pieces, count, sem, local_sem, sending):
            def wait(n):
                copy = remote(pieces(n), pieces(n), sem, sem, partner)
                if sending:
                    copy.wait_send()
                else:
                    copy.wait_recv()

            @pl.when(jnp.logical_not(at_home))
            def _():
                wait(count)

            @pl.when(at_home)
            def _():
                wait(count - 1)
                if not sending:
                    pltpu.make_async_copy(pieces(1), pieces(1), local_sem).wait()

        def token_pieces(kind):
            def pieces(n):
                return (TOK.at[pl.ds(0, n), 0], MG.at[pl.ds(0, n), 0], MR.at[pl.ds(0, n)])[kind]

            return pieces

        def send_kind(kind, sequences=range(n_seq)):
            for s in sequences:
                chip = c * n_seq + s
                for core in (0, 1):
                    here = jnp.logical_and(chip == z, c == core)
                    source = (r["tokens"].at[pl.ds(2 * core, 2)], MGS.at[core], MRS)[kind]
                    target = (TOK.at[z, core], MG.at[z, core], MR.at[z])[kind]
                    sems = (r["tok_send"].at[kind], r["tok_recv"].at[kind])
                    move(here, source, target, *sems, local_sems.at[kind], (chip, p * 2 + core))

        def take_kind(kind):
            wait_pieces(token_pieces(kind), n_blk, r["tok_recv"].at[kind], local_sems.at[kind], False)

        if gather:
            weight_refs = (WA, WI, WD)
            ag_recv = {}
            ag_send = {}
            for kind in (0, 1, 2):
                ref = weight_refs[kind]
                likes = (ref.at[:, 0:2, 0], ref.at[0], ref.at[0, 0:2])
                ag_send[kind] = [links.send_sem(like) for like in likes]
                ag_send[kind].append(links.send_sem_if(in_middle, likes[0]))
            ag_send["small"] = [links.send_sem(like) for like in (SP.at[0:2, 0], SP.at[:, 0:2], SP.at[0:2, 0:2])]
            ag_send["small"].append(links.send_sem_if(in_middle, SP.at[0:2, 0]))

            def rows_at(name, z_at, p_at):
                if name == "small":
                    return SP.at[z_at, p_at]
                return weight_refs[name[0]].at[name[1], z_at, p_at]

            def ag_push(name, stage, z_at, p_at, device):
                ref = rows_at(name, z_at, p_at)
                send_sem = ag_send[name if name == "small" else name[0]][stage]
                links.push(ref, ref, send_sem, ag_recv[name][stage % 3], device)

            every, z_low, z_high = slice(0, 4), slice(0, 2), slice(2, 4)

            def ag_z(name):
                ag_recv[name] = [links.recv_sem() for _ in range(3)]
                ag_push(name, 0, z, p, z_far)
                ag_push(name, 0, z, p, z_next)

            def ag_xy(name):
                links.arrived(rows_at(name, 0, slice(0, 3)), ag_recv[name][0])

                @pl.when(in_middle)
                def _():
                    ag_push(name, 3, far_pair, p, z_next)

                ag_push(name, 1, every, p, x_peer)
                ag_push(name, 1, every, p, y_peer)

            def ag_pass(name):
                links.arrived(rows_at(name, every, z_low), ag_recv[name][1])
                ag_push(name, 2, z_low, p ^ 1, y_peer)
                ag_push(name, 2, z_high, p ^ 2, x_peer)

            def ag_ready(name):
                links.arrived(rows_at(name, z_low, z_low), ag_recv[name][2])

            def merge_rows(kind, l):
                own = own_rows[kind][l]
                other = r["R0"][kind].astype(F32)[8 * l : 8 * l + 8]
                merged = jnp.concatenate([jnp.where(c == 0, own, other), jnp.where(c == 0, other, own)], axis=0)
                weight_refs[kind][l, z, p] = merged.astype(BF16)

        if gather:
            links.arrived(r["R0"], rows_in)
            merge_rows(0, 0)
            ag_z((0, 0))
            links.arrived(SP.at[0, 0, 0], small_in)
            ag_z("small")
            merge_rows(1, 0)
            ag_z((1, 0))
            ag_z((2, 0))
        send_kind(0)
        if gather:
            merge_rows(0, 1)
            merge_rows(1, 1)
            ag_z((0, 1))
            ag_z((1, 1))
            ag_z((2, 1))
            ag_xy((0, 0))
            ag_xy("small")
            ag_xy((1, 0))
            ag_xy((2, 0))
            ag_pass((0, 0))
            ag_pass("small")
            ag_pass((1, 0))
            ag_pass((2, 0))

        take_kind(0)
        tokens_in = links.recv_sem()
        links.push(TOK.at[:, c], TOK.at[:, c], links.send_sem(TOK.at[:, 0]), tokens_in, partner)
        links.arrived(PGV.at[0], place_in)
        to_scalars = pltpu.make_async_copy(PGV, PGS, local_sems.at[3])
        to_scalars.start()
        to_scalars.wait()
        links.arrived(TOK.at[:, 0], tokens_in)
        X, XL = r["X"], r["XL"]
        for b in range(NB):
            at = jnp.int32(0)
            for j in range(n_slots):
                at = jnp.where(PGS[group, 0, j] == seq * NB + b, j, at)
            block = TOK[lax.div(at, 4), lax.rem(lax.div(at, 2), 2), lax.rem(at, 2)]
            X[b * BS : (b + 1) * BS] = block.astype(F32)
            XL[0, b * BS : (b + 1) * BS] = block

        send_kind(1)
        send_kind(2)

        PV, LG = r["PV"], r["LG"]
        if gather:
            ag_ready("small")
            lane = lanes((1, 128))
            for l in range(LAYERS):
                for first_row, count, width, kind_row in ((0, 20, widths[0], 0), (20, 4, widths[1], 2)):
                    tiles = [jnp.zeros((1, 128), F32)] * count
                    for device in range(n_blk * n_wa):
                        t, offset = divmod(device * width, 128)
                        dz, dw = divmod(device, n_wa)
                        piece = SP[dz, dw // 2, dw % 2, kind_row + l : kind_row + l + 1, :]
                        if offset:
                            piece = turn(piece, offset)
                        if offset + width <= 128:
                            tiles[t] = tiles[t] + piece
                        else:
                            tiles[t] = tiles[t] + jnp.where(lane >= offset, piece, 0.0)
                            tiles[t + 1] = tiles[t + 1] + jnp.where(lane < offset, piece, 0.0)
                    for t in range(count):
                        PV[l, first_row + t : first_row + t + 1, :] = tiles[t]
                for h in range(H):
                    for i in range(NB):
                        LG[l, h, i : i + 1, :] = SP[h, i // 2, i % 2, 4 + l : 5 + l, :]

        def wide(l, row):
            return jnp.concatenate([PV[l, row : row + 1, :], PV[l, row + 1 : row + 2, :]], axis=1)

        def mine(l, row):
            return jnp.where(c == 0, PV[l, row : row + 1, :], PV[l, row + 1 : row + 2, :])

        BIAS = r["BIAS"]
        spread = lax.broadcasted_iota(jnp.int32, (16, SEQ), 1) // BS
        spread = (spread == lax.broadcasted_iota(jnp.int32, (16, SEQ), 0)).astype(F32).astype(BF16)

        def over_rows(table):
            table = jnp.concatenate([table, jnp.zeros_like(table)], axis=0).astype(BF16)
            return tn(table, spread)[0:NB]

        for h in (0, 1):
            allowed = over_rows(r["block_mask"][2 * c + h].astype(F32)) > 0.5
            for l in range(LAYERS):
                logit = over_rows(LG[l, 2 * c + h])
                log_sig = jnp.minimum(logit, 0.0) - jnp.log1p(jnp.exp(-jnp.abs(logit)))
                BIAS[l, h] = jnp.where(allowed, log_sig, NEG)

        PSEND, PRECV = r["PSEND"], r["PRECV"]
        exchange_out = links.send_sem(PSEND)
        most = max(CHUNKS, FWD_CHUNKS)
        exchange_in = [links.recv_sem() for _ in range(2 * most)]

        def part_of(step, chunk):
            size = FWD if step < 2 * LAYERS else HALF
            return pl.ds(chunk * size, size)

        def give(step, chunk, value):
            part = part_of(step, chunk)
            PSEND[step, part] = value.astype(BF16)
            sem = exchange_in[most * (step % 2) + chunk]
            links.push(PSEND.at[step, part], PRECV.at[step, part], exchange_out, sem, partner)

        def take(step, chunk):
            links.arrived(PRECV.at[step, part_of(step, chunk)], exchange_in[most * (step % 2) + chunk])

        def of_head(value, h):
            keep = (lanes(value.shape) // HD) == h
            return jnp.where(keep, value, jnp.zeros_like(value))

        def fwd_rows(chunk):
            return slice(chunk * FWD, (chunk + 1) * FWD)

        def rows_of(chunk):
            return slice(chunk * HALF, (chunk + 1) * HALF)

        YB, SND, RET = ((r[name + "0"], r[name + "1"]) for name in ("YB", "SND", "RET"))

        def send_back(which):
            for dest in range(n_blk):
                for j in range(2):
                    position = lax.rem(PGS[group, 0, dest * BLK_DEV + 2 * c + j], NB)
                    SND[which][dest, j] = YB[which][position]
                here = jnp.logical_and(dest == z, c == group)
                sems = (r["ret_send"].at[which], r["ret_recv"].at[which])
                target = RET[which].at[seq, c]
                move(here, SND[which].at[dest], target, *sems, local_sems.at[4 + which], (dest, p * 2 + group))

        def return_pieces(which):
            return lambda n: SND[which].at[pl.ds(0, n)]

        def take_back(which, target_ref):
            wait_pieces(return_pieces(which), 2 * n_seq, r["ret_recv"].at[which], local_sems.at[4 + which], False)
            for j in range(BLK_DEV):
                from_seq = lax.div(place_smem[0, z * BLK_DEV + j], NB)
                target_ref[j] = RET[which][from_seq, j // 2, j % 2].astype(F32)

        QKV, KT, VT, PR, AT, AN, AX = (r[n] for n in ("QKV", "KT", "VT", "PR", "AT", "AN", "AX"))
        ST, DS, PO, FS, G, GP, Y1B = (r[n] for n in ("ST", "DS", "PO", "FS", "G", "GP", "Y1B"))
        U1, R1, U2, R2 = (r[n] for n in ("U1", "R1", "U2", "R2"))
        WO = r["WO"]
        attended_out, attended_in = links.send_sem(AX), links.recv_sem()
        if gather:
            wo_out = links.send_sem(r["WOX"])

        def weight(kind, l):
            if gather:
                ref = weight_refs[kind]
                return ref[l].reshape(ref.shape[1] * ref.shape[2] * ref.shape[3], ref.shape[4])
            return (r["WA"], r["WI"], r["WD"])[kind][l]

        def weight_qkv(l):
            if gather:
                return WA[l, :, :, :, 0:384].reshape(D, 384)
            return r["WA"][l, :, 0:384]

        for l in range(LAYERS):
            step = 2 * l
            if gather:
                ag_ready((0, l))
                part = n_blk // 2
                wo_in = links.recv_sem()
                theirs = WA.at[l, pl.ds((1 - c) * part, part), :, :, pl.ds(384, 128)]
                links.push(theirs, r["WOX"].at[l], wo_out, wo_in, partner)
                WO[l, :, my_cols] = WA[l, pl.ds(c * part, part), :, :, 384:512].reshape(128, 128)
            bias = jnp.concatenate([mine(l, ROW_BQ), jnp.zeros((1, 128), F32), mine(l, ROW_BV)], axis=1)
            scale = jnp.where(lanes((1, 384)) < 128, 0.125, 1.0)
            for chunk in range(FWD_CHUNKS):
                rows = fwd_rows(chunk)
                QKV[l, rows] = ((nn(XL[l, rows], weight_qkv(l)) + bias) * scale).astype(BF16)
            keys = QKV[l, :, 128:256]
            VT[...] = QKV[l, :, 256:384].astype(F32).T.astype(BF16)
            if gather:
                if l + 1 < LAYERS:
                    ag_xy((0, l + 1))
                    ag_xy((1, l + 1))
                    ag_xy((2, l + 1))
                links.arrived(r["WOX"].at[l], wo_in)
                WO[l, :, other_cols] = r["WOX"][l].reshape(128, 128)
            for chunk in range(FWD_CHUNKS):
                rows = fwd_rows(chunk)
                for h in (0, 1):
                    queries = of_head(QKV[l, rows, 0:128], h)
                    ST[:, 0:FWD] = nt(keys, queries)
                    top = jnp.full((8, FWD), NEG, F32)
                    for kb in range(NB):
                        score = ST[kb * BS : (kb + 1) * BS, 0:FWD] + BIAS[l, h, kb : kb + 1, rows]
                        top = jnp.maximum(top, jnp.max(score.reshape(8, 8, FWD), axis=0))
                    top = jnp.max(top, axis=0, keepdims=True)
                    total = jnp.zeros((8, FWD), F32)
                    for kb in range(NB):
                        score = ST[kb * BS : (kb + 1) * BS, 0:FWD] + BIAS[l, h, kb : kb + 1, rows]
                        weight_of = jnp.exp(score - top)
                        ST[kb * BS : (kb + 1) * BS, 0:FWD] = weight_of
                        total = total + fold(weight_of)
                    inverse = 1.0 / column_sum(total)
                    for kb in range(NB):
                        PR[l, h, kb * BS : (kb + 1) * BS, rows] = (ST[kb * BS : (kb + 1) * BS, 0:FWD] * inverse).astype(BF16)
                    AT[l, h * HD : (h + 1) * HD, rows] = nn(VT[h * HD : (h + 1) * HD], PR[l, h, :, rows])
                AN[l, rows] = AT[l, :, rows].T.astype(BF16)
                branch = nn(AN[l, rows], WO[l])
                give(step, chunk, branch)
                PO[rows] = X[rows] + branch + wide(l, ROW_BO)
                part = pl.ds(chunk * FWD, FWD)
                links.push(AN.at[l, part], AX.at[l, part], attended_out, attended_in, partner)
            KT[l] = keys.astype(F32).T.astype(BF16)
            if l == LAYERS - 1:
                take_kind(1)
                take_kind(2)
                grads_in = links.recv_sem()
                links.push(MG.at[:, c], MG.at[:, c], links.send_sem(MG.at[:, 0]), grads_in, partner)
            if gather:
                if l + 1 < LAYERS:
                    ag_pass((0, l + 1))
                ag_ready((1, l))
                ag_ready((2, l))
            for chunk in range(FWD_CHUNKS):
                rows = fwd_rows(chunk)
                take(step, chunk)
                gain, shift = wide(l, ROW_G1), wide(l, ROW_S1)
                for t in range(0, FWD, BS):
                    tile = slice(chunk * FWD + t, chunk * FWD + t + BS)
                    hidden = PO[tile] + PRECV[step, tile].astype(F32)
                    normed, unit, rstd = layer_norm(hidden, gain, shift)
                    U1[l, tile] = unit
                    R1[l, tile] = rstd
                    X[tile] = normed
                    Y1B[l, tile] = normed.astype(BF16)
                FS[0:FWD] = nn(Y1B[l, rows], weight(1, l))
                inner_bias = []
                for t in range(4):
                    row = ROW_BI + 2 * t
                    inner_bias.append(pick_groups(PV[l, row : row + 1, :], PV[l, row + 1 : row + 2, :], c))
                inner_bias = jnp.concatenate(inner_bias, axis=1)
                for t in range(0, FWD, 32):
                    tile = slice(chunk * FWD + t, chunk * FWD + t + 32)
                    inner = FS[t : t + 32] + inner_bias
                    below = 0.5 + 0.5 * lax.erf(inner * 0.7071067811865476)
                    G[l, tile] = (inner * below).astype(BF16)
                    FS[t : t + 32] = inner
                    r["CDF"][t : t + 32] = below
                branch = nn(G[l, rows], weight(2, l))
                give(step + 1, chunk, branch)
                PO[rows] = X[rows] + branch + wide(l, ROW_BD)
                for t in range(0, FWD, 32):
                    tile = slice(chunk * FWD + t, chunk * FWD + t + 32)
                    inner = FS[t : t + 32]
                    bell = jnp.exp(inner * inner * -0.5) * 0.3989422804014327
                    GP[l, tile] = (r["CDF"][t : t + 32] + inner * bell).astype(BF16)
            if gather and l + 1 < LAYERS:
                ag_pass((1, l + 1))
                ag_pass((2, l + 1))
            for chunk in range(FWD_CHUNKS):
                take(step + 1, chunk)
                gain, shift = wide(l, ROW_G2), wide(l, ROW_S2)
                for t in range(0, FWD, BS):
                    tile = slice(chunk * FWD + t, chunk * FWD + t + BS)
                    hidden = PO[tile] + PRECV[step + 1, tile].astype(F32)
                    normed, unit, rstd = layer_norm(hidden, gain, shift)
                    U2[l, tile] = unit
                    R2[l, tile] = rstd
                    X[tile] = normed
                    if l + 1 < LAYERS:
                        XL[l + 1, tile] = normed.astype(BF16)
                    else:
                        YB[0][(chunk * FWD + t) // BS] = normed.astype(BF16)
        send_back(0)

        DY, DD, DF, DH, DO, DA, DAT, DQKV = (r[n] for n in ("DY", "DD", "DF", "DH", "DO", "DA", "DAT", "DQKV"))
        LR, SGL = r["LR"], r["SGL"]
        links.arrived(MG.at[:, 0], grads_in)
        wanted = []
        lane = lanes((1, 128))
        for t in range(n_blk // 2):
            wanted.append(jnp.where(lane < 64, MR[2 * t, 0:1, :], MR[2 * t + 1, 0:1, :]))
        wanted = jnp.concatenate(wanted, axis=1) - seq * SEQ
        listed = MG[...].reshape(n_blk * 64, D)
        for chunk in range(CHUNKS):
            row_ids = lax.broadcasted_iota(jnp.int32, (HALF, n_blk * 64), 0) + chunk * HALF
            DY[rows_of(chunk)] = nn((row_ids == wanted).astype(F32).astype(BF16), listed)

        rs_recv = {}
        if gather:
            rs_out = {kind: (links.send_sem(r["RP_" + kind]), links.send_sem(r["RZ_" + kind])) for kind in RS_KINDS}

        def rs_start(kind, l):
            if not gather:
                return
            rs_recv[kind, l] = [links.recv_sem() for _ in range(2)]
            grad, parts, sem = r["G_" + kind], r["RP_" + kind], rs_recv[kind, l][0]
            out = rs_out[kind][0]
            devices = (x_peer, y_peer, (z, w ^ 6))
            for m in range(3):
                links.push(grad.at[l, z_low, p ^ (m + 1)], parts.at[l, 0, m], out, sem, devices[m])
                links.push(grad.at[l, z_high, p ^ (m + 1)], parts.at[l, 1, m], out, sem, devices[m])

        def rs_z(kind, l):
            if not gather:
                return
            grad, parts, total = r["G_" + kind], r["RP_" + kind], r["SZ_" + kind]
            links.arrived(parts.at[l], rs_recv[kind, l][0])
            for at, half in enumerate((z_low, z_high)):
                value = grad[l, half, p].astype(F32)
                for m in range(3):
                    value = value + parts[l, at, m].astype(F32)
                total[l, half] = value.astype(BF16)
            for m in range(1, n_blk):
                links.push(total.at[l, z ^ m], r["RZ_" + kind].at[l, m - 1], rs_out[kind][1], rs_recv[kind, l][1], (z ^ m, w))

        def rs_end(kind, l):
            total = r["SZ_" + kind][l, z].astype(F32)
            links.arrived(r["RZ_" + kind].at[l], rs_recv[kind, l][1])
            for m in range(1, n_blk):
                total = total + r["RZ_" + kind][l, m - 1].astype(F32)
            return total

        sg_recv = {}
        if gather:
            SLO, SLP, SLS, SLZ = (r[name] for name in ("SLO", "SLP", "SLS", "SLZ"))
            sg_out = (links.send_sem(SLP), links.send_sem(SLZ))

        def small_start(l):
            if not gather:
                return
            for owner in range(n_blk):
                parts = [SGL[l, at : at + 1, :] for at in SLAB_ROWS[owner]]
                parts += [jnp.zeros((1, 128), F32)] * (5 - len(parts))
                parts += [SGL[l, SLAB_GAINS[owner] : SLAB_GAINS[owner] + 1, :], jnp.zeros((2, 128), F32)]
                at = SG_LG + 8 * (owner % 2)
                slab = jnp.concatenate(parts + [SGL[l, at : at + 8, :]], axis=0)
                SLO[l, owner] = slab.astype(BF16)
            sg_recv[l] = [links.recv_sem() for _ in range(2)]
            for m in range(1, n_plane):
                links.push(SLO.at[l], SLP.at[l, m - 1], sg_out[0], sg_recv[l][0], (z, w ^ (2 * m)))

        def small_z(l):
            if not gather:
                return
            links.arrived(SLP.at[l], sg_recv[l][0])
            total = SLO[l].astype(F32)
            for m in range(1, n_plane):
                total = total + SLP[l, m - 1].astype(F32)
            SLS[l] = total.astype(BF16)
            for m in range(1, n_blk):
                links.push(SLS.at[l, z ^ m], SLZ.at[l, m - 1], sg_out[1], sg_recv[l][1], (z ^ m, w))

        def small_end(l):
            links.arrived(SLZ.at[l], sg_recv[l][1])
            total = SLS[l, z].astype(F32)
            for m in range(1, n_blk):
                total = total + SLZ[l, m - 1].astype(F32)
            return total

        def store_grad(kind, l, value):
            if gather:
                shape = r["G_" + kind].shape
                r["G_" + kind][l] = value.astype(BF16).reshape(shape[1:])
            else:
                r["G_" + kind][l] = value

        def two_rows(l, row, value):
            SGL[l, row : row + 1, :] = value[:, 0:128]
            SGL[l, row + 1 : row + 2, :] = value[:, 128:256]

        SGL[...] = jnp.zeros_like(SGL)
        for l in reversed(range(LAYERS)):
            step = 4 + 2 * (LAYERS - 1 - l)
            gain = wide(l, ROW_G2)
            sums = [jnp.zeros((8, D), F32) for _ in range(3)]
            inner_sum = jnp.zeros((8, MY_FF), F32)
            for chunk in range(CHUNKS):
                rows = rows_of(chunk)
                for t in range(0, HALF, BS):
                    tile = slice(chunk * HALF + t, chunk * HALF + t + BS)
                    grad, unit = DY[tile], U2[l, tile]
                    if l < LAYERS - 1:
                        if t == 0:
                            take(step - 1, chunk)
                        grad = grad + PRECV[step - 1, tile].astype(F32)
                    d_hidden = layer_norm_back(grad, unit, R2[l, tile], gain)
                    low = d_hidden.astype(BF16)
                    DH[tile] = d_hidden
                    DD[tile] = low
                    sums[0] = sums[0] + fold(grad * unit)
                    sums[1] = sums[1] + fold(grad)
                    sums[2] = sums[2] + fold(low.astype(F32))
                FS[...] = nt(DD[rows], weight(2, l))
                for t in range(0, HALF, 32):
                    tile = slice(chunk * HALF + t, chunk * HALF + t + 32)
                    d_inner = (FS[t : t + 32] * GP[l, tile].astype(F32)).astype(BF16)
                    DF[tile] = d_inner
                    inner_sum = inner_sum + fold(d_inner.astype(F32))
                branch = nt(DF[rows], weight(1, l))
                give(step, chunk, branch)
                DH[rows] = DH[rows] + branch
            two_rows(l, SG_G2, column_sum(sums[0]))
            two_rows(l, SG_S2, column_sum(sums[1]))
            two_rows(l, SG_BD, column_sum(sums[2]))
            inner_sum = column_sum(inner_sum)
            for t in range(4):
                SGL[l, SG_BI + t : SG_BI + t + 1, :] = inner_sum[:, 128 * t : 128 * t + 128]
            store_grad("d", l, tn(G[l], DD[...]))
            rs_start("d", l)
            store_grad("i", l, tn(Y1B[l], DF[...]))
            rs_start("i", l)
            gain = wide(l, ROW_G1)
            sums = [jnp.zeros((8, D), F32) for _ in range(3)]
            for chunk in range(CHUNKS):
                rows = rows_of(chunk)
                take(step, chunk)
                for t in range(0, HALF, BS):
                    tile = slice(chunk * HALF + t, chunk * HALF + t + BS)
                    grad = DH[tile] + PRECV[step, tile].astype(F32)
                    unit = U1[l, tile]
                    d_hidden = layer_norm_back(grad, unit, R1[l, tile], gain)
                    low = d_hidden.astype(BF16)
                    DH[tile] = d_hidden
                    DO[tile] = low
                    sums[0] = sums[0] + fold(grad * unit)
                    sums[1] = sums[1] + fold(grad)
                    sums[2] = sums[2] + fold(low.astype(F32))
                DA[rows] = nt(DO[rows], WO[l]).astype(BF16)
                DAT[:, rows] = nt(WO[l], DO[rows]).astype(BF16).astype(F32)
            two_rows(l, SG_G1, column_sum(sums[0]))
            two_rows(l, SG_S1, column_sum(sums[1]))
            two_rows(l, SG_BO, column_sum(sums[2]))
            if l == LAYERS - 1:
                links.arrived(AX, attended_in)
            own_part = tn(AN[l], DO[:, my_cols])
            other_part = tn(AX[l], DO[:, my_cols])
            if gather:
                part = n_blk // 2
                shape = (part, n_plane, 16, 128)
                r["G_o"][l, pl.ds(c * part, part)] = own_part.astype(BF16).reshape(shape)
                r["G_o"][l, pl.ds((1 - c) * part, part)] = other_part.astype(BF16).reshape(shape)
            else:
                r["G_o"][l, c] = own_part
                r["G_o"][l, 1 - c] = other_part
            rs_start("o", l)
            keys, values = QKV[l, :, 128:256], QKV[l, :, 256:384]
            for chunk in range(CHUNKS):
                rows = rows_of(chunk)
                d_query = []
                for h in (0, 1):
                    head = slice(h * HD, (h + 1) * HD)
                    ST[...] = nt(values, of_head(DA[rows], h))
                    inner = column_sum(DAT[head, rows] * AT[l, head, rows])
                    for kb in range(NB):
                        block = slice(kb * BS, (kb + 1) * BS)
                        d_score = PR[l, h, block, rows].astype(F32) * (ST[block] - inner)
                        DS[h, block, rows] = d_score.astype(BF16)
                        LR[h, kb : kb + 1, rows] = column_sum(fold(d_score))
                    d_query.append(nn(KT[l, head], DS[h, :, rows]))
                d_query = jnp.concatenate(d_query, axis=0) * 0.125
                DQKV[rows, 0:128] = d_query.T.astype(BF16)
                if l < LAYERS - 1:
                    rs_z("d", 1)
                    rs_z("i", 1)
            d_keys = jnp.zeros((SEQ, 128), F32)
            d_values = jnp.zeros((SEQ, 128), F32)
            for h in (0, 1):
                d_keys = d_keys + nn(DS[h], of_head(QKV[l, :, 0:128], h))
                d_values = d_values + nn(PR[l, h], of_head(DA[...], h))
            DQKV[:, 128:256] = d_keys.astype(BF16)
            DQKV[:, 256:384] = d_values.astype(BF16)
            by_block = lax.broadcasted_iota(jnp.int32, (128, SEQ), 1) // BS
            by_block = (by_block == lax.broadcasted_iota(jnp.int32, (128, SEQ), 0)).astype(F32)
            for h in (0, 1):
                table = lax.dot_general(
                    LR[h], by_block, (((1,), (1,)), ((), ())), preferred_element_type=F32, precision=HIGHEST
                )
                SGL[l, SG_LG + 8 * h : SG_LG + 8 * h + 8, :] = table
            for chunk in range(CHUNKS):
                rows = rows_of(chunk)
                branch = nt(DQKV[rows], weight_qkv(l))
                give(step + 1, chunk, branch)
                DY[rows] = DH[rows] + branch
            store_grad("q", l, tn(XL[l], DQKV[...]))
            rs_start("q", l)
            SGL[l, SG_BQ : SG_BQ + 1, :] = column_sum(fold(DQKV[:, 0:128].astype(F32)))
            SGL[l, SG_BV : SG_BV + 1, :] = column_sum(fold(DQKV[:, 256:384].astype(F32)))
            small_start(l)
            if l < LAYERS - 1:
                rs_z("o", 1)
                rs_z("q", 1)
                small_z(1)
        for chunk in range(CHUNKS):
            take(step + 1, chunk)
            for t in range(0, HALF, BS):
                tile = slice(chunk * HALF + t, chunk * HALF + t + BS)
                grad = DY[tile] + PRECV[step + 1, tile].astype(F32)
                YB[1][(chunk * HALF + t) // BS] = grad.astype(BF16)
        send_back(1)
        SGF = r["SGF"]
        if gather:
            rs_z("d", 0)
            rs_z("i", 0)
            rs_z("o", 0)
            small_z(0)
            FX, RX = r["FX"], r["RX"]
            kept = {}

            def finish(kind, l, at):
                total = rs_end(kind, l)
                width = total.shape[1]
                kept[kind, l] = jnp.where(c == 0, total[0:8], total[8:16])
                FX[l, :, at : at + width] = jnp.where(c == 0, total[8:16], total[0:8])

            for l in reversed(range(LAYERS)):
                r["gdown"][l] = rs_end("d", l)
                finish("i", l, 512)
                if l > 0:
                    finish("o", l, 384)
                    finish("q", l, 0)
                    SGF[c, l] = small_end(l)
                if l == LAYERS - 1:
                    rs_z("q", 0)
        take_back(0, r["out"])
        if gather:
            finish("o", 0, 384)
            SGF[c, 0] = small_end(0)
            sgf_in = links.recv_sem()
            links.push(SGF.at[c], SGF.at[c], links.send_sem(SGF.at[0]), sgf_in, partner)
            finish("q", 0, 0)
            fx_in = links.recv_sem()
            links.push(FX, RX, links.send_sem(FX), fx_in, partner)
            links.arrived(SGF.at[0], sgf_in)
        else:
            SGF[c] = SGL[...]
            SGF[1 - c] = jnp.zeros(SGL.shape, F32)
        for l in range(LAYERS):

            def row(core, at):
                return SGF[core, l, at : at + 1, :]

            if gather:
                woven = [weave_groups(row(0, at), row(1, at)) for at in (0, 1, 2, 3)]
                tiles = (
                    (row(0, 0), row(1, 0), row(0, 1), row(1, 1), row(0, 2)),
                    (row(0, 0), row(0, 1), row(0, 2), *woven[3]),
                    (*woven[0], *woven[1], woven[2][0]),
                    (woven[0][1], row(0, 1), row(0, 2), row(0, 3), row(0, 4)),
                )
                for t in range(5):
                    choice = tiles[0][t]
                    for owner in range(1, n_blk):
                        choice = jnp.where(z == owner, tiles[owner][t], choice)
                    r["BT"][l, t : t + 1, :] = choice
                lane = lanes((1, 128))
                start = w * widths[0]
                tile, offset = lax.div(start, 128), lax.rem(start, 128)
                shift = lax.rem(128 - offset, 128)
                first = pltpu.roll(r["BT"][l, pl.ds(tile, 1), :], shift, 1)
                second = pltpu.roll(r["BT"][l, pl.ds(tile + 1, 1), :], shift, 1)
                r["gbias"][l : l + 1, :] = jnp.where(lane < 128 - offset, first, second)[:, 0 : widths[0]]
                gain = pltpu.roll(row(0, 5), lax.rem(128 - w * widths[1], 128), 1)
                r["ggain"][l : l + 1, :] = gain[:, 0 : widths[1]]
                table = SGF[lax.div(z, 2), l, 8:16, :]
                wide_lane = lanes((8, 128))
                column = jnp.sum(jnp.where(wide_lane == w, table, 0.0), axis=1, keepdims=True)
                diagonal = wide_lane == lax.broadcasted_iota(jnp.int32, (8, 128), 0)
                values_row = column_sum(jnp.where(diagonal, column, 0.0))[:, 0:NB]
                logit = r["mask_logits"][...].astype(F32)[l : l + 1]
                r["glog"][l : l + 1, :] = values_row / (1.0 + jnp.exp(logit))
                continue

            def put(at, value):
                if at < ROW_G1:
                    r["gbias"][l : l + 1, 128 * at : 128 * at + 128] = value
                else:
                    at -= ROW_G1
                    r["ggain"][l : l + 1, 128 * at : 128 * at + 128] = value

            for core in (0, 1):
                put(ROW_BQ + core, row(core, SG_BQ))
                put(ROW_BV + core, row(core, SG_BV))
                for h in (0, 1):
                    r["glog"][l, 2 * core + h] = SGF[core, l, SG_LG + 8 * h : SG_LG + 8 * h + 8, :]
            singles = ((ROW_BO, SG_BO), (ROW_S1, SG_S1), (ROW_BD, SG_BD), (ROW_S2, SG_S2), (ROW_G1, SG_G1), (ROW_G2, SG_G2))
            for at, source in singles:
                for j in (0, 1):
                    put(at + j, row(0, source + j))
            for t in range(4):
                first, second = weave_groups(row(0, SG_BI + t), row(1, SG_BI + t))
                put(ROW_BI + 2 * t, first)
                put(ROW_BI + 2 * t + 1, second)
        if gather:
            links.arrived(RX, fx_in)
            for l in range(LAYERS):
                own = jnp.concatenate([kept[kind, l] for kind in ("q", "o", "i")], axis=1)
                other = RX[l]
                zero = jnp.where(c == 0, own, other)
                one = jnp.where(c == 0, other, own)
                for j in range(3):
                    r["gqkv"][l, :, 256 * j : 256 * j + 128] = zero[:, 128 * j : 128 * j + 128]
                    r["gqkv"][l, :, 256 * j + 128 : 256 * j + 256] = one[:, 128 * j : 128 * j + 128]
                r["gout"][l, :, 0:128] = zero[:, 384:512]
                r["gout"][l, :, 128:256] = one[:, 384:512]
                for t in range(4):
                    at = 512 + 128 * t
                    first, second = weave_groups(zero[:, at : at + 128], one[:, at : at + 128])
                    r["gin"][l, :, 256 * t : 256 * t + 128] = first
                    r["gin"][l, :, 256 * t + 128 : 256 * t + 256] = second
        take_back(1, r["gtok"])
        links.drain()
        for kind in range(3):
            wait_pieces(token_pieces(kind), 2 * n_seq, r["tok_send"].at[kind], None, True)
        for which in range(2):
            wait_pieces(return_pieces(which), n_blk, r["ret_send"].at[which], None, True)

    return kernel


def call_kernel(n_blk, n_wa, gather, named):
    vmem = pl.BlockSpec(memory_space=pltpu.VMEM)
    smem = pl.BlockSpec(memory_space=pltpu.SMEM)
    in_names = list(named)
    shapes = dict(out=(BLK_DEV, BS, D), gtok=(BLK_DEV, BS, D))
    if gather:
        sources = ("w_qkv", "w_out", "w_in", "w_down", "biases", "gains", "mask_logits")
        results = ("gqkv", "gout", "gin", "gdown", "gbias", "ggain", "glog")
        shapes.update({result: named[source].shape for result, source in zip(results, sources)})
    else:
        shapes.update(
            gbias=(LAYERS, 6 * D + FF),
            ggain=(LAYERS, 2 * D),
            glog=(LAYERS, H, NB, 128),
            G_d=(LAYERS, MY_FF, D),
            G_i=(LAYERS, D, MY_FF),
            G_o=(LAYERS, 2, 128, 128),
            G_q=(LAYERS, D, 384),
        )
    hold = pltpu.VMEM if gather else jax.ShapeDtypeStruct
    scratch = scratch_shapes(n_blk, n_wa, gather)
    kernel = make_kernel(n_blk, n_wa, gather, in_names, list(shapes), list(scratch))
    results = pl.pallas_call(
        kernel,
        out_shape=[hold(shape, F32) for shape in shapes.values()],
        in_specs=[smem if name in ("place_smem", "masked_count") else vmem for name in in_names],
        out_specs=[vmem] * len(shapes),
        scratch_shapes=list(scratch.values()),
        compiler_params=pltpu.CompilerParams(
            collective_id=0, has_side_effects=True, vmem_limit_bytes=60 * 2**20
        ),
        name="encoder",
    )(*named.values())
    if gather:
        results = pl.pallas_call(
            write_out,
            out_shape=[jax.ShapeDtypeStruct(shape, F32) for shape in shapes.values()],
            in_specs=[vmem] * len(shapes),
            out_specs=[pl.BlockSpec(memory_space=pl.ANY)] * len(shapes),
            scratch_shapes=[pltpu.SemaphoreType.DMA((len(shapes),))],
            name="write_out",
        )(*[pltpu.with_memory_space_constraint(result, pltpu.VMEM) for result in results])
    return dict(zip(shapes, results))


def write_out(*refs):
    count = (len(refs) - 1) // 2
    sems = refs[-1]
    copies = [pltpu.make_async_copy(refs[k], refs[count + k], sems.at[k]) for k in range(count)]
    for copy in copies:
        copy.start()
    for copy in copies:
        copy.wait()


def local(
    tokens,
    placement,
    block_mask,
    w_qkv,
    w_out,
    w_in,
    w_down,
    biases,
    gains,
    mask_logits,
    masked_pos,
    masked_count,
    masked_grad,
):
    n_blk, n_wa = lax.axis_size("blk"), lax.axis_size("wa")
    both = ("blk", "wa")
    core = lax.rem(lax.axis_index("wa"), 2)
    gather = w_qkv.shape[1] == 8 and n_blk == H and n_wa == NB
    named = dict(
        tokens=tokens.reshape(BLK_DEV, BS, D),
        place_smem=placement,
        place_vmem=placement,
        block_mask=block_mask,
        masked_pos=masked_pos.reshape(1, -1),
        masked_count=masked_count,
        masked_grad=masked_grad.reshape(-1, D),
    )
    if gather:
        named.update(
            w_qkv=w_qkv, w_out=w_out, w_in=w_in, w_down=w_down, biases=biases, gains=gains, mask_logits=mask_logits
        )
    else:
        shards = (w_qkv, w_out, w_in, w_down, biases, gains, mask_logits)
        whole = [lax.all_gather(shard, both, axis=1, tiled=True) for shard in shards]
        qkv = lax.dynamic_index_in_dim(whole[0].reshape(LAYERS, D, 3, 2, 128), core, 3, False)
        qkv = qkv.reshape(LAYERS, D, 384)
        inner = lax.dynamic_index_in_dim(whole[2].reshape(LAYERS, D, 16, 2, 32), core, 3, False)
        down = lax.dynamic_index_in_dim(whole[3].reshape(LAYERS, 16, 2, 32, D), core, 2, False)
        vectors = jnp.concatenate([whole[4], whole[5]], axis=1).astype(F32)
        logits = whole[6].astype(F32).reshape(LAYERS, H, NB, NB)
        named.update(
            WA=qkv,
            WO=lax.dynamic_slice_in_dim(whole[1], core * 128, 128, axis=1),
            WI=inner.reshape(LAYERS, D, MY_FF),
            WD=down.reshape(LAYERS, MY_FF, D),
            PV=vectors.reshape(LAYERS, PV_ROWS, 128),
            LG=jnp.pad(logits, ((0, 0), (0, 0), (0, 0), (0, 128 - NB))),
        )
    got = call_kernel(n_blk, n_wa, gather, named)
    if gather:
        weight_grads = (got["gqkv"], got["gout"], got["gin"], got["gdown"])
        small = (got["gbias"], got["ggain"], got["glog"])
    else:
        grad_logits = jnp.swapaxes(got["glog"][..., 0:NB], 2, 3).reshape(LAYERS, H * NB * NB)

        def one_core(part, axis):
            halves = [jnp.where(core == side, part, 0.0) for side in (0, 1)]
            return jnp.stack(halves, axis=axis)

        whole = (
            one_core(got["G_q"].reshape(LAYERS, D, 3, 128), 3).reshape(LAYERS, D, 3 * D),
            one_core(got["G_o"].reshape(LAYERS, D, 128), 2).reshape(LAYERS, D, D),
            one_core(got["G_i"].reshape(LAYERS, D, 16, 32), 3).reshape(LAYERS, D, FF),
            one_core(got["G_d"].reshape(LAYERS, 16, 32, D), 2).reshape(LAYERS, FF, D),
            got["gbias"],
            got["ggain"],
            grad_logits,
        )
        summed = [lax.psum_scatter(part, both, scatter_dimension=1, tiled=True) for part in whole]
        grad_mask = summed[6] * jax.nn.sigmoid(-mask_logits.astype(F32))
        weight_grads, small = tuple(summed[:4]), (summed[4], summed[5], grad_mask)
    return (
        got["out"].reshape(tokens.shape),
        got["gtok"].reshape(tokens.shape),
        *weight_grads,
        *small,
    )


def solution(mesh):
    placed = (
        P("wa", "blk", None, None),
        P("wa", None),
        P(),
        P(None, ("blk", "wa"), None),
        P(None, ("blk", "wa"), None),
        P(None, ("blk", "wa"), None),
        P(None, ("blk", "wa"), None),
        P(None, ("blk", "wa")),
        P(None, ("blk", "wa")),
        P(None, ("blk", "wa")),
        P("wa", "blk", None),
        P("wa", "blk"),
        P("wa", "blk", None, None),
    )
    return jax.shard_map(
        local,
        mesh=mesh,
        in_specs=placed,
        out_specs=(
            P("wa", "blk", None, None),
            P("wa", "blk", None, None),
            P(None, ("blk", "wa"), None),
            P(None, ("blk", "wa"), None),
            P(None, ("blk", "wa"), None),
            P(None, ("blk", "wa"), None),
            P(None, ("blk", "wa")),
            P(None, ("blk", "wa")),
            P(None, ("blk", "wa")),
        ),
        check_vma=False,
    )
```
